32 devices in a mesh: tile: 16 (over z, y, x), dp: 2 (over core).
Axes of the slice: x: 2, y: 2, z: 4, core: 2. Of those that a mesh axis runs over, the one named last changes fastest.
Arguments:
- features: bfloat16 [2, 192, 384, 128], P('dp', 'tile'), may hold values from -6 to 6
- cotangent: bfloat16 [2, 192, 384, 128], P('dp', 'tile'), may hold values from -6 to 6
- tile_mask: int32 [2, 16, 32], P('dp', 'tile'), may hold values from 0 to 1, as said below
- work_lists: int32 [2, 16, 22], P('dp'), may hold values from 0 to 511, as said below
- dilations: int32 [2, 16], P('dp'), may hold values from 1 to 2
- conv_weight: bfloat16 [3, 3, 128, 128], replicated, may hold values from -0.1875 to 0.1875
- conv_bias: float32 [128], replicated, may hold values from -4 to 4
Outputs:
- input_grad: bfloat16 [2, 192, 384, 128], P('dp', 'tile')
- weight_grads: float32 [147456], P(('tile', 'dp'))
The draws below stay inside these ranges and needn't reach their ends.
Inputs may be any that keep to these rules, and one draw needn't show every extreme that they name: `tile_mask`: exactly 352 tiles of each copy are 1. `work_lists`: for each copy, the work lists name every tile whose mask is 1 exactly once, as row * 32 + column, 22 for each worker; at most 2 of one worker's ids lie in one row of tiles, and in every draw some worker has 2 ids in one row.
All inputs are finite; a program needn't handle non-finite values.
Results may differ from the reference program's by a relative error of at most 0.0055.
Values may be sent and summed in bfloat16 or wider, within the bound.
No kernel may reach another device: no remote copies, remote signals or barrier semaphores. Data moves between devices by JAX's collectives and lax.ppermute only.
A program may use at most 128 MiB of HBM per device.

```python
import math
import jax
import jax.numpy as jnp
from jax import lax

C = 128
TILE = 12
HALO = 2
GX = 32
WORK = 22
LIVE = 352
COPIES = 2
NY = 192
NX = 384
N_TILE = 16


def live_layout(key):
    mask_list = []
    work_list = []
    for copy_index in range(COPIES):
        copy_key = jax.random.fold_in(jax.random.fold_in(key, 7711), copy_index)
        all_tiles = N_TILE * GX
        tile_ids = jnp.arange(all_tiles, dtype=jnp.int32)
        tile_rows = tile_ids // GX
        band_start = N_TILE // 8
        in_band = ((tile_rows >= band_start) & (tile_rows < band_start + N_TILE // 4)).astype(jnp.int32)
        jitter = jax.random.randint(jax.random.fold_in(copy_key, 1), (all_tiles,), 0, 1 << 20, dtype=jnp.int32)
        scores = in_band * (1 << 21) + jitter
        middle = N_TILE // 2
        forced = (tile_rows == 0) | (tile_ids == all_tiles - 1) | (tile_rows >= middle - 1) & (tile_rows <= middle + 1)
        scores = jnp.where(forced, -1, scores)
        ranking = jnp.argsort(scores, stable=True)
        observed = jnp.zeros((all_tiles,), jnp.int32).at[ranking[:LIVE]].set(1)
        live_ids = jnp.argsort(1 - observed, stable=True)[:LIVE].astype(jnp.int32)
        shuffle = jax.random.permutation(jax.random.fold_in(copy_key, 2), N_TILE)
        inverse = jnp.argsort(shuffle)
        lists_here = live_ids.reshape(WORK, N_TILE).T[inverse]
        mask_list.append(observed.reshape(N_TILE, GX))
        work_list.append(lists_here.astype(jnp.int32))
    return (jnp.stack(mask_list), jnp.stack(work_list))


def draw_tile_mask(key, part):
    return live_layout(key)[0]


def draw_work_lists(key, part):
    return live_layout(key)[1]


def plant(drawn, key, least, high):
    spot = [jax.random.randint(jax.random.fold_in(key, axis), (), 0, length) for axis, length in enumerate(drawn.shape)]
    widest = drawn.shape.index(max(drawn.shape))
    neighbour = spot[:widest] + [(spot[widest] + 1) % drawn.shape[widest]] + spot[widest + 1:]
    return drawn.at[tuple(spot)].set(least).at[tuple(neighbour)].set(high)


def level_of(key, shape, cuts, low, largest):
    level, own = 1.0, jax.random.fold_in(key, 6)
    for dim, parts in cuts:
        steps = jnp.exp(jax.random.uniform(jax.random.fold_in(own, dim), (parts,), jnp.float32, low / len(cuts), largest / len(cuts)))
        level = level * jnp.repeat(steps, shape[dim] // parts).reshape([-1 if axis == dim else 1 for axis in range(len(shape))])
    return level


def centred(rng, shape, spread, most, split=(), held_as=jnp.bfloat16):
    drawn = spread * jax.random.normal(rng, shape, jnp.float32)
    if split:
        drawn = drawn * level_of(rng, shape, split, -0.22, 0.18)
    return jnp.clip(drawn, -most, most).astype(held_as)


def setup_inputs(seed: int = 0) -> dict:
    splits = jax.random.split(jax.random.key(seed), 8)
    return {
        "features": centred(splits[0], (COPIES, NY, NX, C), 1.0, 6.0, ((0, 2), (1, 16))),
        "cotangent": centred(splits[1], (COPIES, NY, NX, C), 1.0, 6.0, ((0, 2), (1, 16))),
        "tile_mask": draw_tile_mask(jax.random.fold_in(splits[7], 71), 0),
        "work_lists": draw_work_lists(jax.random.fold_in(splits[7], 71), 0),
        "dilations": plant(jax.random.randint(splits[4], (COPIES, N_TILE), 1, 3), jax.random.fold_in(splits[4], 1), 1, 2).astype(jnp.int32),
        "conv_weight": centred(splits[5], (3, 3, C, C), (9 * C) ** -0.5, 0.1875),
        "conv_bias": centred(splits[6], (C,), 1.0, 4.0, (), jnp.float32),
    }


def tap_product(source, weight, anchor, stride, extent, mirror, merged):
    number = source.shape[1]
    channels = source.shape[3]
    zero_index = jnp.zeros((), jnp.int32)
    summed = jnp.zeros((extent * number * extent, weight.shape[3]), jnp.float32)
    for tap_row in range(3):
        sliced = []
        matrices = []
        for tap_col in range(3):
            if mirror:
                row_start = anchor - (tap_row - 1) * stride
                col_start = anchor - (tap_col - 1) * stride
                matrices.append(weight[tap_row, tap_col].T)
            else:
                row_start = anchor + (tap_row - 1) * stride
                col_start = anchor + (tap_col - 1) * stride
                matrices.append(weight[tap_row, tap_col])
            region = lax.dynamic_slice(source, (jnp.asarray(row_start).astype(jnp.int32), zero_index, jnp.asarray(col_start).astype(jnp.int32), zero_index), (extent, number, extent, channels))
            sliced.append(region.reshape(extent * number * extent, channels))
        if merged:
            summed = summed + jnp.dot(jnp.concatenate(sliced, axis=1), jnp.concatenate(matrices, axis=0), preferred_element_type=jnp.float32)
        else:
            for region, matrix in zip(sliced, matrices):
                summed = summed + jnp.dot(region, matrix, preferred_element_type=jnp.float32)
    return summed.reshape(extent, number, extent, weight.shape[3])

def tap_weight_grad(source, grad_rows, anchor, stride, extent, merged):
    number = source.shape[1]
    channels = source.shape[3]
    zero_index = jnp.zeros((), jnp.int32)
    contract = (((0,), (0,)), ((), ()))
    rows_out = []
    for tap_row in range(3):
        sliced = []
        for tap_col in range(3):
            row_start = anchor + (tap_row - 1) * stride
            col_start = anchor + (tap_col - 1) * stride
            region = lax.dynamic_slice(source, (jnp.asarray(row_start).astype(jnp.int32), zero_index, jnp.asarray(col_start).astype(jnp.int32), zero_index), (extent, number, extent, channels))
            sliced.append(region.reshape(extent * number * extent, channels))
        if merged:
            product = lax.dot_general(jnp.concatenate(sliced, axis=1), grad_rows, contract, preferred_element_type=jnp.float32)
            rows_out.append(product.reshape(3, channels, grad_rows.shape[1]))
        else:
            rows_out.append(jnp.stack([lax.dot_general(region, grad_rows, contract, preferred_element_type=jnp.float32) for region in sliced]))
    return jnp.stack(rows_out)

def tile_grads(windows, tile_cotan, conv_weight, conv_bias, dilation, merged):
    channels = windows.shape[3]
    before = tap_product(windows, conv_weight, HALO, dilation, TILE, False, merged) + conv_bias
    sigmoid_pre = jax.nn.sigmoid(before)
    before_grad = (tile_cotan.astype(jnp.float32) * sigmoid_pre * (1.0 + before * (1.0 - sigmoid_pre))).astype(jnp.bfloat16)
    tap_grad = tap_weight_grad(windows, before_grad.reshape(-1, channels), HALO, dilation, TILE, merged)
    grad_pad = jnp.pad(before_grad, ((2 * HALO, 2 * HALO), (0, 0), (2 * HALO, 2 * HALO), (0, 0)))
    window_grad = tap_product(grad_pad, conv_weight, HALO, dilation, TILE + 2 * HALO, True, merged)
    cot_pad = jnp.pad(tile_cotan, ((HALO, HALO), (0, 0), (HALO, HALO), (0, 0)))
    window_grad = (window_grad + cot_pad.astype(jnp.float32)).astype(jnp.bfloat16)
    return (window_grad, tap_grad)

def reference(features, cotangent, tile_mask, work_lists, dilations, conv_weight, conv_bias):
    extent = TILE + 2 * HALO
    zero_index = jnp.zeros((), jnp.int32)
    tap_total = jnp.zeros((3, 3, C, C), jnp.float32)
    results = []
    for copy_index in range(COPIES):
        cell_mask = jnp.repeat(jnp.repeat(tile_mask[copy_index], TILE, axis=0), TILE, axis=1)
        masked = features[copy_index] * cell_mask.astype(jnp.bfloat16)[:, :, None]
        padded = jnp.pad(masked, ((HALO, HALO), (HALO, HALO), (0, 0)))
        cotan_full = cotangent[copy_index]
        row_rates = dilations[copy_index]

        def visit_tile(carried, tile_id):
            summed, tap_acc = carried
            tile_row = (tile_id // GX).astype(jnp.int32)
            tile_col = (tile_id % GX).astype(jnp.int32)
            dilation = row_rates[tile_row]
            row_start = tile_row * TILE
            col_start = tile_col * TILE
            window = lax.dynamic_slice(padded, (row_start, col_start, zero_index), (extent, extent, C))[:, None]
            tile_cotan = lax.dynamic_slice(cotan_full, (row_start, col_start, zero_index), (TILE, TILE, C))[:, None]
            window_grad, tap_grad = tile_grads(window, tile_cotan, conv_weight, conv_bias, dilation, False)
            current = lax.dynamic_slice(summed, (row_start, col_start, zero_index), (extent, extent, C))
            summed = lax.dynamic_update_slice(summed, current + window_grad[:, 0].astype(jnp.float32), (row_start, col_start, zero_index))
            return ((summed, tap_acc + tap_grad), None)
        initial = (jnp.zeros((NY + 2 * HALO, NX + 2 * HALO, C), jnp.float32), tap_total)
        (summed, tap_total), _ = lax.scan(visit_tile, initial, work_lists[copy_index].reshape(-1))
        own_cells = summed[HALO:HALO + NY, HALO:HALO + NX] * cell_mask[:, :, None].astype(jnp.float32)
        results.append(own_cells.astype(jnp.bfloat16))
    grad_scale = 1.0 / math.sqrt(COPIES * LIVE * TILE * TILE)
    weight_grads = tap_total.reshape(-1) * grad_scale
    return (jnp.stack(results), weight_grads)
```

```python
import functools
import math

import jax
import jax.numpy as jnp
from jax import lax
from jax.experimental import pallas as pl
from jax.experimental.pallas import tpu as pltpu
from jax.sharding import PartitionSpec as P

TILE = 12
HALO = 2
LANES = 128
EDGE = 8
VMEM_LIMIT = 48 * 1024 * 1024

F32 = jnp.float32
BF16 = jnp.bfloat16


def expand_mask(obs_ref, row, columns):
    first = TILE * lax.broadcasted_iota(jnp.int32, (columns, LANES), 1)
    cell = lax.broadcasted_iota(jnp.int32, (columns, LANES), 0)
    inside = (cell >= first) & (cell < first + TILE)
    picked = jnp.where(inside, obs_ref[row : row + 1, :], 0.0).astype(BF16)
    return jnp.dot(picked, jnp.ones((LANES, LANES), BF16), preferred_element_type=F32)


def pair_start(index, rate):
    return jnp.where(rate == 1, 2 * index, 4 * (index // 2) + index % 2)


def shifted_three(pad_ref, rate, sign, columns):
    return [
        pad_ref[pl.ds(EDGE - sign * rate, columns), :].astype(BF16),
        pad_ref[pl.ds(EDGE, columns), :].astype(BF16),
        pad_ref[pl.ds(EDGE + sign * rate, columns), :].astype(BF16),
    ]


def taps_kernel(
    rate_ref, obs_ref, low_ref, x_ref, high_ref, cot_ref, w_ref, bias_ref,
    tap_ref, grad_ref,
    pad, masks, xcat, xt, gcat, wide, total, flat,
):
    columns, channels = x_ref.shape[1], x_ref.shape[2]
    rate = rate_ref[0]
    for row in range(3):
        masks[row] = expand_mask(obs_ref, row, columns)
    pad[:EDGE] = jnp.zeros((EDGE, channels), F32)
    pad[EDGE + columns :] = jnp.zeros((EDGE, channels), F32)
    for row in range(4):
        for out in range(2):
            tap = row - out
            for col in range(3):
                block = (
                    w_ref[tap * 3 + col] if 0 <= tap < 3 else jnp.zeros((channels, channels), BF16)
                )
                start = (row * 3 + col) * channels
                wide[start : start + channels, out * channels : (out + 1) * channels] = block

    def prepare(source, row, target, mask):
        value = source[row].astype(F32) * masks[mask]
        pad[EDGE : EDGE + columns] = value
        left, here, right = shifted_three(pad, rate, 1, columns)
        xcat[target, :, :channels] = left
        xcat[target, :, channels : 2 * channels] = here
        xcat[target, :, 2 * channels :] = right
        xt[target] = here.T

    for row in range(HALO):
        prepare(low_ref, row, row, 0)
        prepare(high_ref, row, HALO + TILE + row, 2)

    @pl.loop(0, TILE)
    def _(row):
        prepare(x_ref, row, HALO + row, 1)

    total[...] = jnp.zeros_like(total)

    @pl.loop(0, TILE // 2)
    def _(index):
        first = pair_start(index, rate)
        rows = jnp.concatenate([xcat[first + HALO + rate * (k - 1)] for k in range(4)], axis=1)
        both = jnp.dot(rows, wide[...], preferred_element_type=F32)
        for out in range(2):
            row = first + rate * out
            pre = both[:, out * channels : (out + 1) * channels] + bias_ref[...]
            sig = 0.5 * jnp.tanh(0.5 * pre) + 0.5
            grad = cot_ref[row].astype(F32) * masks[1] * sig * (1.0 + pre * (1.0 - sig))
            grad_ref[row] = grad.astype(BF16)
            pad[EDGE : EDGE + columns] = grad
            left, here, right = shifted_three(pad, rate, -1, columns)
            part = slice(out * columns, (out + 1) * columns)
            gcat[part, :channels] = left
            gcat[part, channels : 2 * channels] = here
            gcat[part, 2 * channels :] = right
        flipped = jnp.concatenate(
            [
                jnp.concatenate(
                    [xt[first + HALO + rate * (a + out)] for out in range(2)], axis=1
                )
                for a in (-1, 0, 1)
            ],
            axis=0,
        )
        total[...] += jnp.dot(flipped, gcat[...], preferred_element_type=F32)

    for a in range(3):
        for b in range(3):
            start = (a * 3 + b) * channels
            flat[start : start + channels] = total[
                a * channels : (a + 1) * channels, b * channels : (b + 1) * channels
            ]
    share = tap_ref.shape[1]
    for part in range(tap_ref.shape[0]):
        tap_ref[part] = flat[part * share : (part + 1) * share].astype(BF16)


def inputs_kernel(
    rate_ref, obs_ref, grad_ref, cot_ref, w_ref,
    out_ref, edge_ref, low_ref, high_ref,
    pad, mask, gcat, wide, sums,
):
    columns, channels = grad_ref.shape[1], grad_ref.shape[2]
    rate = rate_ref[0]
    mask[...] = expand_mask(obs_ref, 1, columns)
    pad[:EDGE] = jnp.zeros((EDGE, channels), F32)
    pad[EDGE + columns :] = jnp.zeros((EDGE, channels), F32)
    for row in range(4):
        for out in range(2):
            tap = out + 2 - row
            for col in range(3):
                block = (
                    w_ref[tap * 3 + col] if 0 <= tap < 3 else jnp.zeros((channels, channels), BF16)
                )
                start = (row * 3 + col) * channels
                wide[out * channels : (out + 1) * channels, start : start + channels] = block
    rim = jnp.zeros((2 * HALO,) + gcat.shape[1:], BF16)
    gcat[: 2 * HALO] = rim
    gcat[2 * HALO + TILE :] = rim

    @pl.loop(0, TILE)
    def _(row):
        pad[EDGE : EDGE + columns] = grad_ref[row].astype(F32)
        left, here, right = shifted_three(pad, rate, -1, columns)
        gcat[2 * HALO + row, :, :channels] = left
        gcat[2 * HALO + row, :, channels : 2 * channels] = here
        gcat[2 * HALO + row, :, 2 * channels :] = right

    @pl.loop(0, TILE // 2 + HALO)
    def _(index):
        first = pair_start(index, rate)
        rows = jnp.concatenate([gcat[first + HALO + rate * (k - 1)] for k in range(4)], axis=1)
        both = lax.dot_general(
            rows, wide[...], (((1,), (1,)), ((), ())), preferred_element_type=F32
        )
        for out in range(2):
            sums[first + rate * out] = both[:, out * channels : (out + 1) * channels]

    for row in range(HALO):
        low_ref[row] = sums[row].astype(BF16)
        high_ref[row] = sums[HALO + TILE + row].astype(BF16)
        edge_ref[row] = sums[HALO + row] + cot_ref[row].astype(F32)
        edge_ref[HALO + row] = sums[TILE + row] + cot_ref[TILE - HALO + row].astype(F32)
    for row in range(HALO, TILE - HALO):
        value = (sums[HALO + row] + cot_ref[row].astype(F32)) * mask[...]
        out_ref[row] = value.astype(BF16)


def edges_kernel(obs_ref, edge_ref, rim_ref, held_ref, out_ref):
    del held_ref
    mask = expand_mask(obs_ref, 1, edge_ref.shape[1])
    for row in range(HALO):
        value = (edge_ref[row] + rim_ref[row].astype(F32)) * mask
        out_ref[row] = value.astype(BF16)


def exchange(to_next, to_previous, axis):
    count = lax.axis_size(axis)
    forward = [(i, i + 1) for i in range(count - 1)]
    backward = [(target, source) for source, target in forward]
    return lax.ppermute(to_next, axis, forward), lax.ppermute(to_previous, axis, backward)


def shards(features, cotangent, tile_mask, work_lists, dilations, conv_weight, conv_bias):
    x, cot = features[0], cotangent[0]
    columns, channels = x.shape[1], x.shape[2]
    tiles_row = columns // TILE
    axes = ("tile", "dp")
    devices = lax.axis_size("tile") * lax.axis_size("dp")
    my_index = lax.axis_index("tile")

    low, high = exchange(x[TILE - HALO :], x[:HALO], "tile")

    rate = lax.dynamic_slice_in_dim(dilations[0], my_index, 1)
    row_ids = my_index - 1 + jnp.arange(8, dtype=jnp.int32)
    lane = jnp.arange(LANES, dtype=jnp.int32)
    targets = jnp.where(lane < tiles_row, row_ids[:, None] * tiles_row + lane, -1)
    ids = work_lists[0].reshape(-1)
    observed = jnp.any(ids[:, None, None] == targets[None], axis=0).astype(F32)
    weight = conv_weight.reshape(9, channels, channels)
    bias = conv_bias.reshape(1, channels)

    smem = pl.BlockSpec(memory_space=pltpu.SMEM)
    vmem = pl.BlockSpec(memory_space=pltpu.VMEM)
    params = pltpu.CompilerParams(vmem_limit_bytes=VMEM_LIMIT)
    rows_total = 9 * channels
    direct = rows_total % devices == 0
    shape_taps = (devices, rows_total // devices) if direct else (1, rows_total)

    taps, grad = pl.pallas_call(
        taps_kernel,
        out_shape=(
            jax.ShapeDtypeStruct(shape_taps + (channels,), BF16),
            jax.ShapeDtypeStruct((TILE, columns, channels), BF16),
        ),
        in_specs=[smem] + [vmem] * 7,
        out_specs=(vmem, vmem),
        scratch_shapes=[
            pltpu.VMEM((columns + 2 * EDGE, channels), F32),
            pltpu.VMEM((3, columns, channels), F32),
            pltpu.VMEM((TILE + 2 * HALO, columns, 3 * channels), BF16),
            pltpu.VMEM((TILE + 2 * HALO, channels, columns), BF16),
            pltpu.VMEM((2 * columns, 3 * channels), BF16),
            pltpu.VMEM((12 * channels, 2 * channels), BF16),
            pltpu.VMEM((3 * channels, 3 * channels), F32),
            pltpu.VMEM((rows_total, channels), F32),
        ],
        compiler_params=params,
        name="taps",
    )(rate, observed, low, x, high, cot, weight, bias)

    if not direct:
        taps = taps.reshape(devices, -1)
    received = lax.all_to_all(taps, axes, 0, 0, tiled=True)

    held, edge, to_low, to_high = pl.pallas_call(
        inputs_kernel,
        out_shape=(
            jax.ShapeDtypeStruct((TILE, columns, channels), BF16),
            jax.ShapeDtypeStruct((2 * HALO, columns, channels), F32),
            jax.ShapeDtypeStruct((HALO, columns, channels), BF16),
            jax.ShapeDtypeStruct((HALO, columns, channels), BF16),
        ),
        in_specs=[smem] + [vmem] * 4,
        out_specs=(vmem,) * 4,
        scratch_shapes=[
            pltpu.VMEM((columns + 2 * EDGE, channels), F32),
            pltpu.VMEM((columns, channels), F32),
            pltpu.VMEM((TILE + 4 * HALO, columns, 3 * channels), BF16),
            pltpu.VMEM((2 * channels, 12 * channels), BF16),
            pltpu.VMEM((TILE + 2 * HALO, columns, channels), F32),
        ],
        compiler_params=params,
        name="inputs",
    )(rate, observed, grad, cot, weight)

    from_low, from_high = exchange(to_high, to_low, "tile")
    rims = jnp.concatenate([from_low, from_high], axis=0)
    block = (HALO, columns, channels)
    last = TILE // HALO - 1
    input_grad = pl.pallas_call(
        edges_kernel,
        grid=(2,),
        out_shape=jax.ShapeDtypeStruct((TILE, columns, channels), BF16),
        in_specs=[
            pl.BlockSpec((8, LANES), lambda i: (0, 0)),
            pl.BlockSpec(block, lambda i: (i, 0, 0)),
            pl.BlockSpec(block, lambda i: (i, 0, 0)),
            pl.BlockSpec(memory_space=pl.ANY),
        ],
        out_specs=pl.BlockSpec(block, lambda i: (i * last, 0, 0)),
        input_output_aliases={3: 0},
        compiler_params=params,
        name="edges",
    )(observed, edge, rims, held)

    grad_scale = 1.0 / math.sqrt(devices * work_lists.shape[2] * TILE * TILE)
    summed = jnp.sum(received.astype(F32), axis=0) * grad_scale
    return (input_grad[None], summed.reshape(-1))


def solution(mesh):
    placed = (
        P("dp", "tile", None, None),
        P("dp", "tile", None, None),
        P("dp", "tile", None),
        P("dp", None, None),
        P("dp", None),
        P(),
        P(),
    )
    return jax.shard_map(
        shards,
        mesh=mesh,
        in_specs=placed,
        out_specs=(P("dp", "tile", None, None), P(("tile", "dp"))),
        check_vma=False,
    )
```

```python
import math

import jax
import jax.numpy as jnp
from jax import lax
from jax.experimental import pallas as pl
from jax.experimental.pallas import tpu as pltpu
from jax.sharding import PartitionSpec as P

TILE = 12
HALO = 2
LANES = 128
EDGE = 8
VMEM_LIMIT = 32 * 1024 * 1024

F32 = jnp.float32
BF16 = jnp.bfloat16


def cell_mask(lists_ref, row, tiles_row, columns):
    ids = lists_ref[...]
    workers, width = ids.shape
    tile = lax.broadcasted_iota(jnp.int32, (tiles_row, width), 0)
    target = row * tiles_row + tile
    found = ids[0:1] == target
    for worker in range(1, workers):
        found = found | (ids[worker : worker + 1] == target)
    named = jnp.dot(
        jnp.where(found, 1.0, 0.0).astype(BF16),
        jnp.ones((width, LANES), BF16),
        preferred_element_type=F32,
    )
    first = TILE * lax.broadcasted_iota(jnp.int32, (columns, tiles_row), 1)
    cell = lax.broadcasted_iota(jnp.int32, (columns, tiles_row), 0)
    inside = (cell >= first) & (cell < first + TILE)
    return jnp.dot(
        jnp.where(inside, 1.0, 0.0).astype(BF16), named.astype(BF16), preferred_element_type=F32
    )


def pair_start(index, rate):
    return jnp.where(rate == 1, 2 * index, 4 * (index // 2) + index % 2)


def clear_ends(pad_ref, columns):
    ends = jnp.zeros((EDGE, pad_ref.shape[-1]), F32)
    pad_ref[:EDGE] = ends
    pad_ref[EDGE + columns :] = ends


def spread(value, pad_ref, target_ref, rate, sign):
    columns, channels = value.shape
    pad_ref[EDGE : EDGE + columns] = value
    target_ref[:, :channels] = pad_ref[pl.ds(EDGE - sign * rate, columns), :].astype(BF16)
    target_ref[:, channels : 2 * channels] = value.astype(BF16)
    target_ref[:, 2 * channels :] = pad_ref[pl.ds(EDGE + sign * rate, columns), :].astype(BF16)


def silu_grad(cot, pre):
    sig = 0.5 * jnp.tanh(0.5 * pre) + 0.5
    return cot * sig * (1.0 + pre * (1.0 - sig))


def add_tap_sums(total_ref, gcat, flipped):
    total_ref[...] += jnp.dot(flipped, gcat, preferred_element_type=F32)


def first_kernel(
    rates_ref, lists_ref, x_hbm, cot_hbm, w_hbm, bias_ref,
    pre_ref, grad_ref, xt_ref, total_ref, mask_ref, cot_ref,
    xbuf, cbuf, wbuf, pad, masks, xcat, gcat, wide, held, sems,
):
    rows, columns, channels = x_hbm.shape
    tiles_row = columns // TILE
    mine = lax.axis_index("tile")
    rate = rates_ref[0, mine]
    step = rows // 3
    loads = [
        pltpu.make_async_copy(
            x_hbm.at[pl.ds(k * step, step)], xbuf.at[pl.ds(k * step, step)], sems.at[k]
        )
        for k in range(3)
    ]
    loads.append(pltpu.make_async_copy(w_hbm, wbuf, sems.at[3]))
    loads.append(pltpu.make_async_copy(cot_hbm, cbuf, sems.at[4]))
    for load in loads:
        load.start()
    for k in range(3):
        value = cell_mask(lists_ref, mine + k - 1, tiles_row, columns)
        masks[k] = value
        mask_ref[k] = value.astype(BF16)
    clear_ends(pad, columns)
    none = jnp.zeros((HALO,) + xcat.shape[1:], BF16)
    xcat[:HALO] = none
    xcat[HALO + rows :] = none

    for k in range(3):
        loads[k].wait()

        @pl.loop(k * step, (k + 1) * step)
        def _(row):
            value = xbuf[row].astype(F32) * masks[1]
            spread(value, pad, xcat.at[HALO + row], rate, 1)
            xt_ref[row] = value.astype(BF16).T

    loads[3].wait()
    for row in range(4):
        for out in range(2):
            tap = row - out
            for col in range(3):
                block = (
                    wbuf[tap * 3 + col] if 0 <= tap < 3 else jnp.zeros((channels, channels), BF16)
                )
                start = (row * 3 + col) * channels
                wide[start : start + channels, out * channels : (out + 1) * channels] = block

    @pl.loop(0, rows // 2)
    def _(index):
        first = pair_start(index, rate)
        lhs = jnp.concatenate([xcat[first + HALO + rate * (k - 1)] for k in range(4)], axis=1)
        both = jnp.dot(lhs, wide[...], preferred_element_type=F32)
        for out in range(2):
            held[first + rate * out] = (
                both[:, out * channels : (out + 1) * channels] + bias_ref[...]
            )

    loads[4].wait()
    for k in range(HALO):
        for here, row in ((k, k), (HALO + k, rows - HALO + k)):
            pre_ref[here] = held[row]
            cot_ref[here] = (cbuf[row].astype(F32) * masks[1]).astype(BF16)
    total_ref[...] = jnp.zeros_like(total_ref)

    @pl.loop(0, rows // 2 - HALO)
    def _(index):
        first = HALO + 2 * index
        for out in range(2):
            row = first + out
            grad = silu_grad(cbuf[row].astype(F32) * masks[1], held[row])
            grad_ref[row - HALO] = grad.astype(BF16)
            spread(grad, pad, gcat.at[pl.ds(out * columns, columns)], rate, -1)
        flipped = jnp.concatenate(
            [
                jnp.concatenate([xt_ref[first + rate * a + out] for out in range(2)], axis=1)
                for a in (-1, 0, 1)
            ],
            axis=0,
        )
        add_tap_sums(total_ref, gcat[...], flipped)


def rims_kernel(
    rates_ref, low_ref, high_ref, pre_ref, cot_ref, mask_ref, w_ref,
    grad_low_ref, grad_high_ref, xt_ref,
    pad, xcat, terms,
):
    _, columns, channels = low_ref.shape
    rate = rates_ref[0, lax.axis_index("tile")]
    clear_ends(pad, columns)
    for side, ref in enumerate((low_ref, high_ref)):
        mask = mask_ref[2 * side].astype(F32)
        for k in range(HALO):
            value = ref[k].astype(F32) * mask
            spread(value, pad, xcat.at[pl.ds(k * columns, columns)], rate, 1)
            xt_ref[side * HALO + k] = value.astype(BF16).T
        taps = jnp.concatenate([w_ref[6 * side + b] for b in range(3)], axis=0)
        result = jnp.dot(xcat[...], taps, preferred_element_type=F32)
        for k in range(HALO):
            terms[side * HALO + k] = result[k * columns : (k + 1) * columns]
    near = rate == 1
    none = jnp.zeros((columns, channels), F32)
    adds = [
        jnp.where(near, terms[1], terms[0]),
        jnp.where(near, none, terms[1]),
        jnp.where(near, none, terms[2]),
        jnp.where(near, terms[2], terms[3]),
    ]
    for k in range(2 * HALO):
        grad = silu_grad(cot_ref[k].astype(F32), pre_ref[k] + adds[k])
        target = grad_low_ref if k < HALO else grad_high_ref
        target[k % HALO] = grad.astype(BF16)


def taps_kernel(
    rates_ref, grad_low_ref, grad_high_ref, xt_own_ref, xt_halo_ref, total_in_ref,
    tap_ref,
    pad, gcat, xt, total, flat,
):
    _, columns, channels = grad_low_ref.shape
    rows = xt_own_ref.shape[0]
    rate = rates_ref[0, lax.axis_index("tile")]
    clear_ends(pad, columns)
    half = 3 * HALO
    xt[:HALO] = xt_halo_ref[:HALO]
    xt[HALO:half] = xt_own_ref[: 2 * HALO]
    xt[half : half + 2 * HALO] = xt_own_ref[rows - 2 * HALO :]
    xt[half + 2 * HALO :] = xt_halo_ref[HALO:]
    total[...] = total_in_ref[...]
    for side, ref in enumerate((grad_low_ref, grad_high_ref)):
        for k in range(HALO):
            spread(ref[k].astype(F32), pad, gcat.at[pl.ds(k * columns, columns)], rate, -1)
        base = HALO + half * side
        flipped = jnp.concatenate(
            [
                jnp.concatenate([xt[base + rate * a + k] for k in range(HALO)], axis=1)
                for a in (-1, 0, 1)
            ],
            axis=0,
        )
        add_tap_sums(total, gcat[...], flipped)
    for a in range(3):
        for b in range(3):
            start = (a * 3 + b) * channels
            flat[start : start + channels] = total[
                a * channels : (a + 1) * channels, b * channels : (b + 1) * channels
            ]
    share = tap_ref.shape[1]
    for part in range(tap_ref.shape[0]):
        tap_ref[part] = flat[part * share : (part + 1) * share].astype(BF16)


def inputs_kernel(
    rates_ref, grad_ref, grad_low_ref, grad_high_ref, cot_hbm, mask_ref, w_ref,
    out_hbm, edge_ref,
    cbuf, obuf, pad, gcat, wide, sums, sems,
):
    rows, columns, channels = cot_hbm.shape
    rate = rates_ref[0, lax.axis_index("tile")]
    load = pltpu.make_async_copy(cot_hbm, cbuf, sems.at[0])
    load.start()
    clear_ends(pad, columns)
    for row in range(4):
        for out in range(2):
            tap = out + 2 - row
            for col in range(3):
                block = (
                    w_ref[tap * 3 + col] if 0 <= tap < 3 else jnp.zeros((channels, channels), BF16)
                )
                start = (row * 3 + col) * channels
                wide[out * channels : (out + 1) * channels, start : start + channels] = block
    none = jnp.zeros((HALO,) + gcat.shape[1:], BF16)
    gcat[:HALO] = none
    gcat[HALO + rows :] = none
    for k in range(HALO):
        spread(grad_low_ref[k].astype(F32), pad, gcat.at[HALO + k], rate, -1)
        spread(grad_high_ref[k].astype(F32), pad, gcat.at[rows + k], rate, -1)

    @pl.loop(0, rows - 2 * HALO)
    def _(row):
        spread(grad_ref[row].astype(F32), pad, gcat.at[2 * HALO + row], rate, -1)

    @pl.loop(0, rows // 2)
    def _(index):
        first = pair_start(index, rate)
        lhs = jnp.concatenate([gcat[first + HALO + rate * (k - 1)] for k in range(4)], axis=1)
        both = lax.dot_general(
            lhs, wide[...], (((1,), (1,)), ((), ())), preferred_element_type=F32
        )
        for out in range(2):
            sums[first + rate * out] = both[:, out * channels : (out + 1) * channels]

    load.wait()
    inner = rows - 2 * HALO
    for row in range(HALO, rows - HALO):
        value = (sums[row] + cbuf[row].astype(F32)) * mask_ref[1].astype(F32)
        obuf[row - HALO] = value.astype(BF16)
    store = pltpu.make_async_copy(obuf, out_hbm.at[pl.ds(HALO, inner)], sems.at[1])
    store.start()
    for k in range(HALO):
        for here, row in ((k, k), (HALO + k, rows - HALO + k)):
            edge_ref[here] = sums[row] + cbuf[row].astype(F32)
    store.wait()


def edges_kernel(
    rates_ref, low_ref, high_ref, edge_ref, mask_ref, w_ref, held_hbm,
    out_hbm,
    obuf, pad, gcat, terms, sems,
):
    del held_hbm
    _, columns, channels = low_ref.shape
    rows = out_hbm.shape[0]
    mine = lax.axis_index("tile")
    last = rates_ref.shape[1] - 1
    rates = (rates_ref[0, jnp.maximum(mine - 1, 0)], rates_ref[0, jnp.minimum(mine + 1, last)])
    clear_ends(pad, columns)
    for side, ref in enumerate((low_ref, high_ref)):
        for k in range(HALO):
            spread(
                ref[k].astype(F32), pad, gcat.at[pl.ds(k * columns, columns)], rates[side], -1
            )
        taps = jnp.concatenate([w_ref[6 * (1 - side) + b] for b in range(3)], axis=1)
        result = lax.dot_general(
            gcat[...], taps, (((1,), (1,)), ((), ())), preferred_element_type=F32
        )
        for k in range(HALO):
            terms[side * HALO + k] = result[k * columns : (k + 1) * columns]
    none = jnp.zeros((columns, channels), F32)
    adds = [
        jnp.where(rates[0] == 1, terms[1], terms[0]),
        jnp.where(rates[0] == 1, none, terms[1]),
        jnp.where(rates[1] == 1, none, terms[2]),
        jnp.where(rates[1] == 1, terms[2], terms[3]),
    ]
    for k in range(2 * HALO):
        obuf[k] = ((edge_ref[k] + adds[k]) * mask_ref[1].astype(F32)).astype(BF16)
    stores = [
        pltpu.make_async_copy(
            obuf.at[pl.ds(HALO * side, HALO)],
            out_hbm.at[pl.ds((rows - HALO) * side, HALO)],
            sems.at[side],
        )
        for side in range(2)
    ]
    for store in stores:
        store.start()
    for store in stores:
        store.wait()


def exchange(to_next, to_previous, axis):
    count = lax.axis_size(axis)
    forward = [(i, i + 1) for i in range(count - 1)]
    backward = [(target, source) for source, target in forward]
    return lax.ppermute(to_next, axis, forward), lax.ppermute(to_previous, axis, backward)


def call(kernel, name, outs, specs, scratch, cost, aliases=None):
    memory = {"s": pltpu.SMEM, "v": pltpu.VMEM, "h": pltpu.HBM}
    ins, results = (
        [pl.BlockSpec(memory_space=memory[letter]) for letter in part] for part in specs.split(">")
    )
    return pl.pallas_call(
        kernel,
        name=name,
        out_shape=tuple(jax.ShapeDtypeStruct(shape, dtype) for shape, dtype in outs),
        in_specs=ins,
        out_specs=tuple(results),
        scratch_shapes=scratch,
        input_output_aliases=aliases or {},
        cost_estimate=pl.CostEstimate(flops=cost, bytes_accessed=0, transcendentals=0),
        compiler_params=pltpu.CompilerParams(vmem_limit_bytes=VMEM_LIMIT),
    )


def shards(features, cotangent, tile_mask, work_lists, dilations, conv_weight, conv_bias):
    x, cot, lists = features[0], cotangent[0], work_lists[0]
    rows, columns, channels = x.shape
    axes = ("tile", "dp")
    devices = lax.axis_size("tile") * lax.axis_size("dp")
    weight = conv_weight.reshape(9, channels, channels)
    bias = conv_bias.reshape(1, channels)
    inner = rows - 2 * HALO
    wide_row = 3 * channels
    pad = pltpu.VMEM((columns + 2 * EDGE, channels), F32)
    work = 2 * rows * columns * 9 * channels * channels

    low, high = exchange(x[rows - HALO :], x[:HALO], "tile")

    pre, grad, xt, total, mask, cot_edge = call(
        first_kernel,
        "first",
        [
            ((2 * HALO, columns, channels), F32),
            ((inner, columns, channels), BF16),
            ((rows, channels, columns), BF16),
            ((wide_row, wide_row), F32),
            ((3, columns, channels), BF16),
            ((2 * HALO, columns, channels), BF16),
        ],
        "svhhhv>vvvvvv",
        [
            pltpu.VMEM((rows, columns, channels), BF16),
            pltpu.VMEM((rows, columns, channels), BF16),
            pltpu.VMEM((9, channels, channels), BF16),
            pad,
            pltpu.VMEM((3, columns, channels), F32),
            pltpu.VMEM((rows + 2 * HALO, columns, wide_row), BF16),
            pltpu.VMEM((2 * columns, wide_row), BF16),
            pltpu.VMEM((4 * wide_row, 2 * channels), BF16),
            pltpu.VMEM((rows, columns, channels), F32),
            pltpu.SemaphoreType.DMA((5,)),
        ],
        2 * work,
    )(dilations, lists, x, cot, weight, bias)

    grad_low, grad_high, xt_halo = call(
        rims_kernel,
        "rims",
        [
            ((HALO, columns, channels), BF16),
            ((HALO, columns, channels), BF16),
            ((2 * HALO, channels, columns), BF16),
        ],
        "svvvvvv>vvv",
        [
            pad,
            pltpu.VMEM((HALO * columns, wide_row), BF16),
            pltpu.VMEM((2 * HALO, columns, channels), F32),
        ],
        work // 6,
    )(dilations, low, high, pre, cot_edge, mask, weight)

    from_low, from_high = exchange(grad_high, grad_low, "tile")

    tap_rows = 9 * channels
    direct = tap_rows % devices == 0
    share = (devices, tap_rows // devices) if direct else (1, tap_rows)
    (taps,) = call(
        taps_kernel,
        "taps",
        [(share + (channels,), BF16)],
        "svvvvv>v",
        [
            pad,
            pltpu.VMEM((HALO * columns, wide_row), BF16),
            pltpu.VMEM((6 * HALO, channels, columns), BF16),
            pltpu.VMEM((wide_row, wide_row), F32),
            pltpu.VMEM((tap_rows, channels), F32),
        ],
        work // 3,
    )(dilations, grad_low, grad_high, xt, xt_halo, total)
    if not direct:
        taps = taps.reshape(devices, -1)
    received = lax.all_to_all(taps, axes, 0, 0, tiled=True)

    held, edge = call(
        inputs_kernel,
        "inputs",
        [((rows, columns, channels), BF16), ((2 * HALO, columns, channels), F32)],
        "svvvhvv>hv",
        [
            pltpu.VMEM((rows, columns, channels), BF16),
            pltpu.VMEM((inner, columns, channels), BF16),
            pad,
            pltpu.VMEM((rows + 2 * HALO, columns, wide_row), BF16),
            pltpu.VMEM((2 * channels, 4 * wide_row), BF16),
            pltpu.VMEM((rows, columns, channels), F32),
            pltpu.SemaphoreType.DMA((2,)),
        ],
        2 * work,
    )(dilations, grad, grad_low, grad_high, cot, mask, weight)

    (input_grad,) = call(
        edges_kernel,
        "edges",
        [((rows, columns, channels), BF16)],
        "svvvvvh>h",
        [
            pltpu.VMEM((2 * HALO, columns, channels), BF16),
            pad,
            pltpu.VMEM((HALO * columns, wide_row), BF16),
            pltpu.VMEM((2 * HALO, columns, channels), F32),
            pltpu.SemaphoreType.DMA((2,)),
        ],
        work // 6,
        {6: 0},
    )(dilations, from_low, from_high, edge, mask, weight, held)

    grad_scale = 1.0 / math.sqrt(devices * lists.shape[1] * TILE * TILE)
    summed = jnp.sum(received.astype(F32), axis=0) * grad_scale
    return (input_grad[None], summed.reshape(-1))


def solution(mesh):
    placed = (
        P("dp", "tile", None, None),
        P("dp", "tile", None, None),
        P("dp", "tile", None),
        P("dp", None, None),
        P("dp", None),
        P(),
        P(),
    )
    return jax.shard_map(
        shards,
        mesh=mesh,
        in_specs=placed,
        out_specs=(P("dp", "tile", None, None), P(("tile", "dp"))),
        check_vma=False,
    )
```

```python
import math

import jax
import jax.numpy as jnp
from jax import lax
from jax.experimental import pallas as pl
from jax.experimental.pallas import tpu as pltpu
from jax.sharding import PartitionSpec as P

TILE = 12
HALO = 2
LANES = 128
EDGE = 8
RATES = (1, 2)
VMEM_LIMIT = 40 * 1024 * 1024

F32 = jnp.float32
BF16 = jnp.bfloat16


def cell_masks(lists_ref, middle, tiles_row, columns):
    ids = lists_ref[...]
    workers, width = ids.shape
    tile = lax.broadcasted_iota(jnp.int32, (3 * tiles_row, width), 0)
    target = (middle - 1) * tiles_row + tile
    found = ids[0:1] == target
    for worker in range(1, workers):
        found = found | (ids[worker : worker + 1] == target)
    named = jnp.dot(
        jnp.where(found, 1.0, 0.0).astype(BF16),
        jnp.ones((width, LANES), BF16),
        preferred_element_type=F32,
    ).astype(BF16)
    first = TILE * lax.broadcasted_iota(jnp.int32, (columns, tiles_row), 1)
    cell = lax.broadcasted_iota(jnp.int32, (columns, tiles_row), 0)
    inside = jnp.where((cell >= first) & (cell < first + TILE), 1.0, 0.0).astype(BF16)
    return [
        jnp.dot(
            inside, named[k * tiles_row : (k + 1) * tiles_row], preferred_element_type=F32
        ).astype(BF16)
        for k in range(3)
    ]


def row_pairs(rate, rows):
    rows = list(rows)
    pairs = []
    for start in range(0, len(rows), 2 * rate):
        for k in range(rate):
            pairs.append((rows[start + k], rows[start + k + rate]))
    return pairs


def by_rate(rate, body):
    for value in RATES:
        pl.when(rate == value)(lambda value=value: body(value))


def clear_ends(pad_ref, count, columns):
    ends = jnp.zeros((EDGE, pad_ref.shape[-1]), F32)
    for k in range(count):
        pad_ref[k, :EDGE] = ends
        pad_ref[k, EDGE + columns :] = ends


def spread(value, pad_ref, slot, target_ref, offset):
    columns, channels = value.shape
    pad_ref[slot, EDGE : EDGE + columns] = value.astype(F32)
    target_ref[:, :channels] = pad_ref[slot, pl.ds(EDGE - offset, columns)].astype(BF16)
    target_ref[:, channels : 2 * channels] = value.astype(BF16)
    target_ref[:, 2 * channels :] = pad_ref[slot, pl.ds(EDGE + offset, columns)].astype(BF16)


def silu_grad(half_cot, half_pre):
    turn = jnp.tanh(half_pre)
    return half_cot * (1.0 + turn + half_pre * (1.0 - turn * turn))


def tap_sums(grads, xts, rate):
    flipped = jnp.concatenate(
        [
            jnp.concatenate([xts(row + rate * a) for row, _ in grads], axis=1)
            for a in (-1, 0, 1)
        ],
        axis=0,
    )
    return jnp.dot(
        flipped,
        jnp.concatenate([ref[...] for _, ref in grads], axis=0),
        preferred_element_type=F32,
    )


def pair_rows(pair, rate, rows):
    reach = [pair[0] + rate * (k - 1) for k in range(4)]
    inside = [k for k in range(4) if 0 <= reach[k] < rows]
    return [reach[k] for k in inside], inside[0], inside[-1] + 1


def input_sums(pair, rate, rows, grads, wide_ref):
    near, low, high = pair_rows(pair, rate, rows)
    lhs = jnp.concatenate([grads(row)[...] for row in near], axis=1)
    width = wide_ref.shape[1] // 4
    both = lax.dot_general(
        lhs,
        wide_ref[:, low * width : high * width],
        (((1,), (1,)), ((), ())),
        preferred_element_type=F32,
    )
    half = both.shape[1] // 2
    return both[:, :half], both[:, half:]


def first_kernel(
    rates_ref, lists_ref, x_hbm, cot_hbm, w_hbm, bias_ref,
    out_hbm, pre_ref, gcat_ref, xt_ref, total_ref, mask_ref, cot_ref, back_ref,
    xbuf, cbuf, wbuf, obuf, pad, xcat, wide, sems,
):
    rows, columns, channels = x_hbm.shape
    tiles_row = columns // TILE
    mine = lax.axis_index("tile")
    loads = [
        pltpu.make_async_copy(w_hbm, wbuf, sems.at[0]),
        pltpu.make_async_copy(x_hbm, xbuf, sems.at[1]),
        pltpu.make_async_copy(cot_hbm, cbuf, sems.at[2]),
    ]
    for load in loads:
        load.start()
    for k, value in enumerate(cell_masks(lists_ref, mine, tiles_row, columns)):
        mask_ref[k] = value
    clear_ends(pad, rows, columns)
    loads[0].wait()
    none = jnp.zeros((channels, channels), BF16)
    for row in range(4):
        for out in range(2):
            there = slice(out * channels, (out + 1) * channels)
            for col in range(3):
                start = (row * 3 + col) * channels
                here = slice(start, start + channels)
                tap = row - out
                wide[here, there] = wbuf[tap * 3 + col] if 0 <= tap < 3 else none
                tap = out + 2 - row
                back_ref[there, here] = wbuf[tap * 3 + col] if 0 <= tap < 3 else none
    loads[1].wait()
    loads[2].wait()
    half_bias = 0.5 * bias_ref[...]
    middle = range(2 * HALO, rows - 2 * HALO)
    store = pltpu.make_async_copy(
        obuf, out_hbm.at[pl.ds(middle.start, len(middle))], sems.at[3]
    )

    def body(rate):
        done = set()

        def prepare(row):
            if row in done:
                return
            done.add(row)
            value = xbuf[row] * mask_ref[1]
            spread(value, pad, row, xcat.at[row], rate)
            xt_ref[row] = value.T

        def convolve(pair):
            near, low, high = pair_rows(pair, rate, rows)
            for row in near:
                prepare(row)
            lhs = jnp.concatenate([xcat[row] for row in near], axis=1)
            width = wide.shape[0] // 4
            both = jnp.dot(
                lhs, wide[low * width : high * width], preferred_element_type=F32
            )
            return pair, (both[:, :channels], both[:, channels:])

        def finish(pair, sums):
            for row, value in zip(pair, sums):
                half_pre = 0.5 * value + half_bias
                half_cot = cbuf[row] * mask_ref[1] * 0.5
                if HALO <= row < rows - HALO:
                    grad = silu_grad(half_cot.astype(F32), half_pre)
                    spread(grad, pad, row, gcat_ref.at[row - HALO], -rate)
                    ready.append(row)
                else:
                    here = row if row < HALO else row - (rows - 2 * HALO)
                    pre_ref[here] = half_pre
                    cot_ref[here] = half_cot

        ready = []
        summed = []
        waiting = None
        for pair in row_pairs(rate, range(rows)) + [None]:
            result = convolve(pair) if pair else None
            if waiting:
                finish(*waiting)
            waiting = result
            while len(ready) >= 2:
                grads = [(row, gcat_ref.at[row - HALO]) for row in ready[:2]]
                part = tap_sums(grads, lambda row: xt_ref[row], rate)
                total_ref[...] = total_ref[...] + part if summed else part
                summed.extend(ready[:2])
                del ready[:2]
        for pair in row_pairs(rate, middle):
            sums = input_sums(pair, rate, rows, lambda row: gcat_ref.at[row - HALO], back_ref)
            for row, value in zip(pair, sums):
                value = (value + cbuf[row].astype(F32)).astype(BF16)
                obuf[row - middle.start] = value * mask_ref[1]

    by_rate(rates_ref[0, mine], body)
    store.start()
    store.wait()


def rims_kernel(
    rates_ref, low_ref, high_ref, pre_ref, cot_ref, mask_ref, w_ref,
    grad_low_ref, grad_high_ref, xt_ref,
    pad, xcat,
):
    _, columns, channels = low_ref.shape
    clear_ends(pad, 2 * HALO, columns)

    def body(rate):
        for side, ref in enumerate((low_ref, high_ref)):
            used = range(HALO - rate, HALO) if side == 0 else range(rate)
            for place, k in enumerate(used):
                value = ref[k] * mask_ref[2 * side]
                spread(
                    value, pad, side * HALO + k, xcat.at[pl.ds(place * columns, columns)], rate
                )
                xt_ref[side * HALO + k] = value.T
            taps = jnp.concatenate([w_ref[6 * side + b] for b in range(3)], axis=0)
            sums = jnp.dot(
                xcat[: rate * columns], taps, preferred_element_type=F32
            )
            for k in range(HALO):
                half_pre = pre_ref[side * HALO + k]
                place = k if side == 0 else k - (HALO - rate)
                if 0 <= place < rate:
                    half_pre += 0.5 * sums[place * columns : (place + 1) * columns]
                grad = silu_grad(cot_ref[side * HALO + k].astype(F32), half_pre)
                target = grad_high_ref if side else grad_low_ref
                target[k] = grad.astype(BF16)

    by_rate(rates_ref[0, lax.axis_index("tile")], body)


def taps_kernel(
    rates_ref, grad_low_ref, grad_high_ref, xt_own_ref, xt_halo_ref, total_ref,
    tap_ref, gcat_ref,
    pad, flat, *, scale,
):
    _, columns, channels = grad_low_ref.shape
    rows = xt_own_ref.shape[0]
    clear_ends(pad, 2 * HALO, columns)

    def flipped(row):
        if row < 0:
            return xt_halo_ref[row + HALO]
        return xt_own_ref[row] if row < rows else xt_halo_ref[row - rows + HALO]

    def body(rate):
        grads = []
        for side, ref in enumerate((grad_low_ref, grad_high_ref)):
            for k in range(HALO):
                slot = side * HALO + k
                spread(ref[k], pad, slot, gcat_ref.at[slot], -rate)
                grads.append((k + side * (rows - HALO), gcat_ref.at[slot]))
        total = (total_ref[...] + tap_sums(grads, flipped, rate)) * scale
        for a in range(3):
            for b in range(3):
                start = (a * 3 + b) * channels
                flat[start : start + channels] = total[
                    a * channels : (a + 1) * channels, b * channels : (b + 1) * channels
                ]

    by_rate(rates_ref[0, lax.axis_index("tile")], body)
    share = tap_ref.shape[1]
    for part in range(tap_ref.shape[0]):
        tap_ref[part] = flat[part * share : (part + 1) * share].astype(BF16)


def inputs_kernel(
    rates_ref, gcat_ref, gedge_ref, cot_hbm, mask_ref, back_ref, held_hbm,
    out_hbm, edge_ref,
    cbuf, obuf, sems,
):
    del held_hbm
    rows, columns, channels = cot_hbm.shape
    around = 2 * HALO
    loads = [
        pltpu.make_async_copy(
            cot_hbm.at[pl.ds(side * (rows - around), around)],
            cbuf.at[pl.ds(side * around, around)],
            sems.at[side],
        )
        for side in range(2)
    ]
    stores = [
        pltpu.make_async_copy(
            obuf.at[pl.ds(side * HALO, HALO)],
            out_hbm.at[pl.ds(HALO + side * (rows - 3 * HALO), HALO)],
            sems.at[2 + side],
        )
        for side in range(2)
    ]
    for load in loads:
        load.start()
    for load in loads:
        load.wait()

    def grads(row):
        if row < HALO:
            return gedge_ref.at[row]
        if row < rows - HALO:
            return gcat_ref.at[row - HALO]
        return gedge_ref.at[row - (rows - 2 * HALO)]

    def body(rate):
        for side in range(2):
            start = side * (rows - around)
            for pair in row_pairs(rate, range(start, start + around)):
                sums = input_sums(pair, rate, rows, grads, back_ref)
                for row, value in zip(pair, sums):
                    value = value + cbuf[row - start + side * around].astype(F32)
                    if HALO <= row < rows - HALO:
                        here = row - HALO if side == 0 else row - (rows - around) + HALO
                        obuf[here] = value.astype(BF16) * mask_ref[1]
                    else:
                        here = row if side == 0 else row - (rows - around)
                        edge_ref[here] = value

    by_rate(rates_ref[0, lax.axis_index("tile")], body)
    for store in stores:
        store.start()
    for store in stores:
        store.wait()


def edges_kernel(
    rates_ref, low_ref, high_ref, edge_ref, mask_ref, w_ref, received_ref, held_hbm,
    out_hbm, sum_ref,
    obuf, pad, gcat, sems,
):
    del held_hbm
    _, columns, channels = low_ref.shape
    rows = out_hbm.shape[0]
    mine = lax.axis_index("tile")
    last = rates_ref.shape[1] - 1
    clear_ends(pad, 2 * HALO, columns)
    stores = [
        pltpu.make_async_copy(
            obuf.at[pl.ds(HALO * side, HALO)],
            out_hbm.at[pl.ds((rows - HALO) * side, HALO)],
            sems.at[side],
        )
        for side in range(2)
    ]

    def one_side(side, rate):
        ref = high_ref if side else low_ref
        used = range(rate) if side else range(HALO - rate, HALO)
        for place, k in enumerate(used):
            spread(
                ref[k], pad, side * HALO + k, gcat.at[side, pl.ds(place * columns, columns)], -rate
            )
        taps = jnp.concatenate([w_ref[6 * (1 - side) + b] for b in range(3)], axis=1)
        sums = lax.dot_general(
            gcat[side, : rate * columns],
            taps,
            (((1,), (1,)), ((), ())),
            preferred_element_type=F32,
        )
        for k in range(HALO):
            value = edge_ref[side * HALO + k]
            place = k - (HALO - rate) if side else k
            if 0 <= place < rate:
                value = value + sums[place * columns : (place + 1) * columns]
            obuf[side * HALO + k] = value.astype(BF16) * mask_ref[1]

    near = (jnp.maximum(mine - 1, 0), jnp.minimum(mine + 1, last))
    for side in range(2):
        by_rate(rates_ref[0, near[side]], lambda rate, side=side: one_side(side, rate))
        stores[side].start()
    if sum_ref.shape == received_ref.shape[1:]:
        sum_ref[...] = jnp.sum(received_ref[...].astype(F32), axis=0)
    for store in stores:
        store.wait()


def exchange(to_next, to_previous, axis):
    count = lax.axis_size(axis)
    forward = [(i, i + 1) for i in range(count - 1)]
    backward = [(target, source) for source, target in forward]
    return lax.ppermute(to_next, axis, forward), lax.ppermute(to_previous, axis, backward)


def call(kernel, name, outs, specs, scratch, aliases=None):
    memory = {"s": pltpu.SMEM, "v": pltpu.VMEM, "h": pltpu.HBM}
    ins, results = (
        [pl.BlockSpec(memory_space=memory[letter]) for letter in part] for part in specs.split(">")
    )
    return pl.pallas_call(
        kernel,
        name=name,
        out_shape=tuple(jax.ShapeDtypeStruct(shape, dtype) for shape, dtype in outs),
        in_specs=ins,
        out_specs=tuple(results),
        scratch_shapes=scratch,
        input_output_aliases=aliases or {},
        cost_estimate=pl.CostEstimate(flops=0, bytes_accessed=0, transcendentals=0),
        compiler_params=pltpu.CompilerParams(vmem_limit_bytes=VMEM_LIMIT),
    )


def in_hbm(array):
    return pltpu.with_memory_space_constraint(array, pltpu.HBM)


def shards(features, cotangent, tile_mask, work_lists, dilations, conv_weight, conv_bias):
    x, cot, lists = features[0], in_hbm(cotangent[0]), in_hbm(work_lists[0])
    dilations = in_hbm(dilations)
    rows, columns, channels = x.shape
    axes = ("tile", "dp")
    devices = lax.axis_size("tile") * lax.axis_size("dp")
    weight = in_hbm(conv_weight.reshape(9, channels, channels))
    bias = in_hbm(conv_bias.reshape(1, channels))
    inner = rows - 2 * HALO
    wide_row = 3 * channels
    whole = ((rows, columns, channels), BF16)

    def pads(count):
        return pltpu.VMEM((count, columns + 2 * EDGE, channels), F32)

    low, high = exchange(x[rows - HALO :], x[:HALO], "tile")

    held, pre, gcat, xt, total, mask, cot_edge, back = call(
        first_kernel,
        "first",
        [
            whole,
            ((2 * HALO, columns, channels), F32),
            ((inner, columns, wide_row), BF16),
            ((rows, channels, columns), BF16),
            ((wide_row, wide_row), F32),
            ((3, columns, channels), BF16),
            ((2 * HALO, columns, channels), BF16),
            ((2 * channels, 4 * wide_row), BF16),
        ],
        "svhhhv>hvvvvvvv",
        [
            pltpu.VMEM((rows, columns, channels), BF16),
            pltpu.VMEM((rows, columns, channels), BF16),
            pltpu.VMEM((9, channels, channels), BF16),
            pltpu.VMEM((rows - 4 * HALO, columns, channels), BF16),
            pads(rows),
            pltpu.VMEM((rows, columns, wide_row), BF16),
            pltpu.VMEM((4 * wide_row, 2 * channels), BF16),
            pltpu.SemaphoreType.DMA((4,)),
        ],
    )(dilations, lists, in_hbm(x), cot, weight, bias)

    grad_low, grad_high, xt_halo = call(
        rims_kernel,
        "rims",
        [
            ((HALO, columns, channels), BF16),
            ((HALO, columns, channels), BF16),
            ((2 * HALO, channels, columns), BF16),
        ],
        "svvvvvv>vvv",
        [pads(2 * HALO), pltpu.VMEM((HALO * columns, wide_row), BF16)],
    )(dilations, low, high, pre, cot_edge, mask, weight)

    from_low, from_high = exchange(grad_high, grad_low, "tile")

    tap_rows = 9 * channels
    direct = tap_rows % devices == 0
    share = (devices, tap_rows // devices) if direct else (1, tap_rows)
    scale = 1.0 / math.sqrt(devices * lists.shape[1] * TILE * TILE)
    taps, gedge = call(
        lambda *refs: taps_kernel(*refs, scale=scale),
        "taps",
        [(share + (channels,), BF16), ((2 * HALO, columns, wide_row), BF16)],
        "svvvvv>vv",
        [pads(2 * HALO), pltpu.VMEM((tap_rows, channels), F32)],
    )(dilations, grad_low, grad_high, xt, xt_halo, total)
    if not direct:
        taps = taps.reshape(devices, -1)
    received = lax.all_to_all(taps, axes, 0, 0, tiled=True)

    held, edge = call(
        inputs_kernel,
        "inputs",
        [whole, ((2 * HALO, columns, channels), F32)],
        "svvhvvh>hv",
        [
            pltpu.VMEM((4 * HALO, columns, channels), BF16),
            pltpu.VMEM((2 * HALO, columns, channels), BF16),
            pltpu.SemaphoreType.DMA((4,)),
        ],
        {6: 0},
    )(dilations, gcat, gedge, cot, mask, back, held)

    part = received.shape[1:] if direct else (8, LANES)
    input_grad, summed = call(
        edges_kernel,
        "edges",
        [whole, (part, F32)],
        "svvvvvvh>hv",
        [
            pltpu.VMEM((2 * HALO, columns, channels), BF16),
            pads(2 * HALO),
            pltpu.VMEM((2, HALO * columns, wide_row), BF16),
            pltpu.SemaphoreType.DMA((2,)),
        ],
        {7: 0},
    )(dilations, from_low, from_high, edge, mask, weight, received if direct else mask, held)
    if not direct:
        summed = jnp.sum(received.astype(F32), axis=0)
    return (input_grad[None], summed.reshape(-1))


def solution(mesh):
    placed = (
        P("dp", "tile", None, None),
        P("dp", "tile", None, None),
        P("dp", "tile", None),
        P("dp", None, None),
        P("dp", None),
        P(),
        P(),
    )
    return jax.shard_map(
        shards,
        mesh=mesh,
        in_specs=placed,
        out_specs=(P("dp", "tile", None, None), P(("tile", "dp"))),
        check_vma=False,
    )
```

```python
import math

import jax
import jax.numpy as jnp
from jax import lax
from jax.experimental import pallas as pl
from jax.experimental.pallas import tpu as pltpu
from jax.sharding import PartitionSpec as P

TILE = 12
HALO = 2
LANES = 128
EDGE = 8
RATES = (1, 2)
VMEM_LIMIT = 40 * 1024 * 1024
BUSY = 20_000_000_000

F32 = jnp.float32
BF16 = jnp.bfloat16


def cell_masks(lists_ref, middle, tiles_row, columns):
    ids = lists_ref[...]
    workers, width = ids.shape
    tile = lax.broadcasted_iota(jnp.int32, (3 * tiles_row, width), 0)
    target = (middle - 1) * tiles_row + tile
    found = ids[0:1] == target
    for worker in range(1, workers):
        found = found | (ids[worker : worker + 1] == target)
    named = jnp.dot(
        jnp.where(found, 1.0, 0.0).astype(BF16),
        jnp.ones((width, LANES), BF16),
        preferred_element_type=F32,
    ).astype(BF16)
    first = TILE * lax.broadcasted_iota(jnp.int32, (columns, tiles_row), 1)
    cell = lax.broadcasted_iota(jnp.int32, (columns, tiles_row), 0)
    inside = jnp.where((cell >= first) & (cell < first + TILE), 1.0, 0.0).astype(BF16)
    return [
        jnp.dot(
            inside, named[k * tiles_row : (k + 1) * tiles_row], preferred_element_type=F32
        ).astype(BF16)
        for k in range(3)
    ]


def row_pairs(rate, rows):
    rows = list(rows)
    pairs = []
    for start in range(0, len(rows), 2 * rate):
        for k in range(rate):
            pairs.append((rows[start + k], rows[start + k + rate]))
    return pairs


def by_rate(rate, body):
    for value in RATES:
        pl.when(rate == value)(lambda value=value: body(value))


def clear_ends(pad_ref, count, columns):
    ends = jnp.zeros((EDGE, pad_ref.shape[-1]), F32)
    for k in range(count):
        pad_ref[k, :EDGE] = ends
        pad_ref[k, EDGE + columns :] = ends


def spread(value, pad_ref, slot, target_ref, offset):
    columns, channels = value.shape
    pad_ref[slot, EDGE : EDGE + columns] = value.astype(F32)
    target_ref[:, :channels] = pad_ref[slot, pl.ds(EDGE - offset, columns)].astype(BF16)
    target_ref[:, channels : 2 * channels] = value.astype(BF16)
    target_ref[:, 2 * channels :] = pad_ref[slot, pl.ds(EDGE + offset, columns)].astype(BF16)


def silu_grad(half_cot, half_pre):
    turn = jnp.tanh(half_pre)
    return half_cot * (1.0 + turn + half_pre * (1.0 - turn * turn))


def tap_sums(grads, xts, rate):
    flipped = jnp.concatenate(
        [
            jnp.concatenate([xts(row + rate * a) for row, _ in grads], axis=1)
            for a in (-1, 0, 1)
        ],
        axis=0,
    )
    return jnp.dot(
        flipped,
        jnp.concatenate([ref[...] for _, ref in grads], axis=0),
        preferred_element_type=F32,
    )


def pair_rows(pair, rate, rows):
    reach = [pair[0] + rate * (k - 1) for k in range(4)]
    inside = [k for k in range(4) if 0 <= reach[k] < rows]
    return [reach[k] for k in inside], inside[0], inside[-1] + 1


def input_sums(pair, rate, rows, grads, wide_ref):
    near, low, high = pair_rows(pair, rate, rows)
    lhs = jnp.concatenate([grads(row)[...] for row in near], axis=1)
    width = wide_ref.shape[0] // 4
    both = jnp.dot(lhs, wide_ref[low * width : high * width], preferred_element_type=F32)
    half = both.shape[1] // 2
    return both[:, :half], both[:, half:]


def first_kernel(
    rates_ref, lists_ref, x_hbm, cot_hbm, w_hbm, bias_ref,
    out_hbm, pre_ref, gcat_ref, xt_ref, total_ref, mask_ref, cot_ref, back_ref, near_ref, far_ref,
    xbuf, cbuf, wbuf, obuf, pad, xcat, wide, sems,
):
    rows, columns, channels = x_hbm.shape
    tiles_row = columns // TILE
    mine = lax.axis_index("tile")
    loads = [
        pltpu.make_async_copy(w_hbm, wbuf, sems.at[0]),
        pltpu.make_async_copy(x_hbm, xbuf, sems.at[1]),
        pltpu.make_async_copy(cot_hbm, cbuf, sems.at[2]),
    ]
    for load in loads:
        load.start()
    for k, value in enumerate(cell_masks(lists_ref, mine, tiles_row, columns)):
        mask_ref[k] = value
    clear_ends(pad, rows, columns)
    loads[0].wait()
    none = jnp.zeros((channels, channels), BF16)
    for col in range(3):
        there = slice(col * channels, (col + 1) * channels)
        turned = [wbuf[tap * 3 + col].T for tap in range(3)]
        for side in range(2):
            near_ref[side, there] = wbuf[6 * side + col]
            far_ref[side, there] = turned[2 - 2 * side]
        for row in range(4):
            start = (row * 3 + col) * channels
            here = slice(start, start + channels)
            for out in range(2):
                there = slice(out * channels, (out + 1) * channels)
                tap = row - out
                wide[here, there] = wbuf[tap * 3 + col] if 0 <= tap < 3 else none
                tap = out + 2 - row
                back_ref[here, there] = turned[tap] if 0 <= tap < 3 else none
    loads[1].wait()
    loads[2].wait()
    half_bias = 0.5 * bias_ref[...]
    middle = range(2 * HALO, rows - 2 * HALO)
    store = pltpu.make_async_copy(
        obuf, out_hbm.at[pl.ds(middle.start, len(middle))], sems.at[3]
    )

    def body(rate):
        done = set()

        def prepare(row):
            if row in done:
                return
            done.add(row)
            value = xbuf[row] * mask_ref[1]
            spread(value, pad, row, xcat.at[row], rate)
            xt_ref[row] = value.T

        def convolve(pair):
            near, low, high = pair_rows(pair, rate, rows)
            for row in near:
                prepare(row)
            lhs = jnp.concatenate([xcat[row] for row in near], axis=1)
            width = wide.shape[0] // 4
            both = jnp.dot(
                lhs, wide[low * width : high * width], preferred_element_type=F32
            )
            return pair, (both[:, :channels], both[:, channels:])

        def finish(pair, sums):
            for row, value in zip(pair, sums):
                half_pre = 0.5 * value + half_bias
                half_cot = cbuf[row] * mask_ref[1] * 0.5
                if HALO <= row < rows - HALO:
                    grad = silu_grad(half_cot.astype(F32), half_pre)
                    spread(grad, pad, row, gcat_ref.at[row - HALO], -rate)
                    ready.append(row)
                else:
                    here = row if row < HALO else row - (rows - 2 * HALO)
                    pre_ref[here] = half_pre
                    cot_ref[here] = half_cot

        ready = []
        summed = []
        waiting = None
        for pair in row_pairs(rate, range(rows)) + [None]:
            result = convolve(pair) if pair else None
            if waiting:
                finish(*waiting)
            waiting = result
            while len(ready) >= 2:
                grads = [(row, gcat_ref.at[row - HALO]) for row in ready[:2]]
                part = tap_sums(grads, lambda row: xt_ref[row], rate)
                total_ref[...] = total_ref[...] + part if summed else part
                summed.extend(ready[:2])
                del ready[:2]
        for pair in row_pairs(rate, middle):
            sums = input_sums(pair, rate, rows, lambda row: gcat_ref.at[row - HALO], back_ref)
            for row, value in zip(pair, sums):
                value = (value + cbuf[row].astype(F32)).astype(BF16)
                obuf[row - middle.start] = value * mask_ref[1]

    by_rate(rates_ref[0, mine], body)
    store.start()
    store.wait()


def rims_kernel(
    rates_ref, low_ref, high_ref, pre_ref, cot_ref, mask_ref, near_ref,
    grad_low_ref, grad_high_ref, xt_ref,
    pad, xcat,
):
    _, columns, channels = low_ref.shape
    clear_ends(pad, 2 * HALO, columns)

    def body(rate):
        for side, ref in enumerate((low_ref, high_ref)):
            used = range(HALO - rate, HALO) if side == 0 else range(rate)
            for place, k in enumerate(used):
                value = ref[k] * mask_ref[2 * side]
                spread(
                    value, pad, side * HALO + k, xcat.at[pl.ds(place * columns, columns)], rate
                )
                xt_ref[side * HALO + k] = value.T
            sums = jnp.dot(
                xcat[: rate * columns], near_ref[side], preferred_element_type=F32
            )
            for k in range(HALO):
                half_pre = pre_ref[side * HALO + k]
                place = k if side == 0 else k - (HALO - rate)
                if 0 <= place < rate:
                    half_pre += 0.5 * sums[place * columns : (place + 1) * columns]
                grad = silu_grad(cot_ref[side * HALO + k].astype(F32), half_pre)
                target = grad_high_ref if side else grad_low_ref
                target[k] = grad.astype(BF16)

    by_rate(rates_ref[0, lax.axis_index("tile")], body)


def second_kernel(
    rates_ref, grad_low_ref, grad_high_ref, xt_own_ref, xt_halo_ref, total_ref,
    gcat_ref, cot_hbm, mask_ref, back_ref, held_hbm,
    out_hbm, edge_ref, tap_ref,
    cbuf, obuf, pad, gedge, flat, sems, *, scale,
):
    del held_hbm
    rows, columns, channels = cot_hbm.shape
    around = 2 * HALO
    loads = [
        pltpu.make_async_copy(
            cot_hbm.at[pl.ds(side * (rows - around), around)],
            cbuf.at[pl.ds(side * around, around)],
            sems.at[side],
        )
        for side in range(2)
    ]
    stores = [
        pltpu.make_async_copy(
            obuf.at[pl.ds(side * HALO, HALO)],
            out_hbm.at[pl.ds(HALO + side * (rows - 3 * HALO), HALO)],
            sems.at[2 + side],
        )
        for side in range(2)
    ]
    for load in loads:
        load.start()
    clear_ends(pad, 2 * HALO, columns)
    for load in loads:
        load.wait()

    def flipped(row):
        if row < 0:
            return xt_halo_ref[row + HALO]
        return xt_own_ref[row] if row < rows else xt_halo_ref[row - rows + HALO]

    def grads(row):
        if row < HALO:
            return gedge.at[row]
        if row < rows - HALO:
            return gcat_ref.at[row - HALO]
        return gedge.at[row - (rows - 2 * HALO)]

    def body(rate):
        edges = []
        for side, ref in enumerate((grad_low_ref, grad_high_ref)):
            for k in range(HALO):
                slot = side * HALO + k
                spread(ref[k], pad, slot, gedge.at[slot], -rate)
                edges.append((k + side * (rows - HALO), gedge.at[slot]))
        for side in range(2):
            start = side * (rows - around)
            for pair in row_pairs(rate, range(start, start + around)):
                sums = input_sums(pair, rate, rows, grads, back_ref)
                for row, value in zip(pair, sums):
                    value = value + cbuf[row - start + side * around].astype(F32)
                    if HALO <= row < rows - HALO:
                        here = row - HALO if side == 0 else row - (rows - around) + HALO
                        obuf[here] = value.astype(BF16) * mask_ref[1]
                    else:
                        here = row if side == 0 else row - (rows - around)
                        edge_ref[here] = value
            stores[side].start()
        total = (total_ref[...] + tap_sums(edges, flipped, rate)) * scale
        for a in range(3):
            for b in range(3):
                start = (a * 3 + b) * channels
                flat[start : start + channels] = total[
                    a * channels : (a + 1) * channels, b * channels : (b + 1) * channels
                ]

    by_rate(rates_ref[0, lax.axis_index("tile")], body)
    share = tap_ref.shape[1]
    for part in range(tap_ref.shape[0]):
        tap_ref[part] = flat[part * share : (part + 1) * share].astype(BF16)
    for store in stores:
        store.wait()


def edges_kernel(
    rates_ref, low_ref, high_ref, edge_ref, mask_ref, far_ref, received_ref, held_hbm,
    out_hbm, sum_ref,
    obuf, pad, gcat, sems,
):
    del held_hbm
    _, columns, channels = low_ref.shape
    rows = out_hbm.shape[0]
    mine = lax.axis_index("tile")
    last = rates_ref.shape[1] - 1
    clear_ends(pad, 2 * HALO, columns)
    stores = [
        pltpu.make_async_copy(
            obuf.at[pl.ds(HALO * side, HALO)],
            out_hbm.at[pl.ds((rows - HALO) * side, HALO)],
            sems.at[side],
        )
        for side in range(2)
    ]

    def one_side(side, rate):
        ref = high_ref if side else low_ref
        used = range(rate) if side else range(HALO - rate, HALO)
        for place, k in enumerate(used):
            spread(
                ref[k], pad, side * HALO + k, gcat.at[side, pl.ds(place * columns, columns)], -rate
            )
        sums = jnp.dot(
            gcat[side, : rate * columns], far_ref[side], preferred_element_type=F32
        )
        for k in range(HALO):
            value = edge_ref[side * HALO + k]
            place = k - (HALO - rate) if side else k
            if 0 <= place < rate:
                value = value + sums[place * columns : (place + 1) * columns]
            obuf[side * HALO + k] = value.astype(BF16) * mask_ref[1]

    near = (jnp.maximum(mine - 1, 0), jnp.minimum(mine + 1, last))
    for side in range(2):
        by_rate(rates_ref[0, near[side]], lambda rate, side=side: one_side(side, rate))
        stores[side].start()
    if sum_ref.shape == received_ref.shape[1:]:
        sum_ref[...] = jnp.sum(received_ref[...].astype(F32), axis=0)
    for store in stores:
        store.wait()


def exchange(to_next, to_previous, axis):
    count = lax.axis_size(axis)
    forward = [(i, i + 1) for i in range(count - 1)]
    backward = [(target, source) for source, target in forward]
    return lax.ppermute(to_next, axis, forward), lax.ppermute(to_previous, axis, backward)


def call(kernel, name, outs, specs, scratch, aliases=None, flops=0):
    memory = {"s": pltpu.SMEM, "v": pltpu.VMEM, "h": pltpu.HBM}
    ins, results = (
        [pl.BlockSpec(memory_space=memory[letter]) for letter in part] for part in specs.split(">")
    )
    return pl.pallas_call(
        kernel,
        name=name,
        out_shape=tuple(jax.ShapeDtypeStruct(shape, dtype) for shape, dtype in outs),
        in_specs=ins,
        out_specs=tuple(results),
        scratch_shapes=scratch,
        input_output_aliases=aliases or {},
        cost_estimate=pl.CostEstimate(flops=flops, bytes_accessed=0, transcendentals=0),
        compiler_params=pltpu.CompilerParams(vmem_limit_bytes=VMEM_LIMIT),
    )


def in_hbm(array):
    return pltpu.with_memory_space_constraint(array, pltpu.HBM)


def shards(features, cotangent, tile_mask, work_lists, dilations, conv_weight, conv_bias):
    x, cot, lists = features[0], in_hbm(cotangent[0]), in_hbm(work_lists[0])
    dilations = in_hbm(dilations)
    rows, columns, channels = x.shape
    axes = ("tile", "dp")
    devices = lax.axis_size("tile") * lax.axis_size("dp")
    weight = in_hbm(conv_weight.reshape(9, channels, channels))
    bias = in_hbm(conv_bias.reshape(1, channels))
    inner = rows - 2 * HALO
    wide_row = 3 * channels
    whole = ((rows, columns, channels), BF16)

    def pads(count):
        return pltpu.VMEM((count, columns + 2 * EDGE, channels), F32)

    low, high = exchange(x[rows - HALO :], x[:HALO], "tile")

    held, pre, gcat, xt, total, mask, cot_edge, back, near, far = call(
        first_kernel,
        "first",
        [
            whole,
            ((2 * HALO, columns, channels), F32),
            ((inner, columns, wide_row), BF16),
            ((rows, channels, columns), BF16),
            ((wide_row, wide_row), F32),
            ((3, columns, channels), BF16),
            ((2 * HALO, columns, channels), BF16),
            ((4 * wide_row, 2 * channels), BF16),
            ((2, wide_row, channels), BF16),
            ((2, wide_row, channels), BF16),
        ],
        "svhhhv>hvvvvvvvvv",
        [
            pltpu.VMEM((rows, columns, channels), BF16),
            pltpu.VMEM((rows, columns, channels), BF16),
            pltpu.VMEM((9, channels, channels), BF16),
            pltpu.VMEM((rows - 4 * HALO, columns, channels), BF16),
            pads(rows),
            pltpu.VMEM((rows, columns, wide_row), BF16),
            pltpu.VMEM((4 * wide_row, 2 * channels), BF16),
            pltpu.SemaphoreType.DMA((4,)),
        ],
        flops=BUSY,
    )(dilations, lists, in_hbm(x), cot, weight, bias)

    grad_low, grad_high, xt_halo = call(
        rims_kernel,
        "rims",
        [
            ((HALO, columns, channels), BF16),
            ((HALO, columns, channels), BF16),
            ((2 * HALO, channels, columns), BF16),
        ],
        "svvvvvv>vvv",
        [pads(2 * HALO), pltpu.VMEM((HALO * columns, wide_row), BF16)],
    )(dilations, low, high, pre, cot_edge, mask, near)

    from_low, from_high = exchange(grad_high, grad_low, "tile")

    tap_rows = 9 * channels
    direct = tap_rows % devices == 0
    share = (devices, tap_rows // devices) if direct else (1, tap_rows)
    scale = 1.0 / math.sqrt(devices * lists.shape[1] * TILE * TILE)
    held, edge, taps = call(
        lambda *refs: second_kernel(*refs, scale=scale),
        "second",
        [whole, ((2 * HALO, columns, channels), F32), (share + (channels,), BF16)],
        "svvvvvvhvvh>hvv",
        [
            pltpu.VMEM((4 * HALO, columns, channels), BF16),
            pltpu.VMEM((2 * HALO, columns, channels), BF16),
            pads(2 * HALO),
            pltpu.VMEM((2 * HALO, columns, wide_row), BF16),
            pltpu.VMEM((tap_rows, channels), F32),
            pltpu.SemaphoreType.DMA((4,)),
        ],
        {10: 0},
        flops=BUSY,
    )(dilations, grad_low, grad_high, xt, xt_halo, total, gcat, cot, mask, back, held)
    if not direct:
        taps = taps.reshape(devices, -1)
    received = lax.all_to_all(taps, axes, 0, 0, tiled=True)

    part = received.shape[1:] if direct else (8, LANES)
    input_grad, summed = call(
        edges_kernel,
        "edges",
        [whole, (part, F32)],
        "svvvvvvh>hv",
        [
            pltpu.VMEM((2 * HALO, columns, channels), BF16),
            pads(2 * HALO),
            pltpu.VMEM((2, HALO * columns, wide_row), BF16),
            pltpu.SemaphoreType.DMA((2,)),
        ],
        {7: 0},
    )(dilations, from_low, from_high, edge, mask, far, received if direct else mask, held)
    if not direct:
        summed = jnp.sum(received.astype(F32), axis=0)
    return (input_grad[None], summed.reshape(-1))


def solution(mesh):
    placed = (
        P("dp", "tile", None, None),
        P("dp", "tile", None, None),
        P("dp", "tile", None),
        P("dp", None, None),
        P("dp", None),
        P(),
        P(),
    )
    return jax.shard_map(
        shards,
        mesh=mesh,
        in_specs=placed,
        out_specs=(P("dp", "tile", None, None), P(("tile", "dp"))),
        check_vma=False,
    )
```

```python
import math

import jax
import jax.numpy as jnp
from jax import lax
from jax.experimental import pallas as pl
from jax.experimental.pallas import tpu as pltpu
from jax.sharding import PartitionSpec as P

TILE = 12
HALO = 2
LANES = 128
EDGE = 8
RATES = (1, 2)
VMEM_LIMIT = 40 * 1024 * 1024
BUSY = 20_000_000_000

F32 = jnp.float32
BF16 = jnp.bfloat16


def cell_masks(lists_ref, middle, tiles_row, columns):
    ids = lists_ref[...]
    workers, width = ids.shape
    tile = lax.broadcasted_iota(jnp.int32, (3 * tiles_row, width), 0)
    target = (middle - 1) * tiles_row + tile
    found = ids[0:1] == target
    for worker in range(1, workers):
        found = found | (ids[worker : worker + 1] == target)
    named = jnp.dot(
        jnp.where(found, 1.0, 0.0).astype(BF16),
        jnp.ones((width, LANES), BF16),
        preferred_element_type=F32,
    ).astype(BF16)
    first = TILE * lax.broadcasted_iota(jnp.int32, (columns, tiles_row), 1)
    cell = lax.broadcasted_iota(jnp.int32, (columns, tiles_row), 0)
    inside = jnp.where((cell >= first) & (cell < first + TILE), 1.0, 0.0).astype(BF16)
    return [
        jnp.dot(
            inside, named[k * tiles_row : (k + 1) * tiles_row], preferred_element_type=F32
        ).astype(BF16)
        for k in range(3)
    ]


def row_pairs(rate, rows):
    rows = list(rows)
    pairs = []
    for start in range(0, len(rows), 2 * rate):
        for k in range(rate):
            pairs.append((rows[start + k], rows[start + k + rate]))
    return pairs


def by_rate(rate, body):
    for value in RATES:
        pl.when(rate == value)(lambda value=value: body(value))


def clear_ends(pad_ref, count, columns):
    ends = jnp.zeros((EDGE, pad_ref.shape[-1]), F32)
    for k in range(count):
        pad_ref[k, :EDGE] = ends
        pad_ref[k, EDGE + columns :] = ends


def spread(value, pad_ref, slot, target_ref, offset):
    columns, channels = value.shape
    pad_ref[slot, EDGE : EDGE + columns] = value.astype(F32)
    target_ref[:, :channels] = pad_ref[slot, pl.ds(EDGE - offset, columns)].astype(BF16)
    target_ref[:, channels : 2 * channels] = value.astype(BF16)
    target_ref[:, 2 * channels :] = pad_ref[slot, pl.ds(EDGE + offset, columns)].astype(BF16)


def silu_grad(half_cot, half_pre):
    turn = jnp.tanh(half_pre)
    return half_cot * (1.0 + turn + half_pre * (1.0 - turn * turn))


def tap_sums(grads, xts, rate):
    flipped = jnp.concatenate(
        [
            jnp.concatenate([xts(row + rate * a) for row, _ in grads], axis=1)
            for a in (-1, 0, 1)
        ],
        axis=0,
    )
    return jnp.dot(
        flipped,
        jnp.concatenate([ref[...] for _, ref in grads], axis=0),
        preferred_element_type=F32,
    )


def pair_rows(pair, rate, rows):
    reach = [pair[0] + rate * (k - 1) for k in range(4)]
    inside = [k for k in range(4) if 0 <= reach[k] < rows]
    return [reach[k] for k in inside], inside[0], inside[-1] + 1


def input_sums(pair, rate, rows, grads, wide_ref):
    near, low, high = pair_rows(pair, rate, rows)
    lhs = jnp.concatenate([grads(row)[...] for row in near], axis=1)
    width = wide_ref.shape[0] // 4
    both = jnp.dot(lhs, wide_ref[low * width : high * width], preferred_element_type=F32)
    half = both.shape[1] // 2
    return both[:, :half], both[:, half:]


def first_kernel(
    rates_ref, lists_ref, x_hbm, cot_hbm, w_hbm, bias_ref,
    out_hbm, pre_ref, gcat_ref, xt_ref, total_ref, mask_ref, cot_ref, back_ref, near_ref, far_ref,
    xbuf, cbuf, wbuf, obuf, pad, xcat, wide, sems,
):
    rows, columns, channels = x_hbm.shape
    tiles_row = columns // TILE
    mine = lax.axis_index("tile")
    loads = [
        pltpu.make_async_copy(w_hbm, wbuf, sems.at[0]),
        pltpu.make_async_copy(x_hbm, xbuf, sems.at[1]),
        pltpu.make_async_copy(cot_hbm, cbuf, sems.at[2]),
    ]
    for load in loads:
        load.start()
    for k, value in enumerate(cell_masks(lists_ref, mine, tiles_row, columns)):
        mask_ref[k] = value
    clear_ends(pad, rows, columns)
    loads[0].wait()
    none = jnp.zeros((channels, channels), BF16)
    for col in range(3):
        there = slice(col * channels, (col + 1) * channels)
        turned = [wbuf[tap * 3 + col].T for tap in range(3)]
        for side in range(2):
            near_ref[side, there] = wbuf[6 * side + col]
            far_ref[side, there] = turned[2 - 2 * side]
        for row in range(4):
            start = (row * 3 + col) * channels
            here = slice(start, start + channels)
            for out in range(2):
                there = slice(out * channels, (out + 1) * channels)
                tap = row - out
                wide[here, there] = wbuf[tap * 3 + col] if 0 <= tap < 3 else none
                tap = out + 2 - row
                back_ref[here, there] = turned[tap] if 0 <= tap < 3 else none
    loads[1].wait()
    loads[2].wait()
    half_bias = 0.5 * bias_ref[...]
    middle = range(2 * HALO, rows - 2 * HALO)
    store = pltpu.make_async_copy(
        obuf, out_hbm.at[pl.ds(middle.start, len(middle))], sems.at[3]
    )

    def body(rate):
        done = set()

        def prepare(row):
            if row in done:
                return
            done.add(row)
            value = xbuf[row] * mask_ref[1]
            spread(value, pad, row, xcat.at[row], rate)
            xt_ref[row] = value.T

        def convolve(pair):
            near, low, high = pair_rows(pair, rate, rows)
            for row in near:
                prepare(row)
            lhs = jnp.concatenate([xcat[row] for row in near], axis=1)
            width = wide.shape[0] // 4
            both = jnp.dot(
                lhs, wide[low * width : high * width], preferred_element_type=F32
            )
            return pair, (both[:, :channels], both[:, channels:])

        def finish(pair, sums):
            for row, value in zip(pair, sums):
                half_pre = 0.5 * value + half_bias
                half_cot = cbuf[row] * mask_ref[1] * 0.5
                if HALO <= row < rows - HALO:
                    grad = silu_grad(half_cot.astype(F32), half_pre)
                    spread(grad, pad, row, gcat_ref.at[row - HALO], -rate)
                    ready.append(row)
                else:
                    here = row if row < HALO else row - (rows - 2 * HALO)
                    pre_ref[here] = half_pre
                    cot_ref[here] = half_cot

        ready = []
        summed = []
        waiting = None
        for pair in row_pairs(rate, range(rows)) + [None]:
            result = convolve(pair) if pair else None
            if waiting:
                finish(*waiting)
            waiting = result
            while len(ready) >= 2:
                grads = [(row, gcat_ref.at[row - HALO]) for row in ready[:2]]
                part = tap_sums(grads, lambda row: xt_ref[row], rate)
                total_ref[...] = total_ref[...] + part if summed else part
                summed.extend(ready[:2])
                del ready[:2]
        for pair in row_pairs(rate, middle):
            sums = input_sums(pair, rate, rows, lambda row: gcat_ref.at[row - HALO], back_ref)
            for row, value in zip(pair, sums):
                value = (value + cbuf[row].astype(F32)).astype(BF16)
                obuf[row - middle.start] = value * mask_ref[1]

    by_rate(rates_ref[0, mine], body)
    store.start()
    store.wait()


def rims_kernel(
    rates_ref, low_ref, high_ref, pre_ref, cot_ref, mask_ref, near_ref,
    grad_low_ref, grad_high_ref, xt_ref,
    pad, xcat,
):
    _, columns, channels = low_ref.shape
    clear_ends(pad, 2 * HALO, columns)

    def body(rate):
        for side, ref in enumerate((low_ref, high_ref)):
            used = range(HALO - rate, HALO) if side == 0 else range(rate)
            for place, k in enumerate(used):
                value = ref[k] * mask_ref[2 * side]
                spread(
                    value, pad, side * HALO + k, xcat.at[pl.ds(place * columns, columns)], rate
                )
                xt_ref[side * HALO + k] = value.T
            sums = jnp.dot(
                xcat[: rate * columns], near_ref[side], preferred_element_type=F32
            )
            for k in range(HALO):
                half_pre = pre_ref[side * HALO + k]
                place = k if side == 0 else k - (HALO - rate)
                if 0 <= place < rate:
                    half_pre += 0.5 * sums[place * columns : (place + 1) * columns]
                grad = silu_grad(cot_ref[side * HALO + k].astype(F32), half_pre)
                target = grad_high_ref if side else grad_low_ref
                target[k] = grad.astype(BF16)

    by_rate(rates_ref[0, lax.axis_index("tile")], body)


def second_kernel(
    rates_ref, grad_low_ref, grad_high_ref, xt_own_ref, xt_halo_ref, total_ref,
    gcat_ref, cot_hbm, mask_ref, back_ref, held_hbm,
    out_hbm, edge_ref, tap_ref,
    cbuf, obuf, pad, gedge, flat, sems, *, scale,
):
    del held_hbm
    rows, columns, channels = cot_hbm.shape
    around = 2 * HALO
    loads = [
        pltpu.make_async_copy(
            cot_hbm.at[pl.ds(side * (rows - around), around)],
            cbuf.at[pl.ds(side * around, around)],
            sems.at[side],
        )
        for side in range(2)
    ]
    stores = [
        pltpu.make_async_copy(
            obuf.at[pl.ds(side * HALO, HALO)],
            out_hbm.at[pl.ds(HALO + side * (rows - 3 * HALO), HALO)],
            sems.at[2 + side],
        )
        for side in range(2)
    ]
    for load in loads:
        load.start()
    clear_ends(pad, 2 * HALO, columns)
    for load in loads:
        load.wait()

    def flipped(row):
        if row < 0:
            return xt_halo_ref[row + HALO]
        return xt_own_ref[row] if row < rows else xt_halo_ref[row - rows + HALO]

    def grads(row):
        if row < HALO:
            return gedge.at[row]
        if row < rows - HALO:
            return gcat_ref.at[row - HALO]
        return gedge.at[row - (rows - 2 * HALO)]

    def body(rate):
        edges = []
        for side, ref in enumerate((grad_low_ref, grad_high_ref)):
            for k in range(HALO):
                slot = side * HALO + k
                spread(ref[k], pad, slot, gedge.at[slot], -rate)
                edges.append((k + side * (rows - HALO), gedge.at[slot]))
        for side in range(2):
            start = side * (rows - around)
            for pair in row_pairs(rate, range(start, start + around)):
                sums = input_sums(pair, rate, rows, grads, back_ref)
                for row, value in zip(pair, sums):
                    value = value + cbuf[row - start + side * around].astype(F32)
                    if HALO <= row < rows - HALO:
                        here = row - HALO if side == 0 else row - (rows - around) + HALO
                        obuf[here] = value.astype(BF16) * mask_ref[1]
                    else:
                        here = row if side == 0 else row - (rows - around)
                        edge_ref[here] = value
            stores[side].start()
        total = (total_ref[...] + tap_sums(edges, flipped, rate)) * scale
        for a in range(3):
            for b in range(3):
                start = (a * 3 + b) * channels
                flat[start : start + channels] = total[
                    a * channels : (a + 1) * channels, b * channels : (b + 1) * channels
                ]

    by_rate(rates_ref[0, lax.axis_index("tile")], body)
    share = tap_ref.shape[1]
    for part in range(tap_ref.shape[0]):
        tap_ref[part] = flat[part * share : (part + 1) * share].astype(BF16)
    for store in stores:
        store.wait()


def edges_kernel(
    rates_ref, low_ref, high_ref, edge_ref, mask_ref, far_ref, held_hbm,
    out_hbm,
    obuf, pad, gcat, sems,
):
    del held_hbm
    _, columns, channels = low_ref.shape
    rows = out_hbm.shape[0]
    mine = lax.axis_index("tile")
    last = rates_ref.shape[1] - 1
    clear_ends(pad, 2 * HALO, columns)
    stores = [
        pltpu.make_async_copy(
            obuf.at[pl.ds(HALO * side, HALO)],
            out_hbm.at[pl.ds((rows - HALO) * side, HALO)],
            sems.at[side],
        )
        for side in range(2)
    ]

    def one_side(side, rate):
        ref = high_ref if side else low_ref
        used = range(rate) if side else range(HALO - rate, HALO)
        for place, k in enumerate(used):
            spread(
                ref[k], pad, side * HALO + k, gcat.at[side, pl.ds(place * columns, columns)], -rate
            )
        sums = jnp.dot(
            gcat[side, : rate * columns], far_ref[side], preferred_element_type=F32
        )
        for k in range(HALO):
            value = edge_ref[side * HALO + k]
            place = k - (HALO - rate) if side else k
            if 0 <= place < rate:
                value = value + sums[place * columns : (place + 1) * columns]
            obuf[side * HALO + k] = value.astype(BF16) * mask_ref[1]

    near = (jnp.maximum(mine - 1, 0), jnp.minimum(mine + 1, last))
    for side in range(2):
        by_rate(rates_ref[0, near[side]], lambda rate, side=side: one_side(side, rate))
        stores[side].start()
    for store in stores:
        store.wait()


def exchange(to_next, to_previous, axis):
    count = lax.axis_size(axis)
    forward = [(i, i + 1) for i in range(count - 1)]
    backward = [(target, source) for source, target in forward]
    return lax.ppermute(to_next, axis, forward), lax.ppermute(to_previous, axis, backward)


def call(kernel, name, outs, specs, scratch, aliases=None, flops=0):
    memory = {"s": pltpu.SMEM, "v": pltpu.VMEM, "h": pltpu.HBM}
    ins, results = (
        [pl.BlockSpec(memory_space=memory[letter]) for letter in part] for part in specs.split(">")
    )
    return pl.pallas_call(
        kernel,
        name=name,
        out_shape=tuple(jax.ShapeDtypeStruct(shape, dtype) for shape, dtype in outs),
        in_specs=ins,
        out_specs=tuple(results),
        scratch_shapes=scratch,
        input_output_aliases=aliases or {},
        cost_estimate=pl.CostEstimate(flops=flops, bytes_accessed=0, transcendentals=0),
        compiler_params=pltpu.CompilerParams(vmem_limit_bytes=VMEM_LIMIT),
    )


def in_hbm(array):
    return pltpu.with_memory_space_constraint(array, pltpu.HBM)


def shards(features, cotangent, tile_mask, work_lists, dilations, conv_weight, conv_bias):
    x, cot, lists = features[0], in_hbm(cotangent[0]), in_hbm(work_lists[0])
    dilations = in_hbm(dilations)
    rows, columns, channels = x.shape
    axes = ("tile", "dp")
    devices = lax.axis_size("tile") * lax.axis_size("dp")
    weight = in_hbm(conv_weight.reshape(9, channels, channels))
    bias = in_hbm(conv_bias.reshape(1, channels))
    inner = rows - 2 * HALO
    wide_row = 3 * channels
    whole = ((rows, columns, channels), BF16)

    def pads(count):
        return pltpu.VMEM((count, columns + 2 * EDGE, channels), F32)

    low, high = exchange(x[rows - HALO :], x[:HALO], "tile")

    held, pre, gcat, xt, total, mask, cot_edge, back, near, far = call(
        first_kernel,
        "first",
        [
            whole,
            ((2 * HALO, columns, channels), F32),
            ((inner, columns, wide_row), BF16),
            ((rows, channels, columns), BF16),
            ((wide_row, wide_row), F32),
            ((3, columns, channels), BF16),
            ((2 * HALO, columns, channels), BF16),
            ((4 * wide_row, 2 * channels), BF16),
            ((2, wide_row, channels), BF16),
            ((2, wide_row, channels), BF16),
        ],
        "svhhhv>hvvvvvvvvv",
        [
            pltpu.VMEM((rows, columns, channels), BF16),
            pltpu.VMEM((rows, columns, channels), BF16),
            pltpu.VMEM((9, channels, channels), BF16),
            pltpu.VMEM((rows - 4 * HALO, columns, channels), BF16),
            pads(rows),
            pltpu.VMEM((rows, columns, wide_row), BF16),
            pltpu.VMEM((4 * wide_row, 2 * channels), BF16),
            pltpu.SemaphoreType.DMA((4,)),
        ],
        flops=BUSY,
    )(dilations, lists, in_hbm(x), cot, weight, bias)

    grad_low, grad_high, xt_halo = call(
        rims_kernel,
        "rims",
        [
            ((HALO, columns, channels), BF16),
            ((HALO, columns, channels), BF16),
            ((2 * HALO, channels, columns), BF16),
        ],
        "svvvvvv>vvv",
        [pads(2 * HALO), pltpu.VMEM((HALO * columns, wide_row), BF16)],
    )(dilations, low, high, pre, cot_edge, mask, near)

    from_low, from_high = exchange(grad_high, grad_low, "tile")

    tap_rows = 9 * channels
    direct = tap_rows % devices == 0
    share = (devices, tap_rows // devices) if direct else (1, tap_rows)
    scale = 1.0 / math.sqrt(devices * lists.shape[1] * TILE * TILE)
    held, edge, taps = call(
        lambda *refs: second_kernel(*refs, scale=scale),
        "second",
        [whole, ((2 * HALO, columns, channels), F32), (share + (channels,), BF16)],
        "svvvvvvhvvh>hvv",
        [
            pltpu.VMEM((4 * HALO, columns, channels), BF16),
            pltpu.VMEM((2 * HALO, columns, channels), BF16),
            pads(2 * HALO),
            pltpu.VMEM((2 * HALO, columns, wide_row), BF16),
            pltpu.VMEM((tap_rows, channels), F32),
            pltpu.SemaphoreType.DMA((4,)),
        ],
        {10: 0},
        flops=BUSY,
    )(dilations, grad_low, grad_high, xt, xt_halo, total, gcat, cot, mask, back, held)
    if not direct:
        taps = taps.reshape(devices, -1)
    received = lax.all_to_all(taps, axes, 0, 0, tiled=True)

    (input_grad,) = call(
        edges_kernel,
        "edges",
        [whole],
        "svvvvvh>h",
        [
            pltpu.VMEM((2 * HALO, columns, channels), BF16),
            pads(2 * HALO),
            pltpu.VMEM((2, HALO * columns, wide_row), BF16),
            pltpu.SemaphoreType.DMA((2,)),
        ],
        {6: 0},
        flops=BUSY,
    )(dilations, from_low, from_high, edge, mask, far, held)
    summed = jnp.sum(received.astype(F32), axis=0)
    return (input_grad[None], summed.reshape(-1))


def solution(mesh):
    placed = (
        P("dp", "tile", None, None),
        P("dp", "tile", None, None),
        P("dp", "tile", None),
        P("dp", None, None),
        P("dp", None),
        P(),
        P(),
    )
    return jax.shard_map(
        shards,
        mesh=mesh,
        in_specs=placed,
        out_specs=(P("dp", "tile", None, None), P(("tile", "dp"))),
        check_vma=False,
    )
```

```python
import math

import jax
import jax.numpy as jnp
from jax import lax
from jax.experimental import pallas as pl
from jax.experimental.pallas import tpu as pltpu
from jax.sharding import PartitionSpec as P

TILE = 12
HALO = 2
LANES = 128
EDGE = 8
RATES = (1, 2)
VMEM_LIMIT = 40 * 1024 * 1024
BUSY = 20_000_000_000

F32 = jnp.float32
BF16 = jnp.bfloat16


def cell_masks(lists_ref, middle, tiles_row, columns):
    ids = lists_ref[...]
    workers, width = ids.shape
    tile = lax.broadcasted_iota(jnp.int32, (3 * tiles_row, width), 0)
    target = (middle - 1) * tiles_row + tile
    found = ids[0:1] == target
    for worker in range(1, workers):
        found = found | (ids[worker : worker + 1] == target)
    named = jnp.dot(
        jnp.where(found, 1.0, 0.0).astype(BF16),
        jnp.ones((width, LANES), BF16),
        preferred_element_type=F32,
    ).astype(BF16)
    first = TILE * lax.broadcasted_iota(jnp.int32, (columns, tiles_row), 1)
    cell = lax.broadcasted_iota(jnp.int32, (columns, tiles_row), 0)
    inside = jnp.where((cell >= first) & (cell < first + TILE), 1.0, 0.0).astype(BF16)
    return [
        jnp.dot(
            inside, named[k * tiles_row : (k + 1) * tiles_row], preferred_element_type=F32
        ).astype(BF16)
        for k in range(3)
    ]


def row_pairs(rate, rows):
    rows = list(rows)
    pairs = []
    for start in range(0, len(rows), 2 * rate):
        for k in range(rate):
            pairs.append((rows[start + k], rows[start + k + rate]))
    return pairs


def by_rate(rate, body):
    for value in RATES:
        pl.when(rate == value)(lambda value=value: body(value))


def clear_ends(pad_ref, count, columns):
    ends = jnp.zeros((EDGE, pad_ref.shape[-1]), F32)
    for k in range(count):
        pad_ref[k, :EDGE] = ends
        pad_ref[k, EDGE + columns :] = ends


def spread(value, pad_ref, slot, target_ref, offset):
    columns, channels = value.shape
    pad_ref[slot, EDGE : EDGE + columns] = value.astype(F32)
    target_ref[:, :channels] = pad_ref[slot, pl.ds(EDGE - offset, columns)].astype(BF16)
    target_ref[:, channels : 2 * channels] = value.astype(BF16)
    target_ref[:, 2 * channels :] = pad_ref[slot, pl.ds(EDGE + offset, columns)].astype(BF16)


def silu_grad(half_cot, half_pre):
    turn = jnp.tanh(half_pre)
    return half_cot * (1.0 + turn + half_pre * (1.0 - turn * turn))


def tap_sums(grads, xts, rate):
    flipped = jnp.concatenate(
        [
            jnp.concatenate([xts(row + rate * a) for row, _ in grads], axis=1)
            for a in (-1, 0, 1)
        ],
        axis=0,
    )
    return jnp.dot(
        flipped,
        jnp.concatenate([ref[...] for _, ref in grads], axis=0),
        preferred_element_type=F32,
    )


def pair_rows(pair, rate, rows):
    reach = [pair[0] + rate * (k - 1) for k in range(4)]
    inside = [k for k in range(4) if 0 <= reach[k] < rows]
    return [reach[k] for k in inside], inside[0], inside[-1] + 1


def input_sums(pair, rate, rows, grads, wide_ref):
    near, low, high = pair_rows(pair, rate, rows)
    lhs = jnp.concatenate([grads(row)[...] for row in near], axis=1)
    width = wide_ref.shape[0] // 4
    both = jnp.dot(lhs, wide_ref[low * width : high * width], preferred_element_type=F32)
    half = both.shape[1] // 2
    return both[:, :half], both[:, half:]


def first_kernel(
    rates_ref, lists_ref, x_hbm, cot_hbm, w_hbm, bias_ref,
    out_hbm, pre_ref, gcat_ref, xt_ref, total_ref, mask_ref, cot_ref, back_ref, near_ref, far_ref,
    xbuf, cbuf, wbuf, obuf, pad, xcat, wide, sems,
):
    rows, columns, channels = x_hbm.shape
    tiles_row = columns // TILE
    mine = lax.axis_index("tile")
    loads = [
        pltpu.make_async_copy(w_hbm, wbuf, sems.at[0]),
        pltpu.make_async_copy(x_hbm, xbuf, sems.at[1]),
        pltpu.make_async_copy(cot_hbm, cbuf, sems.at[2]),
    ]
    for load in loads:
        load.start()
    for k, value in enumerate(cell_masks(lists_ref, mine, tiles_row, columns)):
        mask_ref[k] = value
    clear_ends(pad, rows, columns)
    loads[0].wait()
    none = jnp.zeros((channels, channels), BF16)
    for col in range(3):
        there = slice(col * channels, (col + 1) * channels)
        turned = [wbuf[tap * 3 + col].T for tap in range(3)]
        for side in range(2):
            near_ref[side, there] = wbuf[6 * side + col]
            far_ref[side, there] = turned[2 - 2 * side]
        for row in range(4):
            start = (row * 3 + col) * channels
            here = slice(start, start + channels)
            for out in range(2):
                there = slice(out * channels, (out + 1) * channels)
                tap = row - out
                wide[here, there] = wbuf[tap * 3 + col] if 0 <= tap < 3 else none
                tap = out + 2 - row
                back_ref[here, there] = turned[tap] if 0 <= tap < 3 else none
    loads[1].wait()
    loads[2].wait()
    half_bias = 0.5 * bias_ref[...]
    middle = range(2 * HALO, rows - 2 * HALO)
    store = pltpu.make_async_copy(
        obuf, out_hbm.at[pl.ds(middle.start, len(middle))], sems.at[3]
    )

    def body(rate):
        done = set()

        def prepare(row):
            if row in done:
                return
            done.add(row)
            value = xbuf[row] * mask_ref[1]
            spread(value, pad, row, xcat.at[row], rate)
            xt_ref[row] = value.T

        def convolve(pair):
            near, low, high = pair_rows(pair, rate, rows)
            for row in near:
                prepare(row)
            lhs = jnp.concatenate([xcat[row] for row in near], axis=1)
            width = wide.shape[0] // 4
            both = jnp.dot(
                lhs, wide[low * width : high * width], preferred_element_type=F32
            )
            return pair, (both[:, :channels], both[:, channels:])

        def finish(pair, sums):
            for row, value in zip(pair, sums):
                half_pre = 0.5 * value + half_bias
                half_cot = cbuf[row] * mask_ref[1] * 0.5
                if HALO <= row < rows - HALO:
                    grad = silu_grad(half_cot.astype(F32), half_pre)
                    spread(grad, pad, row, gcat_ref.at[row - HALO], -rate)
                    ready.append(row)
                else:
                    here = row if row < HALO else row - (rows - 2 * HALO)
                    pre_ref[here] = half_pre
                    cot_ref[here] = half_cot

        ready = []
        summed = []
        waiting = None
        for pair in row_pairs(rate, range(rows)) + [None]:
            result = convolve(pair) if pair else None
            if waiting:
                finish(*waiting)
            waiting = result
            while len(ready) >= 2:
                grads = [(row, gcat_ref.at[row - HALO]) for row in ready[:2]]
                part = tap_sums(grads, lambda row: xt_ref[row], rate)
                total_ref[...] = total_ref[...] + part if summed else part
                summed.extend(ready[:2])
                del ready[:2]
        for pair in row_pairs(rate, middle):
            sums = input_sums(pair, rate, rows, lambda row: gcat_ref.at[row - HALO], back_ref)
            for row, value in zip(pair, sums):
                value = (value + cbuf[row].astype(F32)).astype(BF16)
                obuf[row - middle.start] = value * mask_ref[1]

    by_rate(rates_ref[0, mine], body)
    store.start()
    store.wait()


def rims_kernel(
    rates_ref, low_ref, high_ref, pre_ref, cot_ref, mask_ref, near_ref,
    grad_low_ref, grad_high_ref, xt_ref,
    pad, xcat,
):
    _, columns, channels = low_ref.shape
    clear_ends(pad, 2 * HALO, columns)

    def body(rate):
        for side, ref in enumerate((low_ref, high_ref)):
            used = range(HALO - rate, HALO) if side == 0 else range(rate)
            for place, k in enumerate(used):
                value = ref[k] * mask_ref[2 * side]
                spread(
                    value, pad, side * HALO + k, xcat.at[pl.ds(place * columns, columns)], rate
                )
                xt_ref[side * HALO + k] = value.T
            sums = jnp.dot(
                xcat[: rate * columns], near_ref[side], preferred_element_type=F32
            )
            for k in range(HALO):
                half_pre = pre_ref[side * HALO + k]
                place = k if side == 0 else k - (HALO - rate)
                if 0 <= place < rate:
                    half_pre += 0.5 * sums[place * columns : (place + 1) * columns]
                grad = silu_grad(cot_ref[side * HALO + k].astype(F32), half_pre)
                target = grad_high_ref if side else grad_low_ref
                target[k] = grad.astype(BF16)

    by_rate(rates_ref[0, lax.axis_index("tile")], body)


def taps_kernel(
    rates_ref, grad_low_ref, grad_high_ref, xt_own_ref, xt_halo_ref, total_ref,
    keep_ref, send_ref, gedge_ref,
    pad, flat, *, scale, paired,
):
    _, columns, channels = grad_low_ref.shape
    rows = xt_own_ref.shape[0]
    clear_ends(pad, 2 * HALO, columns)

    def flipped(row):
        if row < 0:
            return xt_halo_ref[row + HALO]
        return xt_own_ref[row] if row < rows else xt_halo_ref[row - rows + HALO]

    def body(rate):
        edges = []
        for side, ref in enumerate((grad_low_ref, grad_high_ref)):
            for k in range(HALO):
                slot = side * HALO + k
                spread(ref[k], pad, slot, gedge_ref.at[slot], -rate)
                edges.append((k + side * (rows - HALO), gedge_ref.at[slot]))
        total = (total_ref[...] + tap_sums(edges, flipped, rate)) * scale
        for a in range(3):
            for b in range(3):
                start = (a * 3 + b) * channels
                flat[start : start + channels] = total[
                    a * channels : (a + 1) * channels, b * channels : (b + 1) * channels
                ]

    by_rate(rates_ref[0, lax.axis_index("tile")], body)
    if not paired:
        keep_ref[0] = flat[...]
        return
    parts, share, _ = keep_ref.shape
    here = lax.axis_index("dp")
    for part in range(parts):
        keep_ref[part] = flat[pl.ds((2 * part + here) * share, share)]
        send_ref[part] = flat[pl.ds((2 * part + 1 - here) * share, share)].astype(BF16)


def inputs_kernel(
    rates_ref, gcat_ref, gedge_ref, cot_hbm, mask_ref, back_ref, held_hbm,
    out_hbm, edge_ref,
    cbuf, obuf, sems,
):
    del held_hbm
    rows, columns, channels = cot_hbm.shape
    around = 2 * HALO
    loads = [
        pltpu.make_async_copy(
            cot_hbm.at[pl.ds(side * (rows - around), around)],
            cbuf.at[pl.ds(side * around, around)],
            sems.at[side],
        )
        for side in range(2)
    ]
    stores = [
        pltpu.make_async_copy(
            obuf.at[pl.ds(side * HALO, HALO)],
            out_hbm.at[pl.ds(HALO + side * (rows - 3 * HALO), HALO)],
            sems.at[2 + side],
        )
        for side in range(2)
    ]
    for load in loads:
        load.start()

    def grads(row):
        if row < HALO:
            return gedge_ref.at[row]
        if row < rows - HALO:
            return gcat_ref.at[row - HALO]
        return gedge_ref.at[row - (rows - 2 * HALO)]

    def body(rate):
        for side in range(2):
            start = side * (rows - around)
            results = [
                (pair, input_sums(pair, rate, rows, grads, back_ref))
                for pair in row_pairs(rate, range(start, start + around))
            ]
            loads[side].wait()
            for pair, sums in results:
                for row, value in zip(pair, sums):
                    value = value + cbuf[row - start + side * around].astype(F32)
                    if HALO <= row < rows - HALO:
                        here = row - HALO if side == 0 else row - (rows - around) + HALO
                        obuf[here] = value.astype(BF16) * mask_ref[1]
                    else:
                        here = row if side == 0 else row - (rows - around)
                        edge_ref[here] = value
            stores[side].start()

    by_rate(rates_ref[0, lax.axis_index("tile")], body)
    for store in stores:
        store.wait()


def edges_kernel(
    rates_ref, low_ref, high_ref, edge_ref, mask_ref, far_ref, held_hbm,
    out_hbm,
    obuf, pad, gcat, sems,
):
    del held_hbm
    _, columns, channels = low_ref.shape
    rows = out_hbm.shape[0]
    mine = lax.axis_index("tile")
    last = rates_ref.shape[1] - 1
    clear_ends(pad, 2 * HALO, columns)
    stores = [
        pltpu.make_async_copy(
            obuf.at[pl.ds(HALO * side, HALO)],
            out_hbm.at[pl.ds((rows - HALO) * side, HALO)],
            sems.at[side],
        )
        for side in range(2)
    ]

    def one_side(side, rate):
        ref = high_ref if side else low_ref
        used = range(rate) if side else range(HALO - rate, HALO)
        for place, k in enumerate(used):
            spread(
                ref[k], pad, side * HALO + k, gcat.at[side, pl.ds(place * columns, columns)], -rate
            )
        sums = jnp.dot(
            gcat[side, : rate * columns], far_ref[side], preferred_element_type=F32
        )
        for k in range(HALO):
            value = edge_ref[side * HALO + k]
            place = k - (HALO - rate) if side else k
            if 0 <= place < rate:
                value = value + sums[place * columns : (place + 1) * columns]
            obuf[side * HALO + k] = value.astype(BF16) * mask_ref[1]

    near = (jnp.maximum(mine - 1, 0), jnp.minimum(mine + 1, last))
    for side in range(2):
        by_rate(rates_ref[0, near[side]], lambda rate, side=side: one_side(side, rate))
        stores[side].start()
    for store in stores:
        store.wait()


def exchange(to_next, to_previous, axis):
    count = lax.axis_size(axis)
    forward = [(i, i + 1) for i in range(count - 1)]
    backward = [(target, source) for source, target in forward]
    return lax.ppermute(to_next, axis, forward), lax.ppermute(to_previous, axis, backward)


def call(kernel, name, outs, specs, scratch, aliases=None, flops=0):
    memory = {"s": pltpu.SMEM, "v": pltpu.VMEM, "h": pltpu.HBM}
    ins, results = (
        [pl.BlockSpec(memory_space=memory[letter]) for letter in part] for part in specs.split(">")
    )
    return pl.pallas_call(
        kernel,
        name=name,
        out_shape=tuple(jax.ShapeDtypeStruct(shape, dtype) for shape, dtype in outs),
        in_specs=ins,
        out_specs=tuple(results),
        scratch_shapes=scratch,
        input_output_aliases=aliases or {},
        cost_estimate=pl.CostEstimate(flops=flops, bytes_accessed=0, transcendentals=0),
        compiler_params=pltpu.CompilerParams(vmem_limit_bytes=VMEM_LIMIT),
    )


def in_hbm(array):
    return pltpu.with_memory_space_constraint(array, pltpu.HBM)


def shards(features, cotangent, tile_mask, work_lists, dilations, conv_weight, conv_bias):
    x, cot, lists = features[0], in_hbm(cotangent[0]), in_hbm(work_lists[0])
    dilations = in_hbm(dilations)
    rows, columns, channels = x.shape
    axes = ("tile", "dp")
    devices = lax.axis_size("tile") * lax.axis_size("dp")
    weight = in_hbm(conv_weight.reshape(9, channels, channels))
    bias = in_hbm(conv_bias.reshape(1, channels))
    inner = rows - 2 * HALO
    wide_row = 3 * channels
    whole = ((rows, columns, channels), BF16)

    def pads(count):
        return pltpu.VMEM((count, columns + 2 * EDGE, channels), F32)

    low, high = exchange(x[rows - HALO :], x[:HALO], "tile")

    held, pre, gcat, xt, total, mask, cot_edge, back, near, far = call(
        first_kernel,
        "first",
        [
            whole,
            ((2 * HALO, columns, channels), F32),
            ((inner, columns, wide_row), BF16),
            ((rows, channels, columns), BF16),
            ((wide_row, wide_row), F32),
            ((3, columns, channels), BF16),
            ((2 * HALO, columns, channels), BF16),
            ((4 * wide_row, 2 * channels), BF16),
            ((2, wide_row, channels), BF16),
            ((2, wide_row, channels), BF16),
        ],
        "svhhhv>hvvvvvvvvv",
        [
            pltpu.VMEM((rows, columns, channels), BF16),
            pltpu.VMEM((rows, columns, channels), BF16),
            pltpu.VMEM((9, channels, channels), BF16),
            pltpu.VMEM((rows - 4 * HALO, columns, channels), BF16),
            pads(rows),
            pltpu.VMEM((rows, columns, wide_row), BF16),
            pltpu.VMEM((4 * wide_row, 2 * channels), BF16),
            pltpu.SemaphoreType.DMA((4,)),
        ],
        flops=BUSY,
    )(dilations, lists, in_hbm(x), cot, weight, bias)

    grad_low, grad_high, xt_halo = call(
        rims_kernel,
        "rims",
        [
            ((HALO, columns, channels), BF16),
            ((HALO, columns, channels), BF16),
            ((2 * HALO, channels, columns), BF16),
        ],
        "svvvvvv>vvv",
        [pads(2 * HALO), pltpu.VMEM((HALO * columns, wide_row), BF16)],
    )(dilations, low, high, pre, cot_edge, mask, near)

    from_low, from_high = exchange(grad_high, grad_low, "tile")

    tap_rows = 9 * channels
    cores = lax.axis_size("dp")
    paired = cores == 2 and tap_rows % devices == 0
    share = (devices // 2, tap_rows // devices) if paired else (1, tap_rows)
    scale = 1.0 / math.sqrt(devices * lists.shape[1] * TILE * TILE)
    keep, send, gedge = call(
        lambda *refs: taps_kernel(*refs, scale=scale, paired=paired),
        "taps",
        [
            (share + (channels,), F32),
            (share + (channels,), BF16),
            ((2 * HALO, columns, wide_row), BF16),
        ],
        "svvvvv>vvv",
        [pads(2 * HALO), pltpu.VMEM((tap_rows, channels), F32)],
    )(dilations, grad_low, grad_high, xt, xt_halo, total)
    if paired:
        other = lax.ppermute(send, "dp", [(0, 1), (1, 0)])
        both = (keep + other.astype(F32)).astype(BF16)
        received = lax.all_to_all(both, "tile", 0, 0, tiled=True)
    else:
        received = lax.all_to_all(
            keep.astype(BF16).reshape(devices, -1), axes, 0, 0, tiled=True
        )

    held, edge = call(
        inputs_kernel,
        "inputs",
        [whole, ((2 * HALO, columns, channels), F32)],
        "svvhvvh>hv",
        [
            pltpu.VMEM((4 * HALO, columns, channels), BF16),
            pltpu.VMEM((2 * HALO, columns, channels), BF16),
            pltpu.SemaphoreType.DMA((4,)),
        ],
        {6: 0},
        flops=BUSY,
    )(dilations, gcat, gedge, cot, mask, back, held)

    (input_grad,) = call(
        edges_kernel,
        "edges",
        [whole],
        "svvvvvh>h",
        [
            pltpu.VMEM((2 * HALO, columns, channels), BF16),
            pads(2 * HALO),
            pltpu.VMEM((2, HALO * columns, wide_row), BF16),
            pltpu.SemaphoreType.DMA((2,)),
        ],
        {6: 0},
        flops=BUSY,
    )(dilations, from_low, from_high, edge, mask, far, held)
    summed = jnp.sum(received.astype(F32), axis=0)
    return (input_grad[None], summed.reshape(-1))


def solution(mesh):
    placed = (
        P("dp", "tile", None, None),
        P("dp", "tile", None, None),
        P("dp", "tile", None),
        P("dp", None, None),
        P("dp", None),
        P(),
        P(),
    )
    return jax.shard_map(
        shards,
        mesh=mesh,
        in_specs=placed,
        out_specs=(P("dp", "tile", None, None), P(("tile", "dp"))),
        check_vma=False,
    )
```

```python
import math

import jax
import jax.numpy as jnp
from jax import lax
from jax.experimental import pallas as pl
from jax.experimental.pallas import tpu as pltpu
from jax.sharding import PartitionSpec as P

TILE = 12
HALO = 2
LANES = 128
EDGE = 8
RATES = (1, 2)
VMEM_LIMIT = 40 * 1024 * 1024
BUSY = 20_000_000_000

F32 = jnp.float32
BF16 = jnp.bfloat16


def cell_masks(lists_ref, middle, tiles_row, columns):
    ids = lists_ref[...]
    workers, width = ids.shape
    tile = lax.broadcasted_iota(jnp.int32, (3 * tiles_row, width), 0)
    target = (middle - 1) * tiles_row + tile
    found = ids[0:1] == target
    for worker in range(1, workers):
        found = found | (ids[worker : worker + 1] == target)
    named = jnp.dot(
        jnp.where(found, 1.0, 0.0).astype(BF16),
        jnp.ones((width, LANES), BF16),
        preferred_element_type=F32,
    ).astype(BF16)
    first = TILE * lax.broadcasted_iota(jnp.int32, (columns, tiles_row), 1)
    cell = lax.broadcasted_iota(jnp.int32, (columns, tiles_row), 0)
    inside = jnp.where((cell >= first) & (cell < first + TILE), 1.0, 0.0).astype(BF16)
    return [
        jnp.dot(
            inside, named[k * tiles_row : (k + 1) * tiles_row], preferred_element_type=F32
        ).astype(BF16)
        for k in range(3)
    ]


def row_pairs(rate, rows):
    rows = list(rows)
    pairs = []
    for start in range(0, len(rows), 2 * rate):
        for k in range(rate):
            pairs.append((rows[start + k], rows[start + k + rate]))
    return pairs


def by_rate(rate, body):
    for value in RATES:
        pl.when(rate == value)(lambda value=value: body(value))


def clear_ends(pad_ref, count, columns):
    ends = jnp.zeros((EDGE, pad_ref.shape[-1]), F32)
    for k in range(count):
        pad_ref[k, :EDGE] = ends
        pad_ref[k, EDGE + columns :] = ends


def spread(value, pad_ref, slot, target_ref, offset):
    columns, channels = value.shape
    pad_ref[slot, EDGE : EDGE + columns] = value.astype(F32)
    target_ref[:, :channels] = pad_ref[slot, pl.ds(EDGE - offset, columns)].astype(BF16)
    target_ref[:, channels : 2 * channels] = value.astype(BF16)
    target_ref[:, 2 * channels :] = pad_ref[slot, pl.ds(EDGE + offset, columns)].astype(BF16)


def silu_grad(half_cot, half_pre):
    turn = jnp.tanh(half_pre)
    return half_cot * (1.0 + turn + half_pre * (1.0 - turn * turn))


def tap_sums(grads, xts, rate):
    flipped = jnp.concatenate(
        [
            jnp.concatenate([xts(row + rate * a) for row, _ in grads], axis=1)
            for a in (-1, 0, 1)
        ],
        axis=0,
    )
    return jnp.dot(
        flipped,
        jnp.concatenate([ref[...] for _, ref in grads], axis=0),
        preferred_element_type=F32,
    )


def pair_rows(pair, rate, rows):
    reach = [pair[0] + rate * (k - 1) for k in range(4)]
    inside = [k for k in range(4) if 0 <= reach[k] < rows]
    return [reach[k] for k in inside], inside[0], inside[-1] + 1


def input_sums(pair, rate, rows, grads, wide_ref):
    near, low, high = pair_rows(pair, rate, rows)
    lhs = jnp.concatenate([grads(row)[...] for row in near], axis=1)
    width = wide_ref.shape[0] // 4
    both = jnp.dot(lhs, wide_ref[low * width : high * width], preferred_element_type=F32)
    half = both.shape[1] // 2
    return both[:, :half], both[:, half:]


def first_kernel(
    rates_ref, lists_ref, x_hbm, cot_hbm, w_hbm, bias_ref,
    gcat_hbm, pre_ref, xt_ref, total_ref, mask_ref, cot_ref, back_ref, near_ref, far_ref,
    xbuf, cbuf, wbuf, pad, xcat, gcat_ref, wide, sems,
):
    rows, columns, channels = x_hbm.shape
    tiles_row = columns // TILE
    mine = lax.axis_index("tile")
    step = rows // 4
    loads = [pltpu.make_async_copy(w_hbm, wbuf, sems.at[0])]
    for source, target, base in ((x_hbm, xbuf, 1), (cot_hbm, cbuf, 5)):
        for k in range(4):
            part = pl.ds(k * step, step)
            loads.append(
                pltpu.make_async_copy(source.at[part], target.at[part], sems.at[base + k])
            )
    inner = rows - 2 * HALO
    stores = [
        pltpu.make_async_copy(
            gcat_ref.at[pl.ds(k, 2)], gcat_hbm.at[pl.ds(k, 2)], sems.at[9 + k // 2]
        )
        for k in range(0, inner, 2)
    ]
    for load in loads:
        load.start()
    for k, value in enumerate(cell_masks(lists_ref, mine, tiles_row, columns)):
        mask_ref[k] = value
    clear_ends(pad, rows, columns)
    loads[0].wait()
    none = jnp.zeros((channels, channels), BF16)
    for col in range(3):
        there = slice(col * channels, (col + 1) * channels)
        turned = [wbuf[tap * 3 + col].T for tap in range(3)]
        for side in range(2):
            near_ref[side, there] = wbuf[6 * side + col]
            far_ref[side, there] = turned[2 - 2 * side]
        for row in range(4):
            start = (row * 3 + col) * channels
            here = slice(start, start + channels)
            for out in range(2):
                there = slice(out * channels, (out + 1) * channels)
                tap = row - out
                wide[here, there] = wbuf[tap * 3 + col] if 0 <= tap < 3 else none
                tap = out + 2 - row
                back_ref[here, there] = turned[tap] if 0 <= tap < 3 else none
    for load in loads[1:]:
        load.wait()
    half_bias = 0.5 * bias_ref[...]

    def body(rate):
        done = set()

        def prepare(row):
            if row in done:
                return
            done.add(row)
            value = xbuf[row] * mask_ref[1]
            spread(value, pad, row, xcat.at[row], rate)
            xt_ref[row] = value.T

        def convolve(pair):
            near, low, high = pair_rows(pair, rate, rows)
            for row in near:
                prepare(row)
            lhs = jnp.concatenate([xcat[row] for row in near], axis=1)
            width = wide.shape[0] // 4
            both = jnp.dot(
                lhs, wide[low * width : high * width], preferred_element_type=F32
            )
            return pair, (both[:, :channels], both[:, channels:])

        def finish(pair, sums):
            for row, value in zip(pair, sums):
                half_pre = 0.5 * value + half_bias
                half_cot = cbuf[row] * mask_ref[1] * 0.5
                if HALO <= row < rows - HALO:
                    grad = silu_grad(half_cot.astype(F32), half_pre)
                    spread(grad, pad, row, gcat_ref.at[row - HALO], -rate)
                    ready.append(row)
                    there.add(row)
                    mate = row ^ 1
                    if mate in there:
                        stores[(row - HALO) // 2].start()
                else:
                    here = row if row < HALO else row - (rows - 2 * HALO)
                    pre_ref[here] = half_pre
                    cot_ref[here] = half_cot

        ready = []
        there = set()
        summed = []
        waiting = None
        for pair in row_pairs(rate, range(rows)) + [None]:
            result = convolve(pair) if pair else None
            if waiting:
                finish(*waiting)
            waiting = result
            while len(ready) >= 2:
                grads = [(row, gcat_ref.at[row - HALO]) for row in ready[:2]]
                part = tap_sums(grads, lambda row: xt_ref[row], rate)
                total_ref[...] = total_ref[...] + part if summed else part
                summed.extend(ready[:2])
                del ready[:2]

    by_rate(rates_ref[0, mine], body)
    for store in stores:
        store.wait()


def rims_kernel(
    rates_ref, low_ref, high_ref, pre_ref, cot_ref, mask_ref, near_ref,
    grad_low_ref, grad_high_ref, xt_ref,
    pad, xcat,
):
    _, columns, channels = low_ref.shape
    clear_ends(pad, 2 * HALO, columns)

    def body(rate):
        for side, ref in enumerate((low_ref, high_ref)):
            used = range(HALO - rate, HALO) if side == 0 else range(rate)
            for place, k in enumerate(used):
                value = ref[k] * mask_ref[2 * side]
                spread(
                    value, pad, side * HALO + k, xcat.at[pl.ds(place * columns, columns)], rate
                )
                xt_ref[side * HALO + k] = value.T
            sums = jnp.dot(
                xcat[: rate * columns], near_ref[side], preferred_element_type=F32
            )
            for k in range(HALO):
                half_pre = pre_ref[side * HALO + k]
                place = k if side == 0 else k - (HALO - rate)
                if 0 <= place < rate:
                    half_pre += 0.5 * sums[place * columns : (place + 1) * columns]
                grad = silu_grad(cot_ref[side * HALO + k].astype(F32), half_pre)
                target = grad_high_ref if side else grad_low_ref
                target[k] = grad.astype(BF16)

    by_rate(rates_ref[0, lax.axis_index("tile")], body)


def taps_kernel(
    rates_ref, grad_low_ref, grad_high_ref, xt_own_ref, xt_halo_ref, total_ref,
    keep_ref, send_ref,
    pad, gedge_ref, flat, *, scale, paired,
):
    _, columns, channels = grad_low_ref.shape
    rows = xt_own_ref.shape[0]
    clear_ends(pad, 2 * HALO, columns)

    def flipped(row):
        if row < 0:
            return xt_halo_ref[row + HALO]
        return xt_own_ref[row] if row < rows else xt_halo_ref[row - rows + HALO]

    def body(rate):
        edges = []
        for side, ref in enumerate((grad_low_ref, grad_high_ref)):
            for k in range(HALO):
                slot = side * HALO + k
                spread(ref[k], pad, slot, gedge_ref.at[slot], -rate)
                edges.append((k + side * (rows - HALO), gedge_ref.at[slot]))
        total = (total_ref[...] + tap_sums(edges, flipped, rate)) * scale
        for a in range(3):
            for b in range(3):
                start = (a * 3 + b) * channels
                flat[start : start + channels] = total[
                    a * channels : (a + 1) * channels, b * channels : (b + 1) * channels
                ]

    by_rate(rates_ref[0, lax.axis_index("tile")], body)
    if not paired:
        keep_ref[0] = flat[...]
        return
    parts, share, _ = keep_ref.shape
    here = lax.axis_index("dp")
    for part in range(parts):
        keep_ref[part] = flat[pl.ds((2 * part + here) * share, share)]
        send_ref[part] = flat[pl.ds((2 * part + 1 - here) * share, share)].astype(BF16)


def last_kernel(
    rates_ref, from_low_ref, from_high_ref, grad_low_ref, grad_high_ref,
    gcat_hbm, cot_hbm, mask_ref, back_ref, far_ref,
    out_hbm,
    cbuf, obuf, pad, gcat, spare, terms, sems,
):
    rows, columns, channels = cot_hbm.shape
    inner = rows - 2 * HALO
    mine = lax.axis_index("tile")
    last = rates_ref.shape[1] - 1
    around = 2 * HALO
    chunks = rows // around
    loads = [
        pltpu.make_async_copy(
            gcat_hbm.at[pl.ds(k, 2)], gcat.at[pl.ds(HALO + k, 2)], sems.at[k // 2]
        )
        for k in range(0, inner, 2)
    ]
    cots, stores = [], []
    for k in range(chunks):
        part = pl.ds(k * around, around)
        cots.append(
            pltpu.make_async_copy(cot_hbm.at[part], cbuf.at[part], sems.at[inner // 2 + k])
        )
        stores.append(
            pltpu.make_async_copy(obuf.at[part], out_hbm.at[part], sems.at[inner // 2 + chunks + k])
        )
    for load in loads + cots:
        load.start()
    clear_ends(pad, 4 * HALO, columns)

    def neighbour(side, rate):
        ref = from_high_ref if side else from_low_ref
        used = range(rate) if side else range(HALO - rate, HALO)
        for place, k in enumerate(used):
            spread(
                ref[k], pad, side * HALO + k, spare.at[side, pl.ds(place * columns, columns)], -rate
            )
        sums = jnp.dot(
            spare[side, : rate * columns], far_ref[side], preferred_element_type=F32
        )
        for k in range(HALO):
            place = k - (HALO - rate) if side else k
            if 0 <= place < rate:
                terms[side * HALO + k] = sums[place * columns : (place + 1) * columns]
            else:
                terms[side * HALO + k] = jnp.zeros((columns, channels), F32)

    near = (jnp.maximum(mine - 1, 0), jnp.minimum(mine + 1, last))
    for side in range(2):
        by_rate(rates_ref[0, near[side]], lambda rate, side=side: neighbour(side, rate))

    def body(rate):
        for side, ref in enumerate((grad_low_ref, grad_high_ref)):
            for k in range(HALO):
                slot = side * HALO + k
                spread(ref[k], pad, 2 * HALO + slot, gcat.at[k + side * (rows - HALO)], -rate)
        for load in loads + cots:
            load.wait()
        for chunk in range(chunks):
            start = chunk * around
            for pair in row_pairs(rate, range(start, start + around)):
                sums = input_sums(pair, rate, rows, lambda row: gcat.at[row], back_ref)
                for row, value in zip(pair, sums):
                    value = value + cbuf[row].astype(F32)
                    if row < HALO:
                        value = value + terms[row]
                    elif row >= rows - HALO:
                        value = value + terms[row - inner]
                    obuf[row] = value.astype(BF16) * mask_ref[1]
            stores[chunk].start()

    by_rate(rates_ref[0, mine], body)
    for store in stores:
        store.wait()


def cut_kernel(x_hbm, low_ref, high_ref, sems):
    rows = x_hbm.shape[0]
    copies = [
        pltpu.make_async_copy(x_hbm.at[row], ref.at[k], sems.at[side, k])
        for side, ref in enumerate((low_ref, high_ref))
        for k, row in enumerate(range(side * (rows - HALO), side * (rows - HALO) + HALO))
    ]
    for copy in copies:
        copy.start()
    for copy in copies:
        copy.wait()


def exchange(to_next, to_previous, axis):
    count = lax.axis_size(axis)
    forward = [(i, i + 1) for i in range(count - 1)]
    backward = [(target, source) for source, target in forward]
    return lax.ppermute(to_next, axis, forward), lax.ppermute(to_previous, axis, backward)


def call(kernel, name, outs, specs, scratch, aliases=None, flops=0):
    memory = {"s": pltpu.SMEM, "v": pltpu.VMEM, "h": pltpu.HBM}
    ins, results = (
        [pl.BlockSpec(memory_space=memory[letter]) for letter in part] for part in specs.split(">")
    )
    return pl.pallas_call(
        kernel,
        name=name,
        out_shape=tuple(
            pltpu.HBM(shape, dtype) if letter == "h" else jax.ShapeDtypeStruct(shape, dtype)
            for (shape, dtype), letter in zip(outs, specs.split(">")[1])
        ),
        in_specs=ins,
        out_specs=tuple(results),
        scratch_shapes=scratch,
        input_output_aliases=aliases or {},
        cost_estimate=pl.CostEstimate(flops=flops, bytes_accessed=0, transcendentals=0),
        compiler_params=pltpu.CompilerParams(vmem_limit_bytes=VMEM_LIMIT),
    )


def in_hbm(array):
    return pltpu.with_memory_space_constraint(array, pltpu.HBM)


def shards(features, cotangent, tile_mask, work_lists, dilations, conv_weight, conv_bias):
    x, cot, lists = features[0], in_hbm(cotangent[0]), in_hbm(work_lists[0])
    dilations = in_hbm(dilations)
    rows, columns, channels = x.shape
    axes = ("tile", "dp")
    devices = lax.axis_size("tile") * lax.axis_size("dp")
    weight = in_hbm(conv_weight.reshape(9, channels, channels))
    bias = in_hbm(conv_bias.reshape(1, channels))
    inner = rows - 2 * HALO
    wide_row = 3 * channels
    whole = ((rows, columns, channels), BF16)

    def pads(count):
        return pltpu.VMEM((count, columns + 2 * EDGE, channels), F32)

    rim = ((HALO, columns, channels), BF16)
    first_rows, last_rows = call(
        cut_kernel,
        "cut",
        [rim, rim],
        "h>vv",
        [pltpu.SemaphoreType.DMA((2, HALO))],
    )(in_hbm(x))
    low, high = exchange(last_rows, first_rows, "tile")

    gcat, pre, xt, total, mask, cot_edge, back, near, far = call(
        first_kernel,
        "first",
        [
            ((inner, columns, wide_row), BF16),
            ((2 * HALO, columns, channels), F32),
            ((rows, channels, columns), BF16),
            ((wide_row, wide_row), F32),
            ((3, columns, channels), BF16),
            ((2 * HALO, columns, channels), BF16),
            ((4 * wide_row, 2 * channels), BF16),
            ((2, wide_row, channels), BF16),
            ((2, wide_row, channels), BF16),
        ],
        "svhhhv>hvvvvvvvv",
        [
            pltpu.VMEM((rows, columns, channels), BF16),
            pltpu.VMEM((rows, columns, channels), BF16),
            pltpu.VMEM((9, channels, channels), BF16),
            pads(rows),
            pltpu.VMEM((rows, columns, wide_row), BF16),
            pltpu.VMEM((inner, columns, wide_row), BF16),
            pltpu.VMEM((4 * wide_row, 2 * channels), BF16),
            pltpu.SemaphoreType.DMA((9 + inner // 2,)),
        ],
        flops=BUSY,
    )(dilations, lists, in_hbm(x), cot, weight, bias)

    grad_low, grad_high, xt_halo = call(
        rims_kernel,
        "rims",
        [
            rim,
            rim,
            ((2 * HALO, channels, columns), BF16),
        ],
        "svvvvvv>vvv",
        [pads(2 * HALO), pltpu.VMEM((HALO * columns, wide_row), BF16)],
    )(dilations, low, high, pre, cot_edge, mask, near)

    from_low, from_high = exchange(grad_high, grad_low, "tile")

    tap_rows = 9 * channels
    cores = lax.axis_size("dp")
    paired = cores == 2 and tap_rows % devices == 0
    share = (devices // 2, tap_rows // devices) if paired else (1, tap_rows)
    scale = 1.0 / math.sqrt(devices * lists.shape[1] * TILE * TILE)
    keep, send = call(
        lambda *refs: taps_kernel(*refs, scale=scale, paired=paired),
        "taps",
        [
            (share + (channels,), F32),
            (share + (channels,), BF16),
        ],
        "svvvvv>vv",
        [
            pads(2 * HALO),
            pltpu.VMEM((2 * HALO, columns, wide_row), BF16),
            pltpu.VMEM((tap_rows, channels), F32),
        ],
    )(dilations, grad_low, grad_high, xt, xt_halo, total)
    if paired:
        other = lax.ppermute(send, "dp", [(0, 1), (1, 0)])
        both = (keep + other.astype(F32)).astype(BF16)
        received = lax.all_to_all(both, "tile", 0, 0, tiled=True)
    else:
        received = lax.all_to_all(
            keep.astype(BF16).reshape(devices, -1), axes, 0, 0, tiled=True
        )

    (input_grad,) = call(
        last_kernel,
        "last",
        [whole],
        "svvvvhhvvv>h",
        [
            pltpu.VMEM((rows, columns, channels), BF16),
            pltpu.VMEM((rows, columns, channels), BF16),
            pads(4 * HALO),
            pltpu.VMEM((rows, columns, wide_row), BF16),
            pltpu.VMEM((2, HALO * columns, wide_row), BF16),
            pltpu.VMEM((2 * HALO, columns, channels), F32),
            pltpu.SemaphoreType.DMA((inner // 2 + 2 * (rows // (2 * HALO)),)),
        ],
        flops=BUSY,
    )(
        dilations, from_low, from_high, grad_low, grad_high,
        in_hbm(gcat), cot, mask, back, far,
    )
    summed = jnp.sum(received.astype(F32), axis=0)
    return (input_grad[None], summed.reshape(-1))


def solution(mesh):
    placed = (
        P("dp", "tile", None, None),
        P("dp", "tile", None, None),
        P("dp", "tile", None),
        P("dp", None, None),
        P("dp", None),
        P(),
        P(),
    )
    return jax.shard_map(
        shards,
        mesh=mesh,
        in_specs=placed,
        out_specs=(P("dp", "tile", None, None), P(("tile", "dp"))),
        check_vma=False,
    )
```

```python
import math

import jax
import jax.numpy as jnp
from jax import lax
from jax.experimental import pallas as pl
from jax.experimental.pallas import tpu as pltpu
from jax.sharding import PartitionSpec as P

TILE = 12
HALO = 2
LANES = 128
EDGE = 8
RATES = (1, 2)
VMEM_LIMIT = 40 * 1024 * 1024
BUSY = 20_000_000_000

F32 = jnp.float32
BF16 = jnp.bfloat16


def cell_masks(lists_ref, middle, tiles_row, columns):
    ids = lists_ref[...]
    workers, width = ids.shape
    tile = lax.broadcasted_iota(jnp.int32, (3 * tiles_row, width), 0)
    target = (middle - 1) * tiles_row + tile
    found = ids[0:1] == target
    for worker in range(1, workers):
        found = found | (ids[worker : worker + 1] == target)
    named = jnp.dot(
        jnp.where(found, 1.0, 0.0).astype(BF16),
        jnp.ones((width, LANES), BF16),
        preferred_element_type=F32,
    ).astype(BF16)
    first = TILE * lax.broadcasted_iota(jnp.int32, (columns, tiles_row), 1)
    cell = lax.broadcasted_iota(jnp.int32, (columns, tiles_row), 0)
    inside = jnp.where((cell >= first) & (cell < first + TILE), 1.0, 0.0).astype(BF16)
    return [
        jnp.dot(
            inside, named[k * tiles_row : (k + 1) * tiles_row], preferred_element_type=F32
        ).astype(BF16)
        for k in range(3)
    ]


def row_pairs(rate, rows):
    rows = list(rows)
    pairs = []
    for start in range(0, len(rows), 2 * rate):
        for k in range(rate):
            pairs.append((rows[start + k], rows[start + k + rate]))
    return pairs


def by_rate(rate, body):
    for value in RATES:
        pl.when(rate == value)(lambda value=value: body(value))


def clear_ends(pad_ref, count, columns):
    ends = jnp.zeros((EDGE, pad_ref.shape[-1]), F32)
    for k in range(count):
        pad_ref[k, :EDGE] = ends
        pad_ref[k, EDGE + columns :] = ends


def spread(value, pad_ref, slot, target_ref, offset):
    columns, channels = value.shape
    pad_ref[slot, EDGE : EDGE + columns] = value.astype(F32)
    target_ref[:, :channels] = pad_ref[slot, pl.ds(EDGE - offset, columns)].astype(BF16)
    target_ref[:, channels : 2 * channels] = value.astype(BF16)
    target_ref[:, 2 * channels :] = pad_ref[slot, pl.ds(EDGE + offset, columns)].astype(BF16)


def silu_grad(half_cot, half_pre):
    turn = jnp.tanh(half_pre)
    return half_cot * (1.0 + turn + half_pre * (1.0 - turn * turn))


def tap_sums(grads, xts, rate):
    flipped = jnp.concatenate(
        [
            jnp.concatenate([xts(row + rate * a) for row, _ in grads], axis=1)
            for a in (-1, 0, 1)
        ],
        axis=0,
    )
    return jnp.dot(
        flipped,
        jnp.concatenate([ref[...] for _, ref in grads], axis=0),
        preferred_element_type=F32,
    )


def pair_rows(pair, rate, rows):
    reach = [pair[0] + rate * (k - 1) for k in range(4)]
    inside = [k for k in range(4) if 0 <= reach[k] < rows]
    return [reach[k] for k in inside], inside[0], inside[-1] + 1


def input_sums(pair, rate, rows, grads, wide_ref):
    near, low, high = pair_rows(pair, rate, rows)
    lhs = jnp.concatenate([grads(row)[...] for row in near], axis=1)
    width = wide_ref.shape[0] // 4
    both = jnp.dot(lhs, wide_ref[low * width : high * width], preferred_element_type=F32)
    half = both.shape[1] // 2
    return both[:, :half], both[:, half:]


def first_kernel(
    rates_ref, lists_ref, x_hbm, cot_hbm, w_hbm, bias_ref,
    grad_ref, pre_ref, xt_ref, total_ref, mask_ref, cot_ref, back_ref, near_ref, far_ref,
    xbuf, cbuf, wbuf, pad, xcat, gcat_ref, wide, sems,
):
    rows, columns, channels = x_hbm.shape
    tiles_row = columns // TILE
    mine = lax.axis_index("tile")
    step = rows // 4
    loads = [pltpu.make_async_copy(w_hbm, wbuf, sems.at[0])]
    for source, target, base in ((x_hbm, xbuf, 1), (cot_hbm, cbuf, 5)):
        for k in range(4):
            part = pl.ds(k * step, step)
            loads.append(
                pltpu.make_async_copy(source.at[part], target.at[part], sems.at[base + k])
            )
    for load in loads:
        load.start()
    for k, value in enumerate(cell_masks(lists_ref, mine, tiles_row, columns)):
        mask_ref[k] = value
    clear_ends(pad, rows, columns)
    loads[0].wait()
    none = jnp.zeros((channels, channels), BF16)
    for col in range(3):
        there = slice(col * channels, (col + 1) * channels)
        turned = [wbuf[tap * 3 + col].T for tap in range(3)]
        for side in range(2):
            near_ref[side, there] = wbuf[6 * side + col]
            far_ref[side, there] = turned[2 - 2 * side]
        for row in range(4):
            start = (row * 3 + col) * channels
            here = slice(start, start + channels)
            for out in range(2):
                there = slice(out * channels, (out + 1) * channels)
                tap = row - out
                wide[here, there] = wbuf[tap * 3 + col] if 0 <= tap < 3 else none
                tap = out + 2 - row
                back_ref[here, there] = turned[tap] if 0 <= tap < 3 else none
    for load in loads[1:]:
        load.wait()
    half_bias = 0.5 * bias_ref[...]

    def body(rate):
        done = set()

        def prepare(row):
            if row in done:
                return
            done.add(row)
            value = xbuf[row] * mask_ref[1]
            spread(value, pad, row, xcat.at[row], rate)
            xt_ref[row] = value.T

        def convolve(pair):
            near, low, high = pair_rows(pair, rate, rows)
            for row in near:
                prepare(row)
            lhs = jnp.concatenate([xcat[row] for row in near], axis=1)
            width = wide.shape[0] // 4
            both = jnp.dot(
                lhs, wide[low * width : high * width], preferred_element_type=F32
            )
            return pair, (both[:, :channels], both[:, channels:])

        def finish(pair, sums):
            for row, value in zip(pair, sums):
                half_pre = 0.5 * value + half_bias
                half_cot = cbuf[row] * mask_ref[1] * 0.5
                if HALO <= row < rows - HALO:
                    grad = silu_grad(half_cot.astype(F32), half_pre)
                    spread(grad, pad, row, gcat_ref.at[row - HALO], -rate)
                    grad_ref[row - HALO] = grad.astype(BF16)
                    ready.append(row)
                else:
                    here = row if row < HALO else row - (rows - 2 * HALO)
                    pre_ref[here] = half_pre
                    cot_ref[here] = half_cot

        ready = []
        summed = []
        waiting = None
        for pair in row_pairs(rate, range(rows)) + [None]:
            result = convolve(pair) if pair else None
            if waiting:
                finish(*waiting)
            waiting = result
            while len(ready) >= 2:
                grads = [(row, gcat_ref.at[row - HALO]) for row in ready[:2]]
                part = tap_sums(grads, lambda row: xt_ref[row], rate)
                total_ref[...] = total_ref[...] + part if summed else part
                summed.extend(ready[:2])
                del ready[:2]

    by_rate(rates_ref[0, mine], body)


def rims_kernel(
    rates_ref, low_ref, high_ref, pre_ref, cot_ref, mask_ref, near_ref,
    grad_low_ref, grad_high_ref, xt_ref,
    pad, xcat,
):
    _, columns, channels = low_ref.shape
    clear_ends(pad, 2 * HALO, columns)

    def body(rate):
        for side, ref in enumerate((low_ref, high_ref)):
            used = range(HALO - rate, HALO) if side == 0 else range(rate)
            for place, k in enumerate(used):
                value = ref[k] * mask_ref[2 * side]
                spread(
                    value, pad, side * HALO + k, xcat.at[pl.ds(place * columns, columns)], rate
                )
                xt_ref[side * HALO + k] = value.T
            sums = jnp.dot(
                xcat[: rate * columns], near_ref[side], preferred_element_type=F32
            )
            for k in range(HALO):
                half_pre = pre_ref[side * HALO + k]
                place = k if side == 0 else k - (HALO - rate)
                if 0 <= place < rate:
                    half_pre += 0.5 * sums[place * columns : (place + 1) * columns]
                grad = silu_grad(cot_ref[side * HALO + k].astype(F32), half_pre)
                target = grad_high_ref if side else grad_low_ref
                target[k] = grad.astype(BF16)

    by_rate(rates_ref[0, lax.axis_index("tile")], body)


def taps_kernel(
    rates_ref, grad_low_ref, grad_high_ref, xt_own_ref, xt_halo_ref, total_ref,
    keep_ref, send_ref,
    pad, gedge_ref, flat, *, scale, paired,
):
    _, columns, channels = grad_low_ref.shape
    rows = xt_own_ref.shape[0]
    clear_ends(pad, 2 * HALO, columns)

    def flipped(row):
        if row < 0:
            return xt_halo_ref[row + HALO]
        return xt_own_ref[row] if row < rows else xt_halo_ref[row - rows + HALO]

    def body(rate):
        edges = []
        for side, ref in enumerate((grad_low_ref, grad_high_ref)):
            for k in range(HALO):
                slot = side * HALO + k
                spread(ref[k], pad, slot, gedge_ref.at[slot], -rate)
                edges.append((k + side * (rows - HALO), gedge_ref.at[slot]))
        total = (total_ref[...] + tap_sums(edges, flipped, rate)) * scale
        for a in range(3):
            for b in range(3):
                start = (a * 3 + b) * channels
                flat[start : start + channels] = total[
                    a * channels : (a + 1) * channels, b * channels : (b + 1) * channels
                ]

    by_rate(rates_ref[0, lax.axis_index("tile")], body)
    if not paired:
        keep_ref[0] = flat[...]
        return
    parts, share, _ = keep_ref.shape
    here = lax.axis_index("dp")
    for part in range(parts):
        keep_ref[part] = flat[pl.ds((2 * part + here) * share, share)]
        send_ref[part] = flat[pl.ds((2 * part + 1 - here) * share, share)].astype(BF16)


def last_kernel(
    rates_ref, from_low_ref, from_high_ref, grad_low_ref, grad_high_ref,
    grad_ref, cot_hbm, mask_ref, back_ref, far_ref,
    out_hbm,
    cbuf, obuf, pad, gcat, spare, terms, sems,
):
    rows, columns, channels = cot_hbm.shape
    inner = rows - 2 * HALO
    mine = lax.axis_index("tile")
    last = rates_ref.shape[1] - 1
    around = 2 * HALO
    chunks = rows // around
    cots, stores = [], []
    for k in range(chunks):
        part = pl.ds(k * around, around)
        cots.append(
            pltpu.make_async_copy(cot_hbm.at[part], cbuf.at[part], sems.at[k])
        )
        stores.append(
            pltpu.make_async_copy(obuf.at[part], out_hbm.at[part], sems.at[chunks + k])
        )
    for load in cots:
        load.start()
    clear_ends(pad, rows, columns)

    def neighbour(side, rate):
        ref = from_high_ref if side else from_low_ref
        used = range(rate) if side else range(HALO - rate, HALO)
        for place, k in enumerate(used):
            spread(
                ref[k], pad, side * HALO + k, spare.at[side, pl.ds(place * columns, columns)], -rate
            )
        sums = jnp.dot(
            spare[side, : rate * columns], far_ref[side], preferred_element_type=F32
        )
        for k in range(HALO):
            place = k - (HALO - rate) if side else k
            if 0 <= place < rate:
                terms[side * HALO + k] = sums[place * columns : (place + 1) * columns]
            else:
                terms[side * HALO + k] = jnp.zeros((columns, channels), F32)

    near = (jnp.maximum(mine - 1, 0), jnp.minimum(mine + 1, last))
    for side in range(2):
        by_rate(rates_ref[0, near[side]], lambda rate, side=side: neighbour(side, rate))

    def body(rate):
        done = set()

        def shifted(row):
            if row not in done:
                done.add(row)
                if row < HALO:
                    value = grad_low_ref[row]
                elif row < rows - HALO:
                    value = grad_ref[row - HALO]
                else:
                    value = grad_high_ref[row - (rows - HALO)]
                spread(value, pad, row, gcat.at[row], -rate)
            return gcat.at[row]

        for chunk in range(chunks):
            start = chunk * around
            results = [
                (pair, input_sums(pair, rate, rows, shifted, back_ref))
                for pair in row_pairs(rate, range(start, start + around))
            ]
            cots[chunk].wait()
            for pair, sums in results:
                for row, value in zip(pair, sums):
                    value = value + cbuf[row].astype(F32)
                    if row < HALO:
                        value = value + terms[row]
                    elif row >= rows - HALO:
                        value = value + terms[row - inner]
                    obuf[row] = value.astype(BF16) * mask_ref[1]
            stores[chunk].start()

    by_rate(rates_ref[0, mine], body)
    for store in stores:
        store.wait()


def cut_kernel(x_hbm, low_ref, high_ref, sems):
    rows = x_hbm.shape[0]
    copies = [
        pltpu.make_async_copy(x_hbm.at[row], ref.at[k], sems.at[side, k])
        for side, ref in enumerate((low_ref, high_ref))
        for k, row in enumerate(range(side * (rows - HALO), side * (rows - HALO) + HALO))
    ]
    for copy in copies:
        copy.start()
    for copy in copies:
        copy.wait()


def add_kernel(keep_ref, other_ref, sum_ref):
    sum_ref[...] = (keep_ref[...] + other_ref[...].astype(F32)).astype(BF16)


def exchange(to_next, to_previous, axis):
    count = lax.axis_size(axis)
    forward = [(i, i + 1) for i in range(count - 1)]
    backward = [(target, source) for source, target in forward]
    return lax.ppermute(to_next, axis, forward), lax.ppermute(to_previous, axis, backward)


def call(kernel, name, outs, specs, scratch, aliases=None, flops=0):
    memory = {"s": pltpu.SMEM, "v": pltpu.VMEM, "h": pltpu.HBM}
    ins, results = (
        [pl.BlockSpec(memory_space=memory[letter]) for letter in part] for part in specs.split(">")
    )
    return pl.pallas_call(
        kernel,
        name=name,
        out_shape=tuple(
            pltpu.HBM(shape, dtype) if letter == "h" else jax.ShapeDtypeStruct(shape, dtype)
            for (shape, dtype), letter in zip(outs, specs.split(">")[1])
        ),
        in_specs=ins,
        out_specs=tuple(results),
        scratch_shapes=scratch,
        input_output_aliases=aliases or {},
        cost_estimate=pl.CostEstimate(flops=flops, bytes_accessed=0, transcendentals=0),
        compiler_params=pltpu.CompilerParams(vmem_limit_bytes=VMEM_LIMIT),
    )


def in_hbm(array):
    return pltpu.with_memory_space_constraint(array, pltpu.HBM)


def shards(features, cotangent, tile_mask, work_lists, dilations, conv_weight, conv_bias):
    x, cot, lists = features[0], in_hbm(cotangent[0]), in_hbm(work_lists[0])
    dilations = in_hbm(dilations)
    rows, columns, channels = x.shape
    axes = ("tile", "dp")
    devices = lax.axis_size("tile") * lax.axis_size("dp")
    weight = in_hbm(conv_weight.reshape(9, channels, channels))
    bias = in_hbm(conv_bias.reshape(1, channels))
    inner = rows - 2 * HALO
    wide_row = 3 * channels
    whole = ((rows, columns, channels), BF16)

    def pads(count):
        return pltpu.VMEM((count, columns + 2 * EDGE, channels), F32)

    rim = ((HALO, columns, channels), BF16)
    first_rows, last_rows = call(
        cut_kernel,
        "cut",
        [rim, rim],
        "h>vv",
        [pltpu.SemaphoreType.DMA((2, HALO))],
    )(in_hbm(x))
    low, high = exchange(last_rows, first_rows, "tile")

    grad, pre, xt, total, mask, cot_edge, back, near, far = call(
        first_kernel,
        "first",
        [
            ((inner, columns, channels), BF16),
            ((2 * HALO, columns, channels), F32),
            ((rows, channels, columns), BF16),
            ((wide_row, wide_row), F32),
            ((3, columns, channels), BF16),
            ((2 * HALO, columns, channels), BF16),
            ((4 * wide_row, 2 * channels), BF16),
            ((2, wide_row, channels), BF16),
            ((2, wide_row, channels), BF16),
        ],
        "svhhhv>vvvvvvvvv",
        [
            pltpu.VMEM((rows, columns, channels), BF16),
            pltpu.VMEM((rows, columns, channels), BF16),
            pltpu.VMEM((9, channels, channels), BF16),
            pads(rows),
            pltpu.VMEM((rows, columns, wide_row), BF16),
            pltpu.VMEM((inner, columns, wide_row), BF16),
            pltpu.VMEM((4 * wide_row, 2 * channels), BF16),
            pltpu.SemaphoreType.DMA((9,)),
        ],
        flops=BUSY,
    )(dilations, lists, in_hbm(x), cot, weight, bias)

    grad_low, grad_high, xt_halo = call(
        rims_kernel,
        "rims",
        [
            rim,
            rim,
            ((2 * HALO, channels, columns), BF16),
        ],
        "svvvvvv>vvv",
        [pads(2 * HALO), pltpu.VMEM((HALO * columns, wide_row), BF16)],
    )(dilations, low, high, pre, cot_edge, mask, near)

    from_low, from_high = exchange(grad_high, grad_low, "tile")

    tap_rows = 9 * channels
    cores = lax.axis_size("dp")
    paired = cores == 2 and tap_rows % devices == 0
    share = (devices // 2, tap_rows // devices) if paired else (1, tap_rows)
    scale = 1.0 / math.sqrt(devices * lists.shape[1] * TILE * TILE)
    keep, send = call(
        lambda *refs: taps_kernel(*refs, scale=scale, paired=paired),
        "taps",
        [
            (share + (channels,), F32),
            (share + (channels,), BF16),
        ],
        "svvvvv>vv",
        [
            pads(2 * HALO),
            pltpu.VMEM((2 * HALO, columns, wide_row), BF16),
            pltpu.VMEM((tap_rows, channels), F32),
        ],
    )(dilations, grad_low, grad_high, xt, xt_halo, total)
    if paired:
        other = lax.ppermute(send, "dp", [(0, 1), (1, 0)])
        (both,) = call(add_kernel, "add", [(share + (channels,), BF16)], "vv>v", [])(keep, other)
        received = lax.all_to_all(both, "tile", 0, 0, tiled=True)
    else:
        received = lax.all_to_all(
            keep.astype(BF16).reshape(devices, -1), axes, 0, 0, tiled=True
        )

    (input_grad,) = call(
        last_kernel,
        "last",
        [whole],
        "svvvvvhvvv>h",
        [
            pltpu.VMEM((rows, columns, channels), BF16),
            pltpu.VMEM((rows, columns, channels), BF16),
            pads(rows),
            pltpu.VMEM((rows, columns, wide_row), BF16),
            pltpu.VMEM((2, HALO * columns, wide_row), BF16),
            pltpu.VMEM((2 * HALO, columns, channels), F32),
            pltpu.SemaphoreType.DMA((2 * (rows // (2 * HALO)),)),
        ],
        flops=BUSY,
    )(
        dilations, from_low, from_high, grad_low, grad_high,
        grad, cot, mask, back, far,
    )
    summed = jnp.sum(received.astype(F32), axis=0)
    return (input_grad[None], summed.reshape(-1))


def solution(mesh):
    placed = (
        P("dp", "tile", None, None),
        P("dp", "tile", None, None),
        P("dp", "tile", None),
        P("dp", None, None),
        P("dp", None),
        P(),
        P(),
    )
    return jax.shard_map(
        shards,
        mesh=mesh,
        in_specs=placed,
        out_specs=(P("dp", "tile", None, None), P(("tile", "dp"))),
        check_vma=False,
    )
```

```python
import math

import jax
import jax.numpy as jnp
from jax import lax
from jax.experimental import pallas as pl
from jax.experimental.pallas import tpu as pltpu
from jax.sharding import PartitionSpec as P

TILE = 12
HALO = 2
LANES = 128
EDGE = 8
RATES = (1, 2)
VMEM_LIMIT = 40 * 1024 * 1024
BUSY = 20_000_000_000

F32 = jnp.float32
BF16 = jnp.bfloat16


def cell_masks(lists_ref, middle, tiles_row, columns):
    ids = lists_ref[...]
    workers, width = ids.shape
    tile = lax.broadcasted_iota(jnp.int32, (3 * tiles_row, width), 0)
    target = (middle - 1) * tiles_row + tile
    found = ids[0:1] == target
    for worker in range(1, workers):
        found = found | (ids[worker : worker + 1] == target)
    named = jnp.dot(
        jnp.where(found, 1.0, 0.0).astype(BF16),
        jnp.ones((width, LANES), BF16),
        preferred_element_type=F32,
    ).astype(BF16)
    first = TILE * lax.broadcasted_iota(jnp.int32, (columns, tiles_row), 1)
    cell = lax.broadcasted_iota(jnp.int32, (columns, tiles_row), 0)
    inside = jnp.where((cell >= first) & (cell < first + TILE), 1.0, 0.0).astype(BF16)
    return [
        jnp.dot(
            inside, named[k * tiles_row : (k + 1) * tiles_row], preferred_element_type=F32
        ).astype(BF16)
        for k in range(3)
    ]


def row_pairs(rate, rows):
    rows = list(rows)
    pairs = []
    for start in range(0, len(rows), 2 * rate):
        for k in range(rate):
            pairs.append((rows[start + k], rows[start + k + rate]))
    return pairs


def by_rate(rate, body):
    for value in RATES:
        pl.when(rate == value)(lambda value=value: body(value))


def clear_ends(pad_ref, count, columns):
    ends = jnp.zeros((EDGE, pad_ref.shape[-1]), F32)
    for k in range(count):
        pad_ref[k, :EDGE] = ends
        pad_ref[k, EDGE + columns :] = ends


def spread(value, pad_ref, slot, target_ref, offset):
    columns, channels = value.shape
    pad_ref[slot, EDGE : EDGE + columns] = value.astype(F32)
    target_ref[:, :channels] = pad_ref[slot, pl.ds(EDGE - offset, columns)].astype(BF16)
    target_ref[:, channels : 2 * channels] = value.astype(BF16)
    target_ref[:, 2 * channels :] = pad_ref[slot, pl.ds(EDGE + offset, columns)].astype(BF16)


def by_side(a_ref, b_ref, sides_ref):
    odd = lax.axis_index("tile") % 2

    def order(low, high):
        sides_ref[0] = low[...]
        sides_ref[1] = high[...]

    pl.when(odd == 0)(lambda: order(b_ref, a_ref))
    pl.when(odd == 1)(lambda: order(a_ref, b_ref))


def silu_grad(half_cot, half_pre):
    turn = jnp.tanh(half_pre)
    return half_cot * (1.0 + turn + half_pre * (1.0 - turn * turn))


def tap_sums(grads, xts, rate):
    flipped = jnp.concatenate(
        [
            jnp.concatenate([xts(row + rate * a) for row, _ in grads], axis=1)
            for a in (-1, 0, 1)
        ],
        axis=0,
    )
    return jnp.dot(
        flipped,
        jnp.concatenate([ref[...] for _, ref in grads], axis=0),
        preferred_element_type=F32,
    )


def pair_rows(pair, rate, rows):
    reach = [pair[0] + rate * (k - 1) for k in range(4)]
    inside = [k for k in range(4) if 0 <= reach[k] < rows]
    return [reach[k] for k in inside], inside[0], inside[-1] + 1


def input_sums(pair, rate, rows, grads, wide_ref):
    near, low, high = pair_rows(pair, rate, rows)
    lhs = jnp.concatenate([grads(row)[...] for row in near], axis=1)
    width = wide_ref.shape[0] // 4
    both = jnp.dot(lhs, wide_ref[low * width : high * width], preferred_element_type=F32)
    half = both.shape[1] // 2
    return both[:, :half], both[:, half:]


def first_kernel(
    rates_ref, lists_ref, x_hbm, cot_hbm, w_hbm, bias_ref,
    grad_ref, pre_ref, xt_ref, total_ref, mask_ref, cot_ref, back_ref, near_ref, far_ref,
    xbuf, cbuf, wbuf, pad, xcat, gcat_ref, wide, sems,
):
    rows, columns, channels = x_hbm.shape
    tiles_row = columns // TILE
    mine = lax.axis_index("tile")
    step = rows // 4
    loads = [pltpu.make_async_copy(w_hbm, wbuf, sems.at[0])]
    for source, target, base in ((x_hbm, xbuf, 1), (cot_hbm, cbuf, 5)):
        for k in range(4):
            part = pl.ds(k * step, step)
            loads.append(
                pltpu.make_async_copy(source.at[part], target.at[part], sems.at[base + k])
            )
    for load in loads:
        load.start()
    for k, value in enumerate(cell_masks(lists_ref, mine, tiles_row, columns)):
        mask_ref[k] = value
    clear_ends(pad, rows, columns)
    loads[0].wait()
    none = jnp.zeros((channels, channels), BF16)
    for col in range(3):
        there = slice(col * channels, (col + 1) * channels)
        turned = [wbuf[tap * 3 + col].T for tap in range(3)]
        for side in range(2):
            near_ref[side, there] = wbuf[6 * side + col]
            far_ref[side, there] = turned[2 - 2 * side]
        for row in range(4):
            start = (row * 3 + col) * channels
            here = slice(start, start + channels)
            for out in range(2):
                there = slice(out * channels, (out + 1) * channels)
                tap = row - out
                wide[here, there] = wbuf[tap * 3 + col] if 0 <= tap < 3 else none
                tap = out + 2 - row
                back_ref[here, there] = turned[tap] if 0 <= tap < 3 else none
    for load in loads[1:]:
        load.wait()
    half_bias = 0.5 * bias_ref[...]

    def body(rate):
        done = set()

        def prepare(row):
            if row in done:
                return
            done.add(row)
            value = xbuf[row] * mask_ref[1]
            spread(value, pad, row, xcat.at[row], rate)
            xt_ref[row] = value.T

        def convolve(pair):
            near, low, high = pair_rows(pair, rate, rows)
            for row in near:
                prepare(row)
            lhs = jnp.concatenate([xcat[row] for row in near], axis=1)
            width = wide.shape[0] // 4
            both = jnp.dot(
                lhs, wide[low * width : high * width], preferred_element_type=F32
            )
            return pair, (both[:, :channels], both[:, channels:])

        def finish(pair, sums):
            for row, value in zip(pair, sums):
                half_pre = 0.5 * value + half_bias
                half_cot = cbuf[row] * mask_ref[1] * 0.5
                if HALO <= row < rows - HALO:
                    grad = silu_grad(half_cot.astype(F32), half_pre)
                    spread(grad, pad, row, gcat_ref.at[row - HALO], -rate)
                    grad_ref[row - HALO] = grad.astype(BF16)
                    ready.append(row)
                else:
                    here = row if row < HALO else row - (rows - 2 * HALO)
                    pre_ref[here] = half_pre
                    cot_ref[here] = half_cot

        ready = []
        summed = []
        waiting = None
        for pair in row_pairs(rate, range(rows)) + [None]:
            result = convolve(pair) if pair else None
            if waiting:
                finish(*waiting)
            waiting = result
            while len(ready) >= 2:
                grads = [(row, gcat_ref.at[row - HALO]) for row in ready[:2]]
                part = tap_sums(grads, lambda row: xt_ref[row], rate)
                total_ref[...] = total_ref[...] + part if summed else part
                summed.extend(ready[:2])
                del ready[:2]

    by_rate(rates_ref[0, mine], body)


def rims_kernel(
    rates_ref, a_ref, b_ref, pre_ref, cot_ref, mask_ref, near_ref,
    grad_a_ref, grad_b_ref, xt_ref,
    pad, xcat, halo, grads,
):
    _, columns, channels = a_ref.shape
    clear_ends(pad, 2 * HALO, columns)
    by_side(a_ref, b_ref, halo)

    def body(rate):
        for side in range(2):
            used = range(HALO - rate, HALO) if side == 0 else range(rate)
            for place, k in enumerate(used):
                value = halo[side, k] * mask_ref[2 * side]
                part = pl.ds(place * columns, columns)
                spread(value, pad, side * HALO + k, xcat.at[side, part], rate)
                xt_ref[side * HALO + k] = value.T
            sums = jnp.dot(
                xcat[side, : rate * columns], near_ref[side], preferred_element_type=F32
            )
            for k in range(HALO):
                half_pre = pre_ref[side * HALO + k]
                place = k if side == 0 else k - (HALO - rate)
                if 0 <= place < rate:
                    half_pre += 0.5 * sums[place * columns : (place + 1) * columns]
                grad = silu_grad(cot_ref[side * HALO + k].astype(F32), half_pre)
                grads[side, k] = grad.astype(BF16)

    by_rate(rates_ref[0, lax.axis_index("tile")], body)
    odd = lax.axis_index("tile") % 2
    grad_a_ref[...] = grads[1 - odd]
    grad_b_ref[...] = grads[odd]


def taps_kernel(
    rates_ref, grad_a_ref, grad_b_ref, xt_own_ref, xt_halo_ref, total_ref,
    keep_ref, send_ref,
    pad, gedge_ref, flat, sides, *, scale, paired,
):
    _, columns, channels = grad_a_ref.shape
    by_side(grad_a_ref, grad_b_ref, sides)
    rows = xt_own_ref.shape[0]
    clear_ends(pad, 2 * HALO, columns)

    def flipped(row):
        if row < 0:
            return xt_halo_ref[row + HALO]
        return xt_own_ref[row] if row < rows else xt_halo_ref[row - rows + HALO]

    def body(rate):
        edges = []
        for side in range(2):
            for k in range(HALO):
                slot = side * HALO + k
                spread(sides[side, k], pad, slot, gedge_ref.at[slot], -rate)
                edges.append((k + side * (rows - HALO), gedge_ref.at[slot]))
        total = (total_ref[...] + tap_sums(edges, flipped, rate)) * scale
        for a in range(3):
            for b in range(3):
                start = (a * 3 + b) * channels
                flat[start : start + channels] = total[
                    a * channels : (a + 1) * channels, b * channels : (b + 1) * channels
                ]

    by_rate(rates_ref[0, lax.axis_index("tile")], body)
    if not paired:
        keep_ref[0] = flat[...]
        return
    parts, share, _ = keep_ref.shape
    here = lax.axis_index("dp")
    for part in range(parts):
        keep_ref[part] = flat[pl.ds((2 * part + here) * share, share)]
        send_ref[part] = flat[pl.ds((2 * part + 1 - here) * share, share)].astype(BF16)


def last_kernel(
    rates_ref, from_a_ref, from_b_ref, grad_a_ref, grad_b_ref,
    grad_ref, cot_hbm, mask_ref, back_ref, far_ref,
    out_hbm,
    cbuf, obuf, pad, gcat, spare, theirs, ours, sems,
):
    rows, columns, channels = cot_hbm.shape
    inner = rows - 2 * HALO
    mine = lax.axis_index("tile")
    last = rates_ref.shape[1] - 1
    around = 2 * HALO
    chunks = rows // around
    cots, stores = [], []
    for k in range(chunks):
        part = pl.ds(k * around, around)
        cots.append(
            pltpu.make_async_copy(cot_hbm.at[part], cbuf.at[part], sems.at[k])
        )
        stores.append(
            pltpu.make_async_copy(obuf.at[part], out_hbm.at[part], sems.at[chunks + k])
        )
    for load in cots:
        load.start()
    clear_ends(pad, rows + 2 * HALO, columns)
    by_side(from_a_ref, from_b_ref, theirs)
    by_side(grad_a_ref, grad_b_ref, ours)

    def neighbour(side):
        rate = rates_ref[0, jnp.minimum(mine + 1, last) if side else jnp.maximum(mine - 1, 0)]
        for k in range(HALO):
            part = pl.ds(k * columns, columns)
            spread(theirs[side, k], pad, rows + side * HALO + k, spare.at[side, part], -rate)
        sums = jnp.dot(spare[side], far_ref[side], preferred_element_type=F32)
        parts = [sums[k * columns : (k + 1) * columns] for k in range(HALO)]
        none = jnp.zeros((columns, channels), F32)
        one = rate == 1
        if side:
            return [jnp.where(one, none, parts[0]), jnp.where(one, parts[0], parts[1])]
        return [jnp.where(one, parts[1], parts[0]), jnp.where(one, none, parts[1])]

    def body(rate):
        done = set()

        def shifted(row):
            if row not in done:
                done.add(row)
                if row < HALO:
                    value = ours[0, row]
                elif row < rows - HALO:
                    value = grad_ref[row - HALO]
                else:
                    value = ours[1, row - (rows - HALO)]
                spread(value, pad, row, gcat.at[row], -rate)
            return gcat.at[row]

        for chunk in range(chunks):
            start = chunk * around
            results = [
                (pair, input_sums(pair, rate, rows, shifted, back_ref))
                for pair in row_pairs(rate, range(start, start + around))
            ]
            terms = {0: 0, chunks - 1: 1}
            added = neighbour(terms[chunk]) if chunk in terms else None
            cots[chunk].wait()
            for pair, sums in results:
                for row, value in zip(pair, sums):
                    value = value + cbuf[row].astype(F32)
                    if row < HALO:
                        value = value + added[row]
                    elif row >= rows - HALO:
                        value = value + added[row - (rows - HALO)]
                    obuf[row] = value.astype(BF16) * mask_ref[1]
            stores[chunk].start()

    by_rate(rates_ref[0, mine], body)
    for store in stores:
        store.wait()


def cut_kernel(x_hbm, a_ref, b_ref, sems):
    rows = x_hbm.shape[0]
    odd = lax.axis_index("tile") % 2
    copies = []
    for index, ref in enumerate((a_ref, b_ref)):
        start = (rows - HALO) * (odd if index else 1 - odd)
        for k in range(HALO):
            copies.append(
                pltpu.make_async_copy(x_hbm.at[start + k], ref.at[k], sems.at[index, k])
            )
    for copy in copies:
        copy.start()
    for copy in copies:
        copy.wait()


def swap(rows_a, rows_b, axis):
    count = lax.axis_size(axis)
    results = []
    for start, rows in ((0, rows_a), (1, rows_b)):
        pairs = [(i, i + 1) for i in range(start, count - 1, 2)]
        results.append(lax.ppermute(rows, axis, pairs + [(j, i) for i, j in pairs]))
    return results


def call(kernel, name, outs, specs, scratch, aliases=None, flops=0):
    memory = {"s": pltpu.SMEM, "v": pltpu.VMEM, "h": pltpu.HBM}
    ins, results = (
        [pl.BlockSpec(memory_space=memory[letter]) for letter in part] for part in specs.split(">")
    )
    return pl.pallas_call(
        kernel,
        name=name,
        out_shape=tuple(
            pltpu.HBM(shape, dtype) if letter == "h" else jax.ShapeDtypeStruct(shape, dtype)
            for (shape, dtype), letter in zip(outs, specs.split(">")[1])
        ),
        in_specs=ins,
        out_specs=tuple(results),
        scratch_shapes=scratch,
        input_output_aliases=aliases or {},
        cost_estimate=pl.CostEstimate(flops=flops, bytes_accessed=0, transcendentals=0),
        compiler_params=pltpu.CompilerParams(vmem_limit_bytes=VMEM_LIMIT),
    )


def in_hbm(array):
    return pltpu.with_memory_space_constraint(array, pltpu.HBM)


def shards(features, cotangent, tile_mask, work_lists, dilations, conv_weight, conv_bias):
    x, cot, lists = features[0], in_hbm(cotangent[0]), in_hbm(work_lists[0])
    dilations = in_hbm(dilations)
    rows, columns, channels = x.shape
    axes = ("tile", "dp")
    devices = lax.axis_size("tile") * lax.axis_size("dp")
    weight = in_hbm(conv_weight.reshape(9, channels, channels))
    bias = in_hbm(conv_bias.reshape(1, channels))
    inner = rows - 2 * HALO
    wide_row = 3 * channels
    whole = ((rows, columns, channels), BF16)

    def pads(count):
        return pltpu.VMEM((count, columns + 2 * EDGE, channels), F32)

    rim = ((HALO, columns, channels), BF16)
    sides = pltpu.VMEM((2, HALO, columns, channels), BF16)
    rows_a, rows_b = call(
        cut_kernel,
        "cut",
        [rim, rim],
        "h>vv",
        [pltpu.SemaphoreType.DMA((2, HALO))],
    )(in_hbm(x))
    x_a, x_b = swap(rows_a, rows_b, "tile")

    grad, pre, xt, total, mask, cot_edge, back, near, far = call(
        first_kernel,
        "first",
        [
            ((inner, columns, channels), BF16),
            ((2 * HALO, columns, channels), F32),
            ((rows, channels, columns), BF16),
            ((wide_row, wide_row), F32),
            ((3, columns, channels), BF16),
            ((2 * HALO, columns, channels), BF16),
            ((4 * wide_row, 2 * channels), BF16),
            ((2, wide_row, channels), BF16),
            ((2, wide_row, channels), BF16),
        ],
        "svhhhv>vvvvvvvvv",
        [
            pltpu.VMEM((rows, columns, channels), BF16),
            pltpu.VMEM((rows, columns, channels), BF16),
            pltpu.VMEM((9, channels, channels), BF16),
            pads(rows),
            pltpu.VMEM((rows, columns, wide_row), BF16),
            pltpu.VMEM((inner, columns, wide_row), BF16),
            pltpu.VMEM((4 * wide_row, 2 * channels), BF16),
            pltpu.SemaphoreType.DMA((9,)),
        ],
        flops=BUSY,
    )(dilations, lists, in_hbm(x), cot, weight, bias)

    grad_a, grad_b, xt_halo = call(
        rims_kernel,
        "rims",
        [
            rim,
            rim,
            ((2 * HALO, channels, columns), BF16),
        ],
        "svvvvvv>vvv",
        [pads(2 * HALO), pltpu.VMEM((2, HALO * columns, wide_row), BF16), sides, sides],
    )(dilations, x_a, x_b, pre, cot_edge, mask, near)

    from_a, from_b = swap(grad_a, grad_b, "tile")

    tap_rows = 9 * channels
    cores = lax.axis_size("dp")
    paired = cores == 2 and tap_rows % devices == 0
    share = (devices // 2, tap_rows // devices) if paired else (1, tap_rows)
    scale = 1.0 / math.sqrt(devices * lists.shape[1] * TILE * TILE)
    keep, send = call(
        lambda *refs: taps_kernel(*refs, scale=scale, paired=paired),
        "taps",
        [
            (share + (channels,), F32),
            (share + (channels,), BF16),
        ],
        "svvvvv>vv",
        [
            pads(2 * HALO),
            pltpu.VMEM((2 * HALO, columns, wide_row), BF16),
            pltpu.VMEM((tap_rows, channels), F32),
            sides,
        ],
    )(dilations, grad_a, grad_b, xt, xt_halo, total)
    if paired:
        other = lax.ppermute(send, "dp", [(0, 1), (1, 0)])
        both = (keep + other.astype(F32)).astype(BF16)
        received = lax.all_to_all(both, "tile", 0, 0, tiled=True)
    else:
        received = lax.all_to_all(
            keep.astype(BF16).reshape(devices, -1), axes, 0, 0, tiled=True
        )

    (input_grad,) = call(
        last_kernel,
        "last",
        [whole],
        "svvvvvhvvv>h",
        [
            pltpu.VMEM((rows, columns, channels), BF16),
            pltpu.VMEM((rows, columns, channels), BF16),
            pads(rows + 2 * HALO),
            pltpu.VMEM((rows, columns, wide_row), BF16),
            pltpu.VMEM((2, HALO * columns, wide_row), BF16),
            sides,
            sides,
            pltpu.SemaphoreType.DMA((2 * (rows // (2 * HALO)),)),
        ],
        flops=BUSY,
    )(
        dilations, from_a, from_b, grad_a, grad_b,
        grad, cot, mask, back, far,
    )
    summed = jnp.sum(received.astype(F32), axis=0)
    return (input_grad[None], summed.reshape(-1))


def solution(mesh):
    placed = (
        P("dp", "tile", None, None),
        P("dp", "tile", None, None),
        P("dp", "tile", None),
        P("dp", None, None),
        P("dp", None),
        P(),
        P(),
    )
    return jax.shard_map(
        shards,
        mesh=mesh,
        in_specs=placed,
        out_specs=(P("dp", "tile", None, None), P(("tile", "dp"))),
        check_vma=False,
    )
```

```python
import math

import jax
import jax.numpy as jnp
from jax import lax
from jax.experimental import pallas as pl
from jax.experimental.pallas import tpu as pltpu
from jax.sharding import PartitionSpec as P

TILE = 12
HALO = 2
LANES = 128
EDGE = 8
RATES = (1, 2)
VMEM_LIMIT = 40 * 1024 * 1024
BUSY = 20_000_000_000

F32 = jnp.float32
BF16 = jnp.bfloat16


def cell_masks(lists_ref, middle, tiles_row, columns):
    ids = lists_ref[...]
    workers, width = ids.shape
    tile = lax.broadcasted_iota(jnp.int32, (3 * tiles_row, width), 0)
    target = (middle - 1) * tiles_row + tile
    found = ids[0:1] == target
    for worker in range(1, workers):
        found = found | (ids[worker : worker + 1] == target)
    named = jnp.dot(
        jnp.where(found, 1.0, 0.0).astype(BF16),
        jnp.ones((width, LANES), BF16),
        preferred_element_type=F32,
    ).astype(BF16)
    first = TILE * lax.broadcasted_iota(jnp.int32, (columns, tiles_row), 1)
    cell = lax.broadcasted_iota(jnp.int32, (columns, tiles_row), 0)
    inside = jnp.where((cell >= first) & (cell < first + TILE), 1.0, 0.0).astype(BF16)
    return [
        jnp.dot(
            inside, named[k * tiles_row : (k + 1) * tiles_row], preferred_element_type=F32
        ).astype(BF16)
        for k in range(3)
    ]


def row_pairs(rate, rows):
    rows = list(rows)
    pairs = []
    for start in range(0, len(rows), 2 * rate):
        for k in range(rate):
            pairs.append((rows[start + k], rows[start + k + rate]))
    return pairs


def by_rate(rate, body):
    for value in RATES:
        pl.when(rate == value)(lambda value=value: body(value))


def clear_ends(pad_ref, count, columns):
    ends = jnp.zeros((EDGE, pad_ref.shape[-1]), F32)
    for k in range(count):
        pad_ref[k, :EDGE] = ends
        pad_ref[k, EDGE + columns :] = ends


def spread(value, pad_ref, slot, target_ref, offset):
    columns, channels = value.shape
    pad_ref[slot, EDGE : EDGE + columns] = value.astype(F32)
    target_ref[:, :channels] = pad_ref[slot, pl.ds(EDGE - offset, columns)].astype(BF16)
    target_ref[:, channels : 2 * channels] = value.astype(BF16)
    target_ref[:, 2 * channels :] = pad_ref[slot, pl.ds(EDGE + offset, columns)].astype(BF16)


def by_side(a_ref, b_ref, sides_ref):
    odd = lax.axis_index("tile") % 2

    def order(low, high):
        sides_ref[0] = low[...]
        sides_ref[1] = high[...]

    pl.when(odd == 0)(lambda: order(b_ref, a_ref))
    pl.when(odd == 1)(lambda: order(a_ref, b_ref))


def silu_grad(half_cot, half_pre):
    turn = jnp.tanh(half_pre)
    return half_cot * (1.0 + turn + half_pre * (1.0 - turn * turn))


def tap_sums(grads, xts, rate):
    flipped = jnp.concatenate(
        [
            jnp.concatenate([xts(row + rate * a) for row, _ in grads], axis=1)
            for a in (-1, 0, 1)
        ],
        axis=0,
    )
    return jnp.dot(
        flipped,
        jnp.concatenate([ref[...] for _, ref in grads], axis=0),
        preferred_element_type=F32,
    )


def pair_rows(pair, rate, rows):
    reach = [pair[0] + rate * (k - 1) for k in range(4)]
    inside = [k for k in range(4) if 0 <= reach[k] < rows]
    return [reach[k] for k in inside], inside[0], inside[-1] + 1


def input_sums(pair, rate, rows, grads, wide_ref):
    near, low, high = pair_rows(pair, rate, rows)
    lhs = jnp.concatenate([grads(row)[...] for row in near], axis=1)
    width = wide_ref.shape[0] // 4
    both = jnp.dot(lhs, wide_ref[low * width : high * width], preferred_element_type=F32)
    half = both.shape[1] // 2
    return both[:, :half], both[:, half:]


def first_kernel(
    rates_ref, lists_ref, x_hbm, cot_hbm, w_hbm, bias_ref,
    grad_ref, pre_ref, xt_ref, total_ref, mask_ref, cot_ref, back_ref, near_ref, far_ref,
    xbuf, cbuf, wbuf, pad, xcat, gcat_ref, wide, sems,
):
    rows, columns, channels = x_hbm.shape
    tiles_row = columns // TILE
    mine = lax.axis_index("tile")
    step = rows // 4
    loads = [pltpu.make_async_copy(w_hbm, wbuf, sems.at[0])]
    for source, target, base in ((x_hbm, xbuf, 1), (cot_hbm, cbuf, 5)):
        for k in range(4):
            part = pl.ds(k * step, step)
            loads.append(
                pltpu.make_async_copy(source.at[part], target.at[part], sems.at[base + k])
            )
    for load in loads:
        load.start()
    for k, value in enumerate(cell_masks(lists_ref, mine, tiles_row, columns)):
        mask_ref[k] = value
    clear_ends(pad, rows, columns)
    loads[0].wait()
    none = jnp.zeros((channels, channels), BF16)
    for col in range(3):
        there = slice(col * channels, (col + 1) * channels)
        turned = [wbuf[tap * 3 + col].T for tap in range(3)]
        for side in range(2):
            near_ref[side, there] = wbuf[6 * side + col]
            far_ref[side, there] = turned[2 - 2 * side]
        for row in range(4):
            start = (row * 3 + col) * channels
            here = slice(start, start + channels)
            for out in range(2):
                there = slice(out * channels, (out + 1) * channels)
                tap = row - out
                wide[here, there] = wbuf[tap * 3 + col] if 0 <= tap < 3 else none
                tap = out + 2 - row
                back_ref[here, there] = turned[tap] if 0 <= tap < 3 else none
    for load in loads[1:]:
        load.wait()
    half_bias = 0.5 * bias_ref[...]

    def body(rate):
        done = set()

        def prepare(row):
            if row in done:
                return
            done.add(row)
            value = xbuf[row] * mask_ref[1]
            spread(value, pad, row, xcat.at[row], rate)
            xt_ref[row] = value.T

        def convolve(pair):
            near, low, high = pair_rows(pair, rate, rows)
            for row in near:
                prepare(row)
            lhs = jnp.concatenate([xcat[row] for row in near], axis=1)
            width = wide.shape[0] // 4
            both = jnp.dot(
                lhs, wide[low * width : high * width], preferred_element_type=F32
            )
            return pair, (both[:, :channels], both[:, channels:])

        def finish(pair, sums):
            for row, value in zip(pair, sums):
                half_pre = 0.5 * value + half_bias
                half_cot = cbuf[row] * mask_ref[1] * 0.5
                if HALO <= row < rows - HALO:
                    grad = silu_grad(half_cot.astype(F32), half_pre)
                    spread(grad, pad, row, gcat_ref.at[row - HALO], -rate)
                    grad_ref[row - HALO] = grad.astype(BF16)
                    ready.append(row)
                else:
                    here = row if row < HALO else row - (rows - 2 * HALO)
                    pre_ref[here] = half_pre
                    cot_ref[here] = half_cot

        ready = []
        summed = []
        waiting = None
        for pair in row_pairs(rate, range(rows)) + [None]:
            result = convolve(pair) if pair else None
            if waiting:
                finish(*waiting)
            waiting = result
            while len(ready) >= 2:
                grads = [(row, gcat_ref.at[row - HALO]) for row in ready[:2]]
                part = tap_sums(grads, lambda row: xt_ref[row], rate)
                total_ref[...] = total_ref[...] + part if summed else part
                summed.extend(ready[:2])
                del ready[:2]

    by_rate(rates_ref[0, mine], body)


def rims_kernel(
    rates_ref, a_ref, b_ref, pre_ref, cot_ref, mask_ref, near_ref,
    grad_a_ref, grad_b_ref, xt_ref,
    pad, xcat, halo, grads,
):
    _, columns, channels = a_ref.shape
    clear_ends(pad, 2 * HALO, columns)
    by_side(a_ref, b_ref, halo)

    def body(rate):
        for side in range(2):
            used = range(HALO - rate, HALO) if side == 0 else range(rate)
            for place, k in enumerate(used):
                value = halo[side, k] * mask_ref[2 * side]
                part = pl.ds(place * columns, columns)
                spread(value, pad, side * HALO + k, xcat.at[side, part], rate)
                xt_ref[side * HALO + k] = value.T
            sums = jnp.dot(
                xcat[side, : rate * columns], near_ref[side], preferred_element_type=F32
            )
            for k in range(HALO):
                half_pre = pre_ref[side * HALO + k]
                place = k if side == 0 else k - (HALO - rate)
                if 0 <= place < rate:
                    half_pre += 0.5 * sums[place * columns : (place + 1) * columns]
                grad = silu_grad(cot_ref[side * HALO + k].astype(F32), half_pre)
                grads[side, k] = grad.astype(BF16)

    by_rate(rates_ref[0, lax.axis_index("tile")], body)
    odd = lax.axis_index("tile") % 2
    grad_a_ref[...] = grads[1 - odd]
    grad_b_ref[...] = grads[odd]


def taps_kernel(
    rates_ref, grad_a_ref, grad_b_ref, xt_own_ref, xt_halo_ref, total_ref,
    keep_ref, send_ref, later_ref,
    pad, gedge_ref, flat, sides, *, scale, paired,
):
    _, columns, channels = grad_a_ref.shape
    later_ref[...] = grad_b_ref[...]
    by_side(grad_a_ref, grad_b_ref, sides)
    rows = xt_own_ref.shape[0]
    clear_ends(pad, 2 * HALO, columns)

    def flipped(row):
        if row < 0:
            return xt_halo_ref[row + HALO]
        return xt_own_ref[row] if row < rows else xt_halo_ref[row - rows + HALO]

    def body(rate):
        edges = []
        for side in range(2):
            for k in range(HALO):
                slot = side * HALO + k
                spread(sides[side, k], pad, slot, gedge_ref.at[slot], -rate)
                edges.append((k + side * (rows - HALO), gedge_ref.at[slot]))
        total = (total_ref[...] + tap_sums(edges, flipped, rate)) * scale
        for a in range(3):
            for b in range(3):
                start = (a * 3 + b) * channels
                flat[start : start + channels] = total[
                    a * channels : (a + 1) * channels, b * channels : (b + 1) * channels
                ]

    by_rate(rates_ref[0, lax.axis_index("tile")], body)
    if not paired:
        keep_ref[0] = flat[...]
        return
    parts, share, _ = keep_ref.shape
    here = lax.axis_index("dp")
    for part in range(parts):
        keep_ref[part] = flat[pl.ds((2 * part + here) * share, share)]
        send_ref[part] = flat[pl.ds((2 * part + 1 - here) * share, share)].astype(BF16)


def last_kernel(
    rates_ref, from_a_ref, from_b_ref, grad_a_ref, grad_b_ref,
    grad_ref, cot_hbm, mask_ref, back_ref, far_ref,
    out_hbm,
    cbuf, obuf, pad, gcat, spare, theirs, ours, sems,
):
    rows, columns, channels = cot_hbm.shape
    inner = rows - 2 * HALO
    mine = lax.axis_index("tile")
    last = rates_ref.shape[1] - 1
    around = 2 * HALO
    chunks = rows // around
    cots, stores = [], []
    for k in range(chunks):
        part = pl.ds(k * around, around)
        cots.append(
            pltpu.make_async_copy(cot_hbm.at[part], cbuf.at[part], sems.at[k])
        )
        stores.append(
            pltpu.make_async_copy(obuf.at[part], out_hbm.at[part], sems.at[chunks + k])
        )
    for load in cots:
        load.start()
    clear_ends(pad, rows + 2 * HALO, columns)
    by_side(from_a_ref, from_b_ref, theirs)
    by_side(grad_a_ref, grad_b_ref, ours)

    def neighbour(side):
        rate = rates_ref[0, jnp.minimum(mine + 1, last) if side else jnp.maximum(mine - 1, 0)]
        for k in range(HALO):
            part = pl.ds(k * columns, columns)
            spread(theirs[side, k], pad, rows + side * HALO + k, spare.at[side, part], -rate)
        sums = jnp.dot(spare[side], far_ref[side], preferred_element_type=F32)
        parts = [sums[k * columns : (k + 1) * columns] for k in range(HALO)]
        none = jnp.zeros((columns, channels), F32)
        one = rate == 1
        if side:
            return [jnp.where(one, none, parts[0]), jnp.where(one, parts[0], parts[1])]
        return [jnp.where(one, parts[1], parts[0]), jnp.where(one, none, parts[1])]

    def body(rate):
        done = set()

        def shifted(row):
            if row not in done:
                done.add(row)
                if row < HALO:
                    value = ours[0, row]
                elif row < rows - HALO:
                    value = grad_ref[row - HALO]
                else:
                    value = ours[1, row - (rows - HALO)]
                spread(value, pad, row, gcat.at[row], -rate)
            return gcat.at[row]

        for chunk in range(chunks):
            start = chunk * around
            results = [
                (pair, input_sums(pair, rate, rows, shifted, back_ref))
                for pair in row_pairs(rate, range(start, start + around))
            ]
            terms = {0: 0, chunks - 1: 1}
            added = neighbour(terms[chunk]) if chunk in terms else None
            cots[chunk].wait()
            for pair, sums in results:
                for row, value in zip(pair, sums):
                    value = value + cbuf[row].astype(F32)
                    if row < HALO:
                        value = value + added[row]
                    elif row >= rows - HALO:
                        value = value + added[row - (rows - HALO)]
                    obuf[row] = value.astype(BF16) * mask_ref[1]
            stores[chunk].start()

    by_rate(rates_ref[0, mine], body)
    for store in stores:
        store.wait()


def cut_kernel(x_hbm, a_ref, b_ref, sems):
    rows = x_hbm.shape[0]
    odd = lax.axis_index("tile") % 2
    copies = []
    for index, ref in enumerate((a_ref, b_ref)):
        start = (rows - HALO) * (odd if index else 1 - odd)
        for k in range(HALO):
            copies.append(
                pltpu.make_async_copy(x_hbm.at[start + k], ref.at[k], sems.at[index, k])
            )
    for copy in copies:
        copy.start()
    for copy in copies:
        copy.wait()


def add_kernel(keep_ref, other_ref, sum_ref):
    sum_ref[...] = (keep_ref[...] + other_ref[...].astype(F32)).astype(BF16)


def swap(rows, axis, start):
    pairs = [(i, i + 1) for i in range(start, lax.axis_size(axis) - 1, 2)]
    return lax.ppermute(rows, axis, pairs + [(j, i) for i, j in pairs])


def call(kernel, name, outs, specs, scratch, aliases=None, flops=0):
    memory = {"s": pltpu.SMEM, "v": pltpu.VMEM, "h": pltpu.HBM}
    ins, results = (
        [pl.BlockSpec(memory_space=memory[letter]) for letter in part] for part in specs.split(">")
    )
    return pl.pallas_call(
        kernel,
        name=name,
        out_shape=tuple(
            pltpu.HBM(shape, dtype) if letter == "h" else jax.ShapeDtypeStruct(shape, dtype)
            for (shape, dtype), letter in zip(outs, specs.split(">")[1])
        ),
        in_specs=ins,
        out_specs=tuple(results),
        scratch_shapes=scratch,
        input_output_aliases=aliases or {},
        cost_estimate=pl.CostEstimate(flops=flops, bytes_accessed=0, transcendentals=0),
        compiler_params=pltpu.CompilerParams(vmem_limit_bytes=VMEM_LIMIT),
    )


def in_hbm(array):
    return pltpu.with_memory_space_constraint(array, pltpu.HBM)


def shards(features, cotangent, tile_mask, work_lists, dilations, conv_weight, conv_bias):
    x, cot, lists = features[0], in_hbm(cotangent[0]), in_hbm(work_lists[0])
    dilations = in_hbm(dilations)
    rows, columns, channels = x.shape
    axes = ("tile", "dp")
    devices = lax.axis_size("tile") * lax.axis_size("dp")
    weight = in_hbm(conv_weight.reshape(9, channels, channels))
    bias = in_hbm(conv_bias.reshape(1, channels))
    inner = rows - 2 * HALO
    wide_row = 3 * channels
    whole = ((rows, columns, channels), BF16)

    def pads(count):
        return pltpu.VMEM((count, columns + 2 * EDGE, channels), F32)

    rim = ((HALO, columns, channels), BF16)
    sides = pltpu.VMEM((2, HALO, columns, channels), BF16)
    rows_a, rows_b = call(
        cut_kernel,
        "cut",
        [rim, rim],
        "h>vv",
        [pltpu.SemaphoreType.DMA((2, HALO))],
    )(in_hbm(x))
    x_a, x_b = swap(rows_a, "tile", 0), swap(rows_b, "tile", 1)

    grad, pre, xt, total, mask, cot_edge, back, near, far = call(
        first_kernel,
        "first",
        [
            ((inner, columns, channels), BF16),
            ((2 * HALO, columns, channels), F32),
            ((rows, channels, columns), BF16),
            ((wide_row, wide_row), F32),
            ((3, columns, channels), BF16),
            ((2 * HALO, columns, channels), BF16),
            ((4 * wide_row, 2 * channels), BF16),
            ((2, wide_row, channels), BF16),
            ((2, wide_row, channels), BF16),
        ],
        "svhhhv>vvvvvvvvv",
        [
            pltpu.VMEM((rows, columns, channels), BF16),
            pltpu.VMEM((rows, columns, channels), BF16),
            pltpu.VMEM((9, channels, channels), BF16),
            pads(rows),
            pltpu.VMEM((rows, columns, wide_row), BF16),
            pltpu.VMEM((inner, columns, wide_row), BF16),
            pltpu.VMEM((4 * wide_row, 2 * channels), BF16),
            pltpu.SemaphoreType.DMA((9,)),
        ],
        flops=BUSY,
    )(dilations, lists, in_hbm(x), cot, weight, bias)

    grad_a, grad_b, xt_halo = call(
        rims_kernel,
        "rims",
        [
            rim,
            rim,
            ((2 * HALO, channels, columns), BF16),
        ],
        "svvvvvv>vvv",
        [pads(2 * HALO), pltpu.VMEM((2, HALO * columns, wide_row), BF16), sides, sides],
    )(dilations, x_a, x_b, pre, cot_edge, mask, near)

    from_a = swap(grad_a, "tile", 0)

    tap_rows = 9 * channels
    cores = lax.axis_size("dp")
    paired = cores == 2 and tap_rows % devices == 0
    share = (devices // 2, tap_rows // devices) if paired else (1, tap_rows)
    scale = 1.0 / math.sqrt(devices * lists.shape[1] * TILE * TILE)
    keep, send, later_b = call(
        lambda *refs: taps_kernel(*refs, scale=scale, paired=paired),
        "taps",
        [
            (share + (channels,), F32),
            (share + (channels,), BF16),
            rim,
        ],
        "svvvvv>vvv",
        [
            pads(2 * HALO),
            pltpu.VMEM((2 * HALO, columns, wide_row), BF16),
            pltpu.VMEM((tap_rows, channels), F32),
            sides,
        ],
    )(dilations, grad_a, grad_b, xt, xt_halo, total)
    from_b = swap(later_b, "tile", 1)
    if paired:
        other = lax.ppermute(send, "dp", [(0, 1), (1, 0)])
        (both,) = call(add_kernel, "add", [(share + (channels,), BF16)], "vv>v", [])(keep, other)
        received = lax.all_to_all(both, "tile", 0, 0, tiled=True)
    else:
        received = lax.all_to_all(
            keep.astype(BF16).reshape(devices, -1), axes, 0, 0, tiled=True
        )

    (input_grad,) = call(
        last_kernel,
        "last",
        [whole],
        "svvvvvhvvv>h",
        [
            pltpu.VMEM((rows, columns, channels), BF16),
            pltpu.VMEM((rows, columns, channels), BF16),
            pads(rows + 2 * HALO),
            pltpu.VMEM((rows, columns, wide_row), BF16),
            pltpu.VMEM((2, HALO * columns, wide_row), BF16),
            sides,
            sides,
            pltpu.SemaphoreType.DMA((2 * (rows // (2 * HALO)),)),
        ],
        flops=BUSY,
    )(
        dilations, from_a, from_b, grad_a, later_b,
        grad, cot, mask, back, far,
    )
    summed = jnp.sum(received.astype(F32), axis=0)
    return (input_grad[None], summed.reshape(-1))


def solution(mesh):
    placed = (
        P("dp", "tile", None, None),
        P("dp", "tile", None, None),
        P("dp", "tile", None),
        P("dp", None, None),
        P("dp", None),
        P(),
        P(),
    )
    return jax.shard_map(
        shards,
        mesh=mesh,
        in_specs=placed,
        out_specs=(P("dp", "tile", None, None), P(("tile", "dp"))),
        check_vma=False,
    )
```

```python
import math

import jax
import jax.numpy as jnp
from jax import lax
from jax.experimental import pallas as pl
from jax.experimental.pallas import tpu as pltpu
from jax.sharding import PartitionSpec as P

TILE = 12
HALO = 2
LANES = 128
EDGE = 8
RATES = (1, 2)
VMEM_LIMIT = 40 * 1024 * 1024
BUSY = 20_000_000_000

F32 = jnp.float32
BF16 = jnp.bfloat16


def cell_masks(lists_ref, middle, tiles_row, columns):
    ids = lists_ref[...]
    workers, width = ids.shape
    tile = lax.broadcasted_iota(jnp.int32, (3 * tiles_row, width), 0)
    target = (middle - 1) * tiles_row + tile
    found = ids[0:1] == target
    for worker in range(1, workers):
        found = found | (ids[worker : worker + 1] == target)
    named = jnp.dot(
        jnp.where(found, 1.0, 0.0).astype(BF16),
        jnp.ones((width, LANES), BF16),
        preferred_element_type=F32,
    ).astype(BF16)
    first = TILE * lax.broadcasted_iota(jnp.int32, (columns, tiles_row), 1)
    cell = lax.broadcasted_iota(jnp.int32, (columns, tiles_row), 0)
    inside = jnp.where((cell >= first) & (cell < first + TILE), 1.0, 0.0).astype(BF16)
    return [
        jnp.dot(
            inside, named[k * tiles_row : (k + 1) * tiles_row], preferred_element_type=F32
        ).astype(BF16)
        for k in range(3)
    ]


def row_pairs(rate, rows):
    rows = list(rows)
    pairs = []
    for start in range(0, len(rows), 2 * rate):
        for k in range(rate):
            pairs.append((rows[start + k], rows[start + k + rate]))
    return pairs


def by_rate(rate, body):
    for value in RATES:
        pl.when(rate == value)(lambda value=value: body(value))


def clear_ends(pad_ref, count, columns):
    ends = jnp.zeros((EDGE, pad_ref.shape[-1]), F32)
    for k in range(count):
        pad_ref[k, :EDGE] = ends
        pad_ref[k, EDGE + columns :] = ends


def spread(value, pad_ref, slot, target_ref, offset):
    columns, channels = value.shape
    pad_ref[slot, EDGE : EDGE + columns] = value.astype(F32)
    target_ref[:, :channels] = pad_ref[slot, pl.ds(EDGE - offset, columns)].astype(BF16)
    target_ref[:, channels : 2 * channels] = value.astype(BF16)
    target_ref[:, 2 * channels :] = pad_ref[slot, pl.ds(EDGE + offset, columns)].astype(BF16)


def by_side(a_ref, b_ref, sides_ref):
    odd = lax.axis_index("tile") % 2

    def order(low, high):
        sides_ref[0] = low[...]
        sides_ref[1] = high[...]

    pl.when(odd == 0)(lambda: order(b_ref, a_ref))
    pl.when(odd == 1)(lambda: order(a_ref, b_ref))


def silu_grad(half_cot, half_pre):
    turn = jnp.tanh(half_pre)
    return half_cot * (1.0 + turn + half_pre * (1.0 - turn * turn))


def tap_sums(grads, xts, rate):
    flipped = jnp.concatenate(
        [
            jnp.concatenate([xts(row + rate * a) for row, _ in grads], axis=1)
            for a in (-1, 0, 1)
        ],
        axis=0,
    )
    return jnp.dot(
        flipped,
        jnp.concatenate([ref[...] for _, ref in grads], axis=0),
        preferred_element_type=F32,
    )


def pair_rows(pair, rate, rows):
    reach = [pair[0] + rate * (k - 1) for k in range(4)]
    inside = [k for k in range(4) if 0 <= reach[k] < rows]
    return [reach[k] for k in inside], inside[0], inside[-1] + 1


def input_sums(pair, rate, rows, grads, wide_ref):
    near, low, high = pair_rows(pair, rate, rows)
    lhs = jnp.concatenate([grads(row)[...] for row in near], axis=1)
    width = wide_ref.shape[0] // 4
    both = jnp.dot(lhs, wide_ref[low * width : high * width], preferred_element_type=F32)
    half = both.shape[1] // 2
    return both[:, :half], both[:, half:]


def first_kernel(
    rates_ref, lists_ref, x_hbm, cot_hbm, w_hbm, bias_ref,
    grad_ref, pre_ref, xt_ref, total_ref, mask_ref, cot_ref, back_ref, near_ref, far_ref,
    xbuf, cbuf, wbuf, pad, xcat, gcat_ref, wide, sems,
):
    rows, columns, channels = x_hbm.shape
    tiles_row = columns // TILE
    mine = lax.axis_index("tile")
    step = rows // 4
    loads = [pltpu.make_async_copy(w_hbm, wbuf, sems.at[0])]
    for source, target, base in ((x_hbm, xbuf, 1), (cot_hbm, cbuf, 5)):
        for k in range(4):
            part = pl.ds(k * step, step)
            loads.append(
                pltpu.make_async_copy(source.at[part], target.at[part], sems.at[base + k])
            )
    for load in loads:
        load.start()
    for k, value in enumerate(cell_masks(lists_ref, mine, tiles_row, columns)):
        mask_ref[k] = value
    clear_ends(pad, rows, columns)
    loads[0].wait()
    none = jnp.zeros((channels, channels), BF16)
    for col in range(3):
        there = slice(col * channels, (col + 1) * channels)
        turned = [wbuf[tap * 3 + col].T for tap in range(3)]
        for side in range(2):
            near_ref[side, there] = wbuf[6 * side + col]
            far_ref[side, there] = turned[2 - 2 * side]
        for row in range(4):
            start = (row * 3 + col) * channels
            here = slice(start, start + channels)
            for out in range(2):
                there = slice(out * channels, (out + 1) * channels)
                tap = row - out
                wide[here, there] = wbuf[tap * 3 + col] if 0 <= tap < 3 else none
                tap = out + 2 - row
                back_ref[here, there] = turned[tap] if 0 <= tap < 3 else none
    for load in loads[1:]:
        load.wait()
    half_bias = 0.5 * bias_ref[...]

    def body(rate):
        done = set()

        def prepare(row):
            if row in done:
                return
            done.add(row)
            value = xbuf[row] * mask_ref[1]
            spread(value, pad, row, xcat.at[row], rate)
            xt_ref[row] = value.T

        def convolve(pair):
            near, low, high = pair_rows(pair, rate, rows)
            for row in near:
                prepare(row)
            lhs = jnp.concatenate([xcat[row] for row in near], axis=1)
            width = wide.shape[0] // 4
            both = jnp.dot(
                lhs, wide[low * width : high * width], preferred_element_type=F32
            )
            return pair, (both[:, :channels], both[:, channels:])

        def finish(pair, sums):
            for row, value in zip(pair, sums):
                half_pre = 0.5 * value + half_bias
                half_cot = cbuf[row] * mask_ref[1] * 0.5
                if HALO <= row < rows - HALO:
                    grad = silu_grad(half_cot.astype(F32), half_pre)
                    spread(grad, pad, row, gcat_ref.at[row - HALO], -rate)
                    grad_ref[row - HALO] = grad.astype(BF16)
                    ready.append(row)
                else:
                    here = row if row < HALO else row - (rows - 2 * HALO)
                    pre_ref[here] = half_pre
                    cot_ref[here] = half_cot

        ready = []
        summed = []
        waiting = None
        for pair in row_pairs(rate, range(rows)) + [None]:
            result = convolve(pair) if pair else None
            if waiting:
                finish(*waiting)
            waiting = result
            while len(ready) >= 2:
                grads = [(row, gcat_ref.at[row - HALO]) for row in ready[:2]]
                part = tap_sums(grads, lambda row: xt_ref[row], rate)
                total_ref[...] = total_ref[...] + part if summed else part
                summed.extend(ready[:2])
                del ready[:2]

    by_rate(rates_ref[0, mine], body)


def rims_kernel(
    rates_ref, a_ref, b_ref, pre_ref, cot_ref, mask_ref, near_ref,
    grad_a_ref, grad_b_ref, xt_ref,
    pad, xcat, halo, grads,
):
    _, columns, channels = a_ref.shape
    clear_ends(pad, 2 * HALO, columns)
    by_side(a_ref, b_ref, halo)

    def body(rate):
        for side in range(2):
            used = range(HALO - rate, HALO) if side == 0 else range(rate)
            for place, k in enumerate(used):
                value = halo[side, k] * mask_ref[2 * side]
                part = pl.ds(place * columns, columns)
                spread(value, pad, side * HALO + k, xcat.at[side, part], rate)
                xt_ref[side * HALO + k] = value.T
            sums = jnp.dot(
                xcat[side, : rate * columns], near_ref[side], preferred_element_type=F32
            )
            for k in range(HALO):
                half_pre = pre_ref[side * HALO + k]
                place = k if side == 0 else k - (HALO - rate)
                if 0 <= place < rate:
                    half_pre += 0.5 * sums[place * columns : (place + 1) * columns]
                grad = silu_grad(cot_ref[side * HALO + k].astype(F32), half_pre)
                grads[side, k] = grad.astype(BF16)

    by_rate(rates_ref[0, lax.axis_index("tile")], body)
    odd = lax.axis_index("tile") % 2
    grad_a_ref[...] = grads[1 - odd]
    grad_b_ref[...] = grads[odd]


def taps_kernel(
    rates_ref, grad_a_ref, grad_b_ref, xt_own_ref, xt_halo_ref, total_ref,
    keep_ref, send_ref, later_ref,
    pad, gedge_ref, flat, sides, *, scale, paired,
):
    _, columns, channels = grad_a_ref.shape
    later_ref[...] = grad_b_ref[...]
    by_side(grad_a_ref, grad_b_ref, sides)
    rows = xt_own_ref.shape[0]
    clear_ends(pad, 2 * HALO, columns)

    def flipped(row):
        if row < 0:
            return xt_halo_ref[row + HALO]
        return xt_own_ref[row] if row < rows else xt_halo_ref[row - rows + HALO]

    def body(rate):
        edges = []
        for side in range(2):
            for k in range(HALO):
                slot = side * HALO + k
                spread(sides[side, k], pad, slot, gedge_ref.at[slot], -rate)
                edges.append((k + side * (rows - HALO), gedge_ref.at[slot]))
        total = (total_ref[...] + tap_sums(edges, flipped, rate)) * scale
        for a in range(3):
            for b in range(3):
                start = (a * 3 + b) * channels
                flat[start : start + channels] = total[
                    a * channels : (a + 1) * channels, b * channels : (b + 1) * channels
                ]

    by_rate(rates_ref[0, lax.axis_index("tile")], body)
    if not paired:
        keep_ref[0] = flat[...]
        return
    parts, share, _ = keep_ref.shape
    here = lax.axis_index("dp")
    for part in range(parts):
        keep_ref[part] = flat[pl.ds((2 * part + here) * share, share)]
        send_ref[part] = flat[pl.ds((2 * part + 1 - here) * share, share)].astype(BF16)


def last_kernel(
    rates_ref, from_a_ref, from_b_ref, grad_a_ref, grad_b_ref,
    grad_ref, cot_hbm, mask_ref, back_ref, far_ref,
    out_hbm,
    cbuf, obuf, pad, gcat, spare, theirs, ours, sems,
):
    rows, columns, channels = cot_hbm.shape
    inner = rows - 2 * HALO
    mine = lax.axis_index("tile")
    last = rates_ref.shape[1] - 1
    around = 2 * HALO
    chunks = rows // around
    cots, stores = [], []
    for k in range(chunks):
        part = pl.ds(k * around, around)
        cots.append(
            pltpu.make_async_copy(cot_hbm.at[part], cbuf.at[part], sems.at[k])
        )
        stores.append(
            pltpu.make_async_copy(obuf.at[part], out_hbm.at[part], sems.at[chunks + k])
        )
    for load in cots:
        load.start()
    clear_ends(pad, rows + 2 * HALO, columns)
    by_side(from_a_ref, from_b_ref, theirs)
    by_side(grad_a_ref, grad_b_ref, ours)

    def neighbour(side):
        rate = rates_ref[0, jnp.minimum(mine + 1, last) if side else jnp.maximum(mine - 1, 0)]
        for k in range(HALO):
            part = pl.ds(k * columns, columns)
            spread(theirs[side, k], pad, rows + side * HALO + k, spare.at[side, part], -rate)
        sums = jnp.dot(spare[side], far_ref[side], preferred_element_type=F32)
        parts = [sums[k * columns : (k + 1) * columns] for k in range(HALO)]
        none = jnp.zeros((columns, channels), F32)
        one = rate == 1
        if side:
            return [jnp.where(one, none, parts[0]), jnp.where(one, parts[0], parts[1])]
        return [jnp.where(one, parts[1], parts[0]), jnp.where(one, none, parts[1])]

    def body(rate):
        done = set()

        def shifted(row):
            if row not in done:
                done.add(row)
                if row < HALO:
                    value = ours[0, row]
                elif row < rows - HALO:
                    value = grad_ref[row - HALO]
                else:
                    value = ours[1, row - (rows - HALO)]
                spread(value, pad, row, gcat.at[row], -rate)
            return gcat.at[row]

        for chunk in range(chunks):
            start = chunk * around
            results = [
                (pair, input_sums(pair, rate, rows, shifted, back_ref))
                for pair in row_pairs(rate, range(start, start + around))
            ]
            terms = {0: 0, chunks - 1: 1}
            added = neighbour(terms[chunk]) if chunk in terms else None
            cots[chunk].wait()
            for pair, sums in results:
                for row, value in zip(pair, sums):
                    value = value + cbuf[row].astype(F32)
                    if row < HALO:
                        value = value + added[row]
                    elif row >= rows - HALO:
                        value = value + added[row - (rows - HALO)]
                    obuf[row] = value.astype(BF16) * mask_ref[1]
            stores[chunk].start()

    by_rate(rates_ref[0, mine], body)
    for store in stores:
        store.wait()


def cut_kernel(x_hbm, a_ref, b_ref, sems):
    rows = x_hbm.shape[0]
    odd = lax.axis_index("tile") % 2
    copies = []
    for index, ref in enumerate((a_ref, b_ref)):
        start = (rows - HALO) * (odd if index else 1 - odd)
        for k in range(HALO):
            copies.append(
                pltpu.make_async_copy(x_hbm.at[start + k], ref.at[k], sems.at[index, k])
            )
    for copy in copies:
        copy.start()
    for copy in copies:
        copy.wait()


def add_kernel(keep_ref, other_ref, rows_ref, sum_ref, later_ref):
    sum_ref[...] = (keep_ref[...] + other_ref[...].astype(F32)).astype(BF16)
    later_ref[...] = rows_ref[...]


def swap(rows, axis, start):
    pairs = [(i, i + 1) for i in range(start, lax.axis_size(axis) - 1, 2)]
    return lax.ppermute(rows, axis, pairs + [(j, i) for i, j in pairs])


def call(kernel, name, outs, specs, scratch, aliases=None, flops=0):
    memory = {"s": pltpu.SMEM, "v": pltpu.VMEM, "h": pltpu.HBM}
    ins, results = (
        [pl.BlockSpec(memory_space=memory[letter]) for letter in part] for part in specs.split(">")
    )
    return pl.pallas_call(
        kernel,
        name=name,
        out_shape=tuple(
            pltpu.HBM(shape, dtype) if letter == "h" else jax.ShapeDtypeStruct(shape, dtype)
            for (shape, dtype), letter in zip(outs, specs.split(">")[1])
        ),
        in_specs=ins,
        out_specs=tuple(results),
        scratch_shapes=scratch,
        input_output_aliases=aliases or {},
        cost_estimate=pl.CostEstimate(flops=flops, bytes_accessed=0, transcendentals=0),
        compiler_params=pltpu.CompilerParams(vmem_limit_bytes=VMEM_LIMIT),
    )


def in_hbm(array):
    return pltpu.with_memory_space_constraint(array, pltpu.HBM)


def shards(features, cotangent, tile_mask, work_lists, dilations, conv_weight, conv_bias):
    x, cot, lists = features[0], in_hbm(cotangent[0]), in_hbm(work_lists[0])
    dilations = in_hbm(dilations)
    rows, columns, channels = x.shape
    axes = ("tile", "dp")
    devices = lax.axis_size("tile") * lax.axis_size("dp")
    weight = in_hbm(conv_weight.reshape(9, channels, channels))
    bias = in_hbm(conv_bias.reshape(1, channels))
    inner = rows - 2 * HALO
    wide_row = 3 * channels
    whole = ((rows, columns, channels), BF16)

    def pads(count):
        return pltpu.VMEM((count, columns + 2 * EDGE, channels), F32)

    rim = ((HALO, columns, channels), BF16)
    sides = pltpu.VMEM((2, HALO, columns, channels), BF16)
    rows_a, rows_b = call(
        cut_kernel,
        "cut",
        [rim, rim],
        "h>vv",
        [pltpu.SemaphoreType.DMA((2, HALO))],
    )(in_hbm(x))
    x_a, x_b = swap(rows_a, "tile", 0), swap(rows_b, "tile", 1)

    grad, pre, xt, total, mask, cot_edge, back, near, far = call(
        first_kernel,
        "first",
        [
            ((inner, columns, channels), BF16),
            ((2 * HALO, columns, channels), F32),
            ((rows, channels, columns), BF16),
            ((wide_row, wide_row), F32),
            ((3, columns, channels), BF16),
            ((2 * HALO, columns, channels), BF16),
            ((4 * wide_row, 2 * channels), BF16),
            ((2, wide_row, channels), BF16),
            ((2, wide_row, channels), BF16),
        ],
        "svhhhv>vvvvvvvvv",
        [
            pltpu.VMEM((rows, columns, channels), BF16),
            pltpu.VMEM((rows, columns, channels), BF16),
            pltpu.VMEM((9, channels, channels), BF16),
            pads(rows),
            pltpu.VMEM((rows, columns, wide_row), BF16),
            pltpu.VMEM((inner, columns, wide_row), BF16),
            pltpu.VMEM((4 * wide_row, 2 * channels), BF16),
            pltpu.SemaphoreType.DMA((9,)),
        ],
        flops=BUSY,
    )(dilations, lists, in_hbm(x), cot, weight, bias)

    grad_a, grad_b, xt_halo = call(
        rims_kernel,
        "rims",
        [
            rim,
            rim,
            ((2 * HALO, channels, columns), BF16),
        ],
        "svvvvvv>vvv",
        [pads(2 * HALO), pltpu.VMEM((2, HALO * columns, wide_row), BF16), sides, sides],
    )(dilations, x_a, x_b, pre, cot_edge, mask, near)

    from_a = swap(grad_a, "tile", 0)

    tap_rows = 9 * channels
    cores = lax.axis_size("dp")
    paired = cores == 2 and tap_rows % devices == 0
    share = (devices // 2, tap_rows // devices) if paired else (1, tap_rows)
    scale = 1.0 / math.sqrt(devices * lists.shape[1] * TILE * TILE)
    keep, send, later_b = call(
        lambda *refs: taps_kernel(*refs, scale=scale, paired=paired),
        "taps",
        [
            (share + (channels,), F32),
            (share + (channels,), BF16),
            rim,
        ],
        "svvvvv>vvv",
        [
            pads(2 * HALO),
            pltpu.VMEM((2 * HALO, columns, wide_row), BF16),
            pltpu.VMEM((tap_rows, channels), F32),
            sides,
        ],
        flops=BUSY,
    )(dilations, grad_a, grad_b, xt, xt_halo, total)
    from_b = swap(later_b, "tile", 1)
    if paired:
        other = lax.ppermute(send, "dp", [(0, 1), (1, 0)])
        both, from_a = call(
            add_kernel, "add", [(share + (channels,), BF16), rim], "vvv>vv", []
        )(keep, other, from_a)
        received = lax.all_to_all(both, "tile", 0, 0, tiled=True)
    else:
        received = lax.all_to_all(
            keep.astype(BF16).reshape(devices, -1), axes, 0, 0, tiled=True
        )

    (input_grad,) = call(
        last_kernel,
        "last",
        [whole],
        "svvvvvhvvv>h",
        [
            pltpu.VMEM((rows, columns, channels), BF16),
            pltpu.VMEM((rows, columns, channels), BF16),
            pads(rows + 2 * HALO),
            pltpu.VMEM((rows, columns, wide_row), BF16),
            pltpu.VMEM((2, HALO * columns, wide_row), BF16),
            sides,
            sides,
            pltpu.SemaphoreType.DMA((2 * (rows // (2 * HALO)),)),
        ],
        flops=BUSY,
    )(
        dilations, from_a, from_b, grad_a, later_b,
        grad, cot, mask, back, far,
    )
    summed = jnp.sum(received.astype(F32), axis=0)
    return (input_grad[None], summed.reshape(-1))


def solution(mesh):
    placed = (
        P("dp", "tile", None, None),
        P("dp", "tile", None, None),
        P("dp", "tile", None),
        P("dp", None, None),
        P("dp", None),
        P(),
        P(),
    )
    return jax.shard_map(
        shards,
        mesh=mesh,
        in_specs=placed,
        out_specs=(P("dp", "tile", None, None), P(("tile", "dp"))),
        check_vma=False,
    )
```

```python
import math

import jax
import jax.numpy as jnp
from jax import lax
from jax.experimental import pallas as pl
from jax.experimental.pallas import tpu as pltpu
from jax.sharding import PartitionSpec as P

TILE = 12
HALO = 2
LANES = 128
EDGE = 8
RATES = (1, 2)
VMEM_LIMIT = 40 * 1024 * 1024
BUSY = 20_000_000_000

F32 = jnp.float32
BF16 = jnp.bfloat16


def cell_masks(lists_ref, middle, tiles_row, columns):
    ids = lists_ref[...]
    workers, width = ids.shape
    tile = lax.broadcasted_iota(jnp.int32, (3 * tiles_row, width), 0)
    target = (middle - 1) * tiles_row + tile
    found = ids[0:1] == target
    for worker in range(1, workers):
        found = found | (ids[worker : worker + 1] == target)
    named = jnp.dot(
        jnp.where(found, 1.0, 0.0).astype(BF16),
        jnp.ones((width, LANES), BF16),
        preferred_element_type=F32,
    ).astype(BF16)
    first = TILE * lax.broadcasted_iota(jnp.int32, (columns, tiles_row), 1)
    cell = lax.broadcasted_iota(jnp.int32, (columns, tiles_row), 0)
    inside = jnp.where((cell >= first) & (cell < first + TILE), 1.0, 0.0).astype(BF16)
    return [
        jnp.dot(
            inside, named[k * tiles_row : (k + 1) * tiles_row], preferred_element_type=F32
        ).astype(BF16)
        for k in range(3)
    ]


def row_pairs(rate, rows):
    rows = list(rows)
    pairs = []
    for start in range(0, len(rows), 2 * rate):
        for k in range(rate):
            pairs.append((rows[start + k], rows[start + k + rate]))
    return pairs


def by_rate(rate, body):
    for value in RATES:
        pl.when(rate == value)(lambda value=value: body(value))


def clear_ends(pad_ref, count, columns):
    ends = jnp.zeros((EDGE, pad_ref.shape[-1]), F32)
    for k in range(count):
        pad_ref[k, :EDGE] = ends
        pad_ref[k, EDGE + columns :] = ends


def spread(value, pad_ref, slot, target_ref, offset):
    columns, channels = value.shape
    pad_ref[slot, EDGE : EDGE + columns] = value.astype(F32)
    target_ref[:, :channels] = pad_ref[slot, pl.ds(EDGE - offset, columns)].astype(BF16)
    target_ref[:, channels : 2 * channels] = value.astype(BF16)
    target_ref[:, 2 * channels :] = pad_ref[slot, pl.ds(EDGE + offset, columns)].astype(BF16)


def by_side(a_ref, b_ref, sides_ref):
    odd = lax.axis_index("tile") % 2

    def order(low, high):
        sides_ref[0] = low[...]
        sides_ref[1] = high[...]

    pl.when(odd == 0)(lambda: order(b_ref, a_ref))
    pl.when(odd == 1)(lambda: order(a_ref, b_ref))


def silu_grad(half_cot, half_pre):
    turn = jnp.tanh(half_pre)
    return half_cot * (1.0 + turn + half_pre * (1.0 - turn * turn))


def tap_sums(grads, xts, rate):
    flipped = jnp.concatenate(
        [
            jnp.concatenate([xts(row + rate * a) for row, _ in grads], axis=1)
            for a in (-1, 0, 1)
        ],
        axis=0,
    )
    return jnp.dot(
        flipped,
        jnp.concatenate([ref[...] for _, ref in grads], axis=0),
        preferred_element_type=F32,
    )


def pair_rows(pair, rate, rows):
    reach = [pair[0] + rate * (k - 1) for k in range(4)]
    inside = [k for k in range(4) if 0 <= reach[k] < rows]
    return [reach[k] for k in inside], inside[0], inside[-1] + 1


def input_sums(pair, rate, rows, grads, wide_ref):
    near, low, high = pair_rows(pair, rate, rows)
    lhs = jnp.concatenate([grads(row)[...] for row in near], axis=1)
    width = wide_ref.shape[0] // 4
    both = jnp.dot(lhs, wide_ref[low * width : high * width], preferred_element_type=F32)
    half = both.shape[1] // 2
    return both[:, :half], both[:, half:]


def first_kernel(
    rates_ref, lists_ref, x_hbm, cot_hbm, w_hbm, bias_ref,
    grad_ref, pre_ref, xt_ref, total_ref, mask_ref, cot_ref, back_ref, near_ref, far_ref,
    xbuf, cbuf, wbuf, pad, xcat, gcat_ref, wide, sems,
):
    rows, columns, channels = x_hbm.shape
    tiles_row = columns // TILE
    mine = lax.axis_index("tile")
    step = rows // 4
    loads = [pltpu.make_async_copy(w_hbm, wbuf, sems.at[0])]
    for source, target, base in ((x_hbm, xbuf, 1), (cot_hbm, cbuf, 5)):
        for k in range(4):
            part = pl.ds(k * step, step)
            loads.append(
                pltpu.make_async_copy(source.at[part], target.at[part], sems.at[base + k])
            )
    for load in loads:
        load.start()
    for k, value in enumerate(cell_masks(lists_ref, mine, tiles_row, columns)):
        mask_ref[k] = value
    clear_ends(pad, rows, columns)
    loads[0].wait()
    none = jnp.zeros((channels, channels), BF16)
    for col in range(3):
        there = slice(col * channels, (col + 1) * channels)
        turned = [wbuf[tap * 3 + col].T for tap in range(3)]
        for side in range(2):
            near_ref[side, there] = wbuf[6 * side + col]
            far_ref[side, there] = turned[2 - 2 * side]
        for row in range(4):
            start = (row * 3 + col) * channels
            here = slice(start, start + channels)
            for out in range(2):
                there = slice(out * channels, (out + 1) * channels)
                tap = row - out
                wide[here, there] = wbuf[tap * 3 + col] if 0 <= tap < 3 else none
                tap = out + 2 - row
                back_ref[here, there] = turned[tap] if 0 <= tap < 3 else none
    for load in loads[1:]:
        load.wait()
    half_bias = 0.5 * bias_ref[...]

    def body(rate):
        done = set()

        def prepare(row):
            if row in done:
                return
            done.add(row)
            value = xbuf[row] * mask_ref[1]
            spread(value, pad, row, xcat.at[row], rate)
            xt_ref[row] = value.T

        def convolve(pair):
            near, low, high = pair_rows(pair, rate, rows)
            for row in near:
                prepare(row)
            lhs = jnp.concatenate([xcat[row] for row in near], axis=1)
            width = wide.shape[0] // 4
            both = jnp.dot(
                lhs, wide[low * width : high * width], preferred_element_type=F32
            )
            return pair, (both[:, :channels], both[:, channels:])

        def finish(pair, sums):
            for row, value in zip(pair, sums):
                half_pre = 0.5 * value + half_bias
                half_cot = cbuf[row] * mask_ref[1] * 0.5
                if HALO <= row < rows - HALO:
                    grad = silu_grad(half_cot.astype(F32), half_pre)
                    spread(grad, pad, row, gcat_ref.at[row - HALO], -rate)
                    grad_ref[row - HALO] = grad.astype(BF16)
                    ready.append(row)
                else:
                    here = row if row < HALO else row - (rows - 2 * HALO)
                    pre_ref[here] = half_pre
                    cot_ref[here] = half_cot

        ready = []
        summed = []
        waiting = None
        for pair in row_pairs(rate, range(rows)) + [None]:
            result = convolve(pair) if pair else None
            if waiting:
                finish(*waiting)
            waiting = result
            while len(ready) >= 2:
                grads = [(row, gcat_ref.at[row - HALO]) for row in ready[:2]]
                part = tap_sums(grads, lambda row: xt_ref[row], rate)
                total_ref[...] = total_ref[...] + part if summed else part
                summed.extend(ready[:2])
                del ready[:2]

    by_rate(rates_ref[0, mine], body)


def rims_kernel(
    rates_ref, a_ref, b_ref, pre_ref, cot_ref, mask_ref, near_ref,
    grad_a_ref, grad_b_ref, xt_ref,
    pad, xcat, halo, grads,
):
    _, columns, channels = a_ref.shape
    clear_ends(pad, 2 * HALO, columns)
    by_side(a_ref, b_ref, halo)

    def body(rate):
        for side in range(2):
            used = range(HALO - rate, HALO) if side == 0 else range(rate)
            for place, k in enumerate(used):
                value = halo[side, k] * mask_ref[2 * side]
                part = pl.ds(place * columns, columns)
                spread(value, pad, side * HALO + k, xcat.at[side, part], rate)
                xt_ref[side * HALO + k] = value.T
            sums = jnp.dot(
                xcat[side, : rate * columns], near_ref[side], preferred_element_type=F32
            )
            for k in range(HALO):
                half_pre = pre_ref[side * HALO + k]
                place = k if side == 0 else k - (HALO - rate)
                if 0 <= place < rate:
                    half_pre += 0.5 * sums[place * columns : (place + 1) * columns]
                grad = silu_grad(cot_ref[side * HALO + k].astype(F32), half_pre)
                grads[side, k] = grad.astype(BF16)

    by_rate(rates_ref[0, lax.axis_index("tile")], body)
    odd = lax.axis_index("tile") % 2
    grad_a_ref[...] = grads[1 - odd]
    grad_b_ref[...] = grads[odd]


def taps_kernel(
    rates_ref, grad_a_ref, grad_b_ref, xt_own_ref, xt_halo_ref, total_ref,
    keep_ref, send_ref,
    pad, gedge_ref, flat, sides, *, scale, paired,
):
    _, columns, channels = grad_a_ref.shape
    by_side(grad_a_ref, grad_b_ref, sides)
    rows = xt_own_ref.shape[0]
    clear_ends(pad, 2 * HALO, columns)

    def flipped(row):
        if row < 0:
            return xt_halo_ref[row + HALO]
        return xt_own_ref[row] if row < rows else xt_halo_ref[row - rows + HALO]

    def body(rate):
        edges = []
        for side in range(2):
            for k in range(HALO):
                slot = side * HALO + k
                spread(sides[side, k], pad, slot, gedge_ref.at[slot], -rate)
                edges.append((k + side * (rows - HALO), gedge_ref.at[slot]))
        total = (total_ref[...] + tap_sums(edges, flipped, rate)) * scale
        for a in range(3):
            for b in range(3):
                start = (a * 3 + b) * channels
                flat[start : start + channels] = total[
                    a * channels : (a + 1) * channels, b * channels : (b + 1) * channels
                ]

    by_rate(rates_ref[0, lax.axis_index("tile")], body)
    if not paired:
        keep_ref[0] = flat[...]
        return
    parts, share, _ = keep_ref.shape
    here = lax.axis_index("dp")
    for part in range(parts):
        keep_ref[part] = flat[pl.ds((2 * part + here) * share, share)]
        send_ref[part] = flat[pl.ds((2 * part + 1 - here) * share, share)].astype(BF16)


def last_kernel(
    rates_ref, from_a_ref, from_b_ref, grad_a_ref, grad_b_ref,
    grad_ref, cot_hbm, mask_ref, back_ref, far_ref,
    out_hbm,
    cbuf, obuf, pad, gcat, spare, theirs, ours, sems,
):
    rows, columns, channels = cot_hbm.shape
    inner = rows - 2 * HALO
    mine = lax.axis_index("tile")
    last = rates_ref.shape[1] - 1
    around = 2 * HALO
    chunks = rows // around
    cots, stores = [], []
    for k in range(chunks):
        part = pl.ds(k * around, around)
        cots.append(
            pltpu.make_async_copy(cot_hbm.at[part], cbuf.at[part], sems.at[k])
        )
        stores.append(
            pltpu.make_async_copy(obuf.at[part], out_hbm.at[part], sems.at[chunks + k])
        )
    for load in cots:
        load.start()
    clear_ends(pad, rows + 2 * HALO, columns)
    by_side(from_a_ref, from_b_ref, theirs)
    by_side(grad_a_ref, grad_b_ref, ours)

    def neighbour(side):
        rate = rates_ref[0, jnp.minimum(mine + 1, last) if side else jnp.maximum(mine - 1, 0)]
        for k in range(HALO):
            part = pl.ds(k * columns, columns)
            spread(theirs[side, k], pad, rows + side * HALO + k, spare.at[side, part], -rate)
        sums = jnp.dot(spare[side], far_ref[side], preferred_element_type=F32)
        parts = [sums[k * columns : (k + 1) * columns] for k in range(HALO)]
        none = jnp.zeros((columns, channels), F32)
        one = rate == 1
        if side:
            return [jnp.where(one, none, parts[0]), jnp.where(one, parts[0], parts[1])]
        return [jnp.where(one, parts[1], parts[0]), jnp.where(one, none, parts[1])]

    def body(rate):
        done = set()

        def shifted(row):
            if row not in done:
                done.add(row)
                if row < HALO:
                    value = ours[0, row]
                elif row < rows - HALO:
                    value = grad_ref[row - HALO]
                else:
                    value = ours[1, row - (rows - HALO)]
                spread(value, pad, row, gcat.at[row], -rate)
            return gcat.at[row]

        for chunk in range(chunks):
            start = chunk * around
            results = [
                (pair, input_sums(pair, rate, rows, shifted, back_ref))
                for pair in row_pairs(rate, range(start, start + around))
            ]
            terms = {0: 0, chunks - 1: 1}
            added = neighbour(terms[chunk]) if chunk in terms else None
            cots[chunk].wait()
            for pair, sums in results:
                for row, value in zip(pair, sums):
                    value = value + cbuf[row].astype(F32)
                    if row < HALO:
                        value = value + added[row]
                    elif row >= rows - HALO:
                        value = value + added[row - (rows - HALO)]
                    obuf[row] = value.astype(BF16) * mask_ref[1]
            stores[chunk].start()

    by_rate(rates_ref[0, mine], body)
    for store in stores:
        store.wait()


def cut_kernel(x_hbm, a_ref, b_ref, sems):
    rows = x_hbm.shape[0]
    odd = lax.axis_index("tile") % 2
    copies = []
    for index, ref in enumerate((a_ref, b_ref)):
        start = (rows - HALO) * (odd if index else 1 - odd)
        for k in range(HALO):
            copies.append(
                pltpu.make_async_copy(x_hbm.at[start + k], ref.at[k], sems.at[index, k])
            )
    for copy in copies:
        copy.start()
    for copy in copies:
        copy.wait()


def add_kernel(keep_ref, other_ref, sum_ref):
    sum_ref[...] = (keep_ref[...] + other_ref[...].astype(F32)).astype(BF16)


def swap(rows_a, rows_b, axis):
    count = lax.axis_size(axis)
    results = []
    for start, rows in ((0, rows_a), (1, rows_b)):
        pairs = [(i, i + 1) for i in range(start, count - 1, 2)]
        results.append(lax.ppermute(rows, axis, pairs + [(j, i) for i, j in pairs]))
    return results


def call(kernel, name, outs, specs, scratch, aliases=None, flops=0):
    memory = {"s": pltpu.SMEM, "v": pltpu.VMEM, "h": pltpu.HBM}
    ins, results = (
        [pl.BlockSpec(memory_space=memory[letter]) for letter in part] for part in specs.split(">")
    )
    return pl.pallas_call(
        kernel,
        name=name,
        out_shape=tuple(
            pltpu.HBM(shape, dtype) if letter == "h" else jax.ShapeDtypeStruct(shape, dtype)
            for (shape, dtype), letter in zip(outs, specs.split(">")[1])
        ),
        in_specs=ins,
        out_specs=tuple(results),
        scratch_shapes=scratch,
        input_output_aliases=aliases or {},
        cost_estimate=pl.CostEstimate(flops=flops, bytes_accessed=0, transcendentals=0),
        compiler_params=pltpu.CompilerParams(vmem_limit_bytes=VMEM_LIMIT),
    )


def in_hbm(array):
    return pltpu.with_memory_space_constraint(array, pltpu.HBM)


def shards(features, cotangent, tile_mask, work_lists, dilations, conv_weight, conv_bias):
    x, cot, lists = features[0], in_hbm(cotangent[0]), in_hbm(work_lists[0])
    dilations = in_hbm(dilations)
    rows, columns, channels = x.shape
    axes = ("tile", "dp")
    devices = lax.axis_size("tile") * lax.axis_size("dp")
    weight = in_hbm(conv_weight.reshape(9, channels, channels))
    bias = in_hbm(conv_bias.reshape(1, channels))
    inner = rows - 2 * HALO
    wide_row = 3 * channels
    whole = ((rows, columns, channels), BF16)

    def pads(count):
        return pltpu.VMEM((count, columns + 2 * EDGE, channels), F32)

    rim = ((HALO, columns, channels), BF16)
    sides = pltpu.VMEM((2, HALO, columns, channels), BF16)
    rows_a, rows_b = call(
        cut_kernel,
        "cut",
        [rim, rim],
        "h>vv",
        [pltpu.SemaphoreType.DMA((2, HALO))],
    )(in_hbm(x))
    x_a, x_b = swap(rows_a, rows_b, "tile")

    grad, pre, xt, total, mask, cot_edge, back, near, far = call(
        first_kernel,
        "first",
        [
            ((inner, columns, channels), BF16),
            ((2 * HALO, columns, channels), F32),
            ((rows, channels, columns), BF16),
            ((wide_row, wide_row), F32),
            ((3, columns, channels), BF16),
            ((2 * HALO, columns, channels), BF16),
            ((4 * wide_row, 2 * channels), BF16),
            ((2, wide_row, channels), BF16),
            ((2, wide_row, channels), BF16),
        ],
        "svhhhv>vvvvvvvvv",
        [
            pltpu.VMEM((rows, columns, channels), BF16),
            pltpu.VMEM((rows, columns, channels), BF16),
            pltpu.VMEM((9, channels, channels), BF16),
            pads(rows),
            pltpu.VMEM((rows, columns, wide_row), BF16),
            pltpu.VMEM((inner, columns, wide_row), BF16),
            pltpu.VMEM((4 * wide_row, 2 * channels), BF16),
            pltpu.SemaphoreType.DMA((9,)),
        ],
        flops=BUSY,
    )(dilations, lists, in_hbm(x), cot, weight, bias)

    grad_a, grad_b, xt_halo = call(
        rims_kernel,
        "rims",
        [
            rim,
            rim,
            ((2 * HALO, channels, columns), BF16),
        ],
        "svvvvvv>vvv",
        [pads(2 * HALO), pltpu.VMEM((2, HALO * columns, wide_row), BF16), sides, sides],
    )(dilations, x_a, x_b, pre, cot_edge, mask, near)

    from_a, from_b = swap(grad_a, grad_b, "tile")

    tap_rows = 9 * channels
    cores = lax.axis_size("dp")
    paired = cores == 2 and tap_rows % devices == 0
    share = (devices // 2, tap_rows // devices) if paired else (1, tap_rows)
    scale = 1.0 / math.sqrt(devices * lists.shape[1] * TILE * TILE)
    keep, send = call(
        lambda *refs: taps_kernel(*refs, scale=scale, paired=paired),
        "taps",
        [
            (share + (channels,), F32),
            (share + (channels,), BF16),
        ],
        "svvvvv>vv",
        [
            pads(2 * HALO),
            pltpu.VMEM((2 * HALO, columns, wide_row), BF16),
            pltpu.VMEM((tap_rows, channels), F32),
            sides,
        ],
    )(dilations, grad_a, grad_b, xt, xt_halo, total)
    if paired:
        other = lax.ppermute(send, "dp", [(0, 1), (1, 0)])
        (both,) = call(add_kernel, "add", [(share + (channels,), BF16)], "vv>v", [])(keep, other)
        received = lax.all_to_all(both, "tile", 0, 0, tiled=True)
    else:
        received = lax.all_to_all(
            keep.astype(BF16).reshape(devices, -1), axes, 0, 0, tiled=True
        )

    (input_grad,) = call(
        last_kernel,
        "last",
        [whole],
        "svvvvvhvvv>h",
        [
            pltpu.VMEM((rows, columns, channels), BF16),
            pltpu.VMEM((rows, columns, channels), BF16),
            pads(rows + 2 * HALO),
            pltpu.VMEM((rows, columns, wide_row), BF16),
            pltpu.VMEM((2, HALO * columns, wide_row), BF16),
            sides,
            sides,
            pltpu.SemaphoreType.DMA((2 * (rows // (2 * HALO)),)),
        ],
        flops=BUSY,
    )(
        dilations, from_a, from_b, grad_a, grad_b,
        grad, cot, mask, back, far,
    )
    summed = jnp.sum(received.astype(F32), axis=0)
    return (input_grad[None], summed.reshape(-1))


def solution(mesh):
    placed = (
        P("dp", "tile", None, None),
        P("dp", "tile", None, None),
        P("dp", "tile", None),
        P("dp", None, None),
        P("dp", None),
        P(),
        P(),
    )
    return jax.shard_map(
        shards,
        mesh=mesh,
        in_specs=placed,
        out_specs=(P("dp", "tile", None, None), P(("tile", "dp"))),
        check_vma=False,
    )
```

```python
import math

import jax
import jax.numpy as jnp
from jax import lax
from jax.experimental import pallas as pl
from jax.experimental.pallas import tpu as pltpu
from jax.sharding import PartitionSpec as P

TILE = 12
HALO = 2
LANES = 128
EDGE = 8
RATES = (1, 2)
VMEM_LIMIT = 40 * 1024 * 1024
BUSY = 20_000_000_000

F32 = jnp.float32
BF16 = jnp.bfloat16


def cell_masks(lists_ref, middle, tiles_row, columns):
    ids = lists_ref[...]
    workers, width = ids.shape
    tile = lax.broadcasted_iota(jnp.int32, (3 * tiles_row, width), 0)
    target = (middle - 1) * tiles_row + tile
    found = ids[0:1] == target
    for worker in range(1, workers):
        found = found | (ids[worker : worker + 1] == target)
    named = jnp.dot(
        jnp.where(found, 1.0, 0.0).astype(BF16),
        jnp.ones((width, LANES), BF16),
        preferred_element_type=F32,
    ).astype(BF16)
    first = TILE * lax.broadcasted_iota(jnp.int32, (columns, tiles_row), 1)
    cell = lax.broadcasted_iota(jnp.int32, (columns, tiles_row), 0)
    inside = jnp.where((cell >= first) & (cell < first + TILE), 1.0, 0.0).astype(BF16)
    return [
        jnp.dot(
            inside, named[k * tiles_row : (k + 1) * tiles_row], preferred_element_type=F32
        ).astype(BF16)
        for k in range(3)
    ]


def row_pairs(rate, rows):
    rows = list(rows)
    pairs = []
    for start in range(0, len(rows), 2 * rate):
        for k in range(rate):
            pairs.append((rows[start + k], rows[start + k + rate]))
    return pairs


def by_rate(rate, body):
    for value in RATES:
        pl.when(rate == value)(lambda value=value: body(value))


def clear_ends(pad_ref, count, columns):
    ends = jnp.zeros((EDGE, pad_ref.shape[-1]), F32)
    for k in range(count):
        pad_ref[k, :EDGE] = ends
        pad_ref[k, EDGE + columns :] = ends


def spread(value, pad_ref, slot, target_ref, offset):
    columns, channels = value.shape
    pad_ref[slot, EDGE : EDGE + columns] = value.astype(F32)
    target_ref[:, :channels] = pad_ref[slot, pl.ds(EDGE - offset, columns)].astype(BF16)
    target_ref[:, channels : 2 * channels] = value.astype(BF16)
    target_ref[:, 2 * channels :] = pad_ref[slot, pl.ds(EDGE + offset, columns)].astype(BF16)


def by_side(a_ref, b_ref, sides_ref):
    odd = lax.axis_index("tile") % 2

    def order(low, high):
        sides_ref[0] = low[...]
        sides_ref[1] = high[...]

    pl.when(odd == 0)(lambda: order(b_ref, a_ref))
    pl.when(odd == 1)(lambda: order(a_ref, b_ref))


def silu_grad(half_cot, half_pre):
    turn = jnp.tanh(half_pre)
    return half_cot * (1.0 + turn + half_pre * (1.0 - turn * turn))


def tap_sums(grads, xts, rate):
    flipped = jnp.concatenate(
        [
            jnp.concatenate([xts(row + rate * a) for row, _ in grads], axis=1)
            for a in (-1, 0, 1)
        ],
        axis=0,
    )
    return jnp.dot(
        flipped,
        jnp.concatenate([ref[...] for _, ref in grads], axis=0),
        preferred_element_type=F32,
    )


def pair_rows(pair, rate, rows):
    reach = [pair[0] + rate * (k - 1) for k in range(4)]
    inside = [k for k in range(4) if 0 <= reach[k] < rows]
    return [reach[k] for k in inside], inside[0], inside[-1] + 1


def input_sums(pair, rate, rows, grads, wide_ref):
    near, low, high = pair_rows(pair, rate, rows)
    lhs = jnp.concatenate([grads(row)[...] for row in near], axis=1)
    width = wide_ref.shape[0] // 4
    both = jnp.dot(lhs, wide_ref[low * width : high * width], preferred_element_type=F32)
    half = both.shape[1] // 2
    return both[:, :half], both[:, half:]


def first_kernel(
    rates_ref, lists_ref, x_hbm, cot_hbm, w_hbm, bias_ref,
    grad_ref, pre_ref, xt_ref, total_ref, mask_ref, cot_ref, back_ref, near_ref, far_ref,
    xbuf, cbuf, wbuf, pad, xcat, gcat_ref, wide, sems,
):
    rows, columns, channels = x_hbm.shape
    tiles_row = columns // TILE
    mine = lax.axis_index("tile")
    step = rows // 4
    loads = [pltpu.make_async_copy(w_hbm, wbuf, sems.at[0])]
    for source, target, base in ((x_hbm, xbuf, 1), (cot_hbm, cbuf, 5)):
        for k in range(4):
            part = pl.ds(k * step, step)
            loads.append(
                pltpu.make_async_copy(source.at[part], target.at[part], sems.at[base + k])
            )
    for load in loads:
        load.start()
    for k, value in enumerate(cell_masks(lists_ref, mine, tiles_row, columns)):
        mask_ref[k] = value
    clear_ends(pad, rows, columns)
    loads[0].wait()
    none = jnp.zeros((channels, channels), BF16)
    for col in range(3):
        there = slice(col * channels, (col + 1) * channels)
        turned = [wbuf[tap * 3 + col].T for tap in range(3)]
        for side in range(2):
            near_ref[side, there] = wbuf[6 * side + col]
            far_ref[side, there] = turned[2 - 2 * side]
        for row in range(4):
            start = (row * 3 + col) * channels
            here = slice(start, start + channels)
            for out in range(2):
                there = slice(out * channels, (out + 1) * channels)
                tap = row - out
                wide[here, there] = wbuf[tap * 3 + col] if 0 <= tap < 3 else none
                tap = out + 2 - row
                back_ref[here, there] = turned[tap] if 0 <= tap < 3 else none
    for load in loads[1:]:
        load.wait()
    half_bias = 0.5 * bias_ref[...]

    def body(rate):
        done = set()

        def prepare(row):
            if row in done:
                return
            done.add(row)
            value = xbuf[row] * mask_ref[1]
            spread(value, pad, row, xcat.at[row], rate)
            xt_ref[row] = value.T

        def convolve(pair):
            near, low, high = pair_rows(pair, rate, rows)
            for row in near:
                prepare(row)
            lhs = jnp.concatenate([xcat[row] for row in near], axis=1)
            width = wide.shape[0] // 4
            both = jnp.dot(
                lhs, wide[low * width : high * width], preferred_element_type=F32
            )
            return pair, (both[:, :channels], both[:, channels:])

        def finish(pair, sums):
            for row, value in zip(pair, sums):
                half_pre = 0.5 * value + half_bias
                half_cot = cbuf[row] * mask_ref[1] * 0.5
                if HALO <= row < rows - HALO:
                    grad = silu_grad(half_cot.astype(F32), half_pre)
                    spread(grad, pad, row, gcat_ref.at[row - HALO], -rate)
                    grad_ref[row - HALO] = grad.astype(BF16)
                    ready.append(row)
                else:
                    here = row if row < HALO else row - (rows - 2 * HALO)
                    pre_ref[here] = half_pre
                    cot_ref[here] = half_cot

        ready = []
        summed = []
        waiting = None
        for pair in row_pairs(rate, range(rows)) + [None]:
            result = convolve(pair) if pair else None
            if waiting:
                finish(*waiting)
            waiting = result
            while len(ready) >= 2:
                grads = [(row, gcat_ref.at[row - HALO]) for row in ready[:2]]
                part = tap_sums(grads, lambda row: xt_ref[row], rate)
                total_ref[...] = total_ref[...] + part if summed else part
                summed.extend(ready[:2])
                del ready[:2]

    by_rate(rates_ref[0, mine], body)


def rims_kernel(
    rates_ref, a_ref, b_ref, pre_ref, cot_ref, mask_ref, near_ref, xt_own_ref, total_ref,
    grad_a_ref, grad_b_ref, keep_ref, send_ref,
    pad, xcat, halo, grads, xt_halo, gedge, flat, *, scale, paired,
):
    _, columns, channels = a_ref.shape
    rows = xt_own_ref.shape[0]
    clear_ends(pad, 4 * HALO, columns)
    by_side(a_ref, b_ref, halo)

    def flipped(row):
        if row < 0:
            return xt_halo[row + HALO]
        return xt_own_ref[row] if row < rows else xt_halo[row - rows + HALO]

    def body(rate):
        halves = []
        for side in range(2):
            used = range(HALO - rate, HALO) if side == 0 else range(rate)
            for place, k in enumerate(used):
                value = halo[side, k] * mask_ref[2 * side]
                part = pl.ds(place * columns, columns)
                spread(value, pad, side * HALO + k, xcat.at[side, part], rate)
                xt_halo[side * HALO + k] = value.T
            halves.append(
                jnp.dot(xcat[side, : rate * columns], near_ref[side], preferred_element_type=F32)
            )
        total = total_ref[...]
        for side, sums in enumerate(halves):
            edges = []
            for k in range(HALO):
                slot = side * HALO + k
                half_pre = pre_ref[slot]
                place = k if side == 0 else k - (HALO - rate)
                if 0 <= place < rate:
                    half_pre += 0.5 * sums[place * columns : (place + 1) * columns]
                grad = silu_grad(cot_ref[slot].astype(F32), half_pre)
                grads[side, k] = grad.astype(BF16)
                spread(grad, pad, 2 * HALO + slot, gedge.at[slot], -rate)
                edges.append((k + side * (rows - HALO), gedge.at[slot]))
            total = total + tap_sums(edges, flipped, rate)
        total = total * scale
        for a in range(3):
            for b in range(3):
                start = (a * 3 + b) * channels
                flat[start : start + channels] = total[
                    a * channels : (a + 1) * channels, b * channels : (b + 1) * channels
                ]

    by_rate(rates_ref[0, lax.axis_index("tile")], body)
    odd = lax.axis_index("tile") % 2
    grad_a_ref[...] = grads[1 - odd]
    grad_b_ref[...] = grads[odd]
    if not paired:
        keep_ref[0] = flat[...]
        return
    parts, share, _ = keep_ref.shape
    here = lax.axis_index("dp")
    for part in range(parts):
        keep_ref[part] = flat[pl.ds((2 * part + here) * share, share)]
        send_ref[part] = flat[pl.ds((2 * part + 1 - here) * share, share)].astype(BF16)


def last_kernel(
    rates_ref, from_a_ref, from_b_ref, grad_a_ref, grad_b_ref,
    grad_ref, cot_hbm, mask_ref, back_ref, far_ref,
    out_hbm,
    cbuf, obuf, pad, gcat, spare, theirs, ours, sems,
):
    rows, columns, channels = cot_hbm.shape
    inner = rows - 2 * HALO
    mine = lax.axis_index("tile")
    last = rates_ref.shape[1] - 1
    around = 2 * HALO
    chunks = rows // around
    cots, stores = [], []
    for k in range(chunks):
        part = pl.ds(k * around, around)
        cots.append(
            pltpu.make_async_copy(cot_hbm.at[part], cbuf.at[part], sems.at[k])
        )
        stores.append(
            pltpu.make_async_copy(obuf.at[part], out_hbm.at[part], sems.at[chunks + k])
        )
    for load in cots:
        load.start()
    clear_ends(pad, rows + 2 * HALO, columns)
    by_side(from_a_ref, from_b_ref, theirs)
    by_side(grad_a_ref, grad_b_ref, ours)

    def neighbour(side):
        rate = rates_ref[0, jnp.minimum(mine + 1, last) if side else jnp.maximum(mine - 1, 0)]
        for k in range(HALO):
            part = pl.ds(k * columns, columns)
            spread(theirs[side, k], pad, rows + side * HALO + k, spare.at[side, part], -rate)
        sums = jnp.dot(spare[side], far_ref[side], preferred_element_type=F32)
        parts = [sums[k * columns : (k + 1) * columns] for k in range(HALO)]
        none = jnp.zeros((columns, channels), F32)
        one = rate == 1
        if side:
            return [jnp.where(one, none, parts[0]), jnp.where(one, parts[0], parts[1])]
        return [jnp.where(one, parts[1], parts[0]), jnp.where(one, none, parts[1])]

    def body(rate):
        done = set()

        def shifted(row):
            if row not in done:
                done.add(row)
                if row < HALO:
                    value = ours[0, row]
                elif row < rows - HALO:
                    value = grad_ref[row - HALO]
                else:
                    value = ours[1, row - (rows - HALO)]
                spread(value, pad, row, gcat.at[row], -rate)
            return gcat.at[row]

        for chunk in range(chunks):
            start = chunk * around
            results = [
                (pair, input_sums(pair, rate, rows, shifted, back_ref))
                for pair in row_pairs(rate, range(start, start + around))
            ]
            terms = {0: 0, chunks - 1: 1}
            added = neighbour(terms[chunk]) if chunk in terms else None
            cots[chunk].wait()
            for pair, sums in results:
                for row, value in zip(pair, sums):
                    value = value + cbuf[row].astype(F32)
                    if row < HALO:
                        value = value + added[row]
                    elif row >= rows - HALO:
                        value = value + added[row - (rows - HALO)]
                    obuf[row] = value.astype(BF16) * mask_ref[1]
            stores[chunk].start()

    by_rate(rates_ref[0, mine], body)
    for store in stores:
        store.wait()


def cut_kernel(x_hbm, a_ref, b_ref, sems):
    rows = x_hbm.shape[0]
    odd = lax.axis_index("tile") % 2
    copies = []
    for index, ref in enumerate((a_ref, b_ref)):
        start = (rows - HALO) * (odd if index else 1 - odd)
        for k in range(HALO):
            copies.append(
                pltpu.make_async_copy(x_hbm.at[start + k], ref.at[k], sems.at[index, k])
            )
    for copy in copies:
        copy.start()
    for copy in copies:
        copy.wait()


def swap(rows_a, rows_b, axis):
    count = lax.axis_size(axis)
    results = []
    for start, rows in ((0, rows_a), (1, rows_b)):
        pairs = [(i, i + 1) for i in range(start, count - 1, 2)]
        results.append(lax.ppermute(rows, axis, pairs + [(j, i) for i, j in pairs]))
    return results


def call(kernel, name, outs, specs, scratch, aliases=None, flops=0):
    memory = {"s": pltpu.SMEM, "v": pltpu.VMEM, "h": pltpu.HBM}
    ins, results = (
        [pl.BlockSpec(memory_space=memory[letter]) for letter in part] for part in specs.split(">")
    )
    return pl.pallas_call(
        kernel,
        name=name,
        out_shape=tuple(
            pltpu.HBM(shape, dtype) if letter == "h" else jax.ShapeDtypeStruct(shape, dtype)
            for (shape, dtype), letter in zip(outs, specs.split(">")[1])
        ),
        in_specs=ins,
        out_specs=tuple(results),
        scratch_shapes=scratch,
        input_output_aliases=aliases or {},
        cost_estimate=pl.CostEstimate(flops=flops, bytes_accessed=0, transcendentals=0),
        compiler_params=pltpu.CompilerParams(vmem_limit_bytes=VMEM_LIMIT),
    )


def in_hbm(array):
    return pltpu.with_memory_space_constraint(array, pltpu.HBM)


def shards(features, cotangent, tile_mask, work_lists, dilations, conv_weight, conv_bias):
    x, cot, lists = features[0], in_hbm(cotangent[0]), in_hbm(work_lists[0])
    dilations = in_hbm(dilations)
    rows, columns, channels = x.shape
    axes = ("tile", "dp")
    devices = lax.axis_size("tile") * lax.axis_size("dp")
    weight = in_hbm(conv_weight.reshape(9, channels, channels))
    bias = in_hbm(conv_bias.reshape(1, channels))
    inner = rows - 2 * HALO
    wide_row = 3 * channels
    whole = ((rows, columns, channels), BF16)

    def pads(count):
        return pltpu.VMEM((count, columns + 2 * EDGE, channels), F32)

    rim = ((HALO, columns, channels), BF16)
    sides = pltpu.VMEM((2, HALO, columns, channels), BF16)
    rows_a, rows_b = call(
        cut_kernel,
        "cut",
        [rim, rim],
        "h>vv",
        [pltpu.SemaphoreType.DMA((2, HALO))],
    )(in_hbm(x))
    x_a, x_b = swap(rows_a, rows_b, "tile")

    grad, pre, xt, total, mask, cot_edge, back, near, far = call(
        first_kernel,
        "first",
        [
            ((inner, columns, channels), BF16),
            ((2 * HALO, columns, channels), F32),
            ((rows, channels, columns), BF16),
            ((wide_row, wide_row), F32),
            ((3, columns, channels), BF16),
            ((2 * HALO, columns, channels), BF16),
            ((4 * wide_row, 2 * channels), BF16),
            ((2, wide_row, channels), BF16),
            ((2, wide_row, channels), BF16),
        ],
        "svhhhv>vvvvvvvvv",
        [
            pltpu.VMEM((rows, columns, channels), BF16),
            pltpu.VMEM((rows, columns, channels), BF16),
            pltpu.VMEM((9, channels, channels), BF16),
            pads(rows),
            pltpu.VMEM((rows, columns, wide_row), BF16),
            pltpu.VMEM((inner, columns, wide_row), BF16),
            pltpu.VMEM((4 * wide_row, 2 * channels), BF16),
            pltpu.SemaphoreType.DMA((9,)),
        ],
        flops=BUSY,
    )(dilations, lists, in_hbm(x), cot, weight, bias)

    tap_rows = 9 * channels
    cores = lax.axis_size("dp")
    paired = cores == 2 and tap_rows % devices == 0
    share = (devices // 2, tap_rows // devices) if paired else (1, tap_rows)
    scale = 1.0 / math.sqrt(devices * lists.shape[1] * TILE * TILE)
    grad_a, grad_b, keep, send = call(
        lambda *refs: rims_kernel(*refs, scale=scale, paired=paired),
        "rims",
        [rim, rim, (share + (channels,), F32), (share + (channels,), BF16)],
        "svvvvvvvv>vvvv",
        [
            pads(4 * HALO),
            pltpu.VMEM((2, HALO * columns, wide_row), BF16),
            sides,
            sides,
            pltpu.VMEM((2 * HALO, channels, columns), BF16),
            pltpu.VMEM((2 * HALO, columns, wide_row), BF16),
            pltpu.VMEM((tap_rows, channels), F32),
        ],
    )(dilations, x_a, x_b, pre, cot_edge, mask, near, xt, total)

    from_a, from_b = swap(grad_a, grad_b, "tile")
    if paired:
        other = lax.ppermute(send, "dp", [(0, 1), (1, 0)])
        both = (keep + other.astype(F32)).astype(BF16)
        received = lax.all_to_all(both, "tile", 0, 0, tiled=True)
    else:
        received = lax.all_to_all(
            keep.astype(BF16).reshape(devices, -1), axes, 0, 0, tiled=True
        )

    (input_grad,) = call(
        last_kernel,
        "last",
        [whole],
        "svvvvvhvvv>h",
        [
            pltpu.VMEM((rows, columns, channels), BF16),
            pltpu.VMEM((rows, columns, channels), BF16),
            pads(rows + 2 * HALO),
            pltpu.VMEM((rows, columns, wide_row), BF16),
            pltpu.VMEM((2, HALO * columns, wide_row), BF16),
            sides,
            sides,
            pltpu.SemaphoreType.DMA((2 * (rows // (2 * HALO)),)),
        ],
        flops=BUSY,
    )(
        dilations, from_a, from_b, grad_a, grad_b,
        grad, cot, mask, back, far,
    )
    summed = jnp.sum(received.astype(F32), axis=0)
    return (input_grad[None], summed.reshape(-1))


def solution(mesh):
    placed = (
        P("dp", "tile", None, None),
        P("dp", "tile", None, None),
        P("dp", "tile", None),
        P("dp", None, None),
        P("dp", None),
        P(),
        P(),
    )
    return jax.shard_map(
        shards,
        mesh=mesh,
        in_specs=placed,
        out_specs=(P("dp", "tile", None, None), P(("tile", "dp"))),
        check_vma=False,
    )
```

```python
import math

import jax
import jax.numpy as jnp
from jax import lax
from jax.experimental import pallas as pl
from jax.experimental.pallas import tpu as pltpu
from jax.sharding import PartitionSpec as P

TILE = 12
HALO = 2
LANES = 128
EDGE = 8
RATES = (1, 2)
VMEM_LIMIT = 40 * 1024 * 1024
BUSY = 20_000_000_000

F32 = jnp.float32
BF16 = jnp.bfloat16


def cell_masks(lists_ref, middle, tiles_row, columns):
    ids = lists_ref[...]
    workers, width = ids.shape
    tile = lax.broadcasted_iota(jnp.int32, (3 * tiles_row, width), 0)
    target = (middle - 1) * tiles_row + tile
    found = ids[0:1] == target
    for worker in range(1, workers):
        found = found | (ids[worker : worker + 1] == target)
    named = jnp.dot(
        jnp.where(found, 1.0, 0.0).astype(BF16),
        jnp.ones((width, LANES), BF16),
        preferred_element_type=F32,
    ).astype(BF16)
    first = TILE * lax.broadcasted_iota(jnp.int32, (columns, tiles_row), 1)
    cell = lax.broadcasted_iota(jnp.int32, (columns, tiles_row), 0)
    inside = jnp.where((cell >= first) & (cell < first + TILE), 1.0, 0.0).astype(BF16)
    return [
        jnp.dot(
            inside, named[k * tiles_row : (k + 1) * tiles_row], preferred_element_type=F32
        ).astype(BF16)
        for k in range(3)
    ]


def row_pairs(rate, rows):
    rows = list(rows)
    pairs = []
    for start in range(0, len(rows), 2 * rate):
        for k in range(rate):
            pairs.append((rows[start + k], rows[start + k + rate]))
    return pairs


def by_rate(rate, body):
    for value in RATES:
        pl.when(rate == value)(lambda value=value: body(value))


def clear_ends(pad_ref, count, columns):
    ends = jnp.zeros((EDGE, pad_ref.shape[-1]), F32)
    for k in range(count):
        pad_ref[k, :EDGE] = ends
        pad_ref[k, EDGE + columns :] = ends


def spread(value, pad_ref, slot, target_ref, offset):
    columns, channels = value.shape
    pad_ref[slot, EDGE : EDGE + columns] = value.astype(F32)
    target_ref[:, :channels] = pad_ref[slot, pl.ds(EDGE - offset, columns)].astype(BF16)
    target_ref[:, channels : 2 * channels] = value.astype(BF16)
    target_ref[:, 2 * channels :] = pad_ref[slot, pl.ds(EDGE + offset, columns)].astype(BF16)


def by_side(a_ref, b_ref, sides_ref):
    odd = lax.axis_index("tile") % 2

    def order(low, high):
        sides_ref[0] = low[...]
        sides_ref[1] = high[...]

    pl.when(odd == 0)(lambda: order(b_ref, a_ref))
    pl.when(odd == 1)(lambda: order(a_ref, b_ref))


def silu_grad(half_cot, half_pre):
    turn = jnp.tanh(half_pre)
    return half_cot * (1.0 + turn + half_pre * (1.0 - turn * turn))


def tap_sums(grads, xts, rate):
    flipped = jnp.concatenate(
        [
            jnp.concatenate([xts(row + rate * a) for row, _ in grads], axis=1)
            for a in (-1, 0, 1)
        ],
        axis=0,
    )
    return jnp.dot(
        flipped,
        jnp.concatenate([ref[...] for _, ref in grads], axis=0),
        preferred_element_type=F32,
    )


def pair_rows(pair, rate, rows):
    reach = [pair[0] + rate * (k - 1) for k in range(4)]
    inside = [k for k in range(4) if 0 <= reach[k] < rows]
    return [reach[k] for k in inside], inside[0], inside[-1] + 1


def input_sums(pair, rate, rows, grads, wide_ref):
    near, low, high = pair_rows(pair, rate, rows)
    lhs = jnp.concatenate([grads(row)[...] for row in near], axis=1)
    width = wide_ref.shape[0] // 4
    both = jnp.dot(lhs, wide_ref[low * width : high * width], preferred_element_type=F32)
    half = both.shape[1] // 2
    return both[:, :half], both[:, half:]


def first_kernel(
    rates_hbm, lists_hbm, x_hbm, cot_hbm, w_hbm, bias_hbm,
    near_rates_ref, grad_ref, pre_ref, xt_ref, total_ref, mask_ref, cot_ref, back_ref, near_ref, far_ref,
    rates_ref, lists_ref, bias_ref, xbuf, cbuf, wbuf, pad, xcat, gcat_ref, wide, sems,
):
    rows, columns, channels = x_hbm.shape
    tiles_row = columns // TILE
    mine = lax.axis_index("tile")
    step = rows // 4
    loads = [pltpu.make_async_copy(w_hbm, wbuf, sems.at[0])]
    for source, target, base in ((x_hbm, xbuf, 1), (cot_hbm, cbuf, 5)):
        for k in range(4):
            part = pl.ds(k * step, step)
            loads.append(
                pltpu.make_async_copy(source.at[part], target.at[part], sems.at[base + k])
            )
    small = [
        pltpu.make_async_copy(source, target, sems.at[9 + k])
        for k, (source, target) in enumerate(
            ((lists_hbm, lists_ref), (rates_hbm, rates_ref), (bias_hbm, bias_ref))
        )
    ]
    for load in small + loads:
        load.start()
    for load in small:
        load.wait()
    last = rates_ref.shape[1] - 1
    for k in range(3):
        row = jnp.clip(mine + k - 1, 0, last)
        near_rates_ref[k] = jnp.full(near_rates_ref.shape[1:], rates_ref[0, row], jnp.int32)
    for k, value in enumerate(cell_masks(lists_ref, mine, tiles_row, columns)):
        mask_ref[k] = value
    clear_ends(pad, rows, columns)
    loads[0].wait()
    none = jnp.zeros((channels, channels), BF16)
    for col in range(3):
        there = slice(col * channels, (col + 1) * channels)
        turned = [wbuf[tap * 3 + col].T for tap in range(3)]
        for side in range(2):
            near_ref[side, there] = wbuf[6 * side + col]
            far_ref[side, there] = turned[2 - 2 * side]
        for row in range(4):
            start = (row * 3 + col) * channels
            here = slice(start, start + channels)
            for out in range(2):
                there = slice(out * channels, (out + 1) * channels)
                tap = row - out
                wide[here, there] = wbuf[tap * 3 + col] if 0 <= tap < 3 else none
                tap = out + 2 - row
                back_ref[here, there] = turned[tap] if 0 <= tap < 3 else none
    for load in loads[1:]:
        load.wait()
    half_bias = 0.5 * bias_ref[...]

    def body(rate):
        done = set()

        def prepare(row):
            if row in done:
                return
            done.add(row)
            value = xbuf[row] * mask_ref[1]
            spread(value, pad, row, xcat.at[row], rate)
            xt_ref[row] = value.T

        def convolve(pair):
            near, low, high = pair_rows(pair, rate, rows)
            for row in near:
                prepare(row)
            lhs = jnp.concatenate([xcat[row] for row in near], axis=1)
            width = wide.shape[0] // 4
            both = jnp.dot(
                lhs, wide[low * width : high * width], preferred_element_type=F32
            )
            return pair, (both[:, :channels], both[:, channels:])

        def finish(pair, sums):
            for row, value in zip(pair, sums):
                half_pre = 0.5 * value + half_bias
                half_cot = cbuf[row] * mask_ref[1] * 0.5
                if HALO <= row < rows - HALO:
                    grad = silu_grad(half_cot.astype(F32), half_pre)
                    spread(grad, pad, row, gcat_ref.at[row - HALO], -rate)
                    grad_ref[row - HALO] = grad.astype(BF16)
                    ready.append(row)
                else:
                    here = row if row < HALO else row - (rows - 2 * HALO)
                    pre_ref[here] = half_pre
                    cot_ref[here] = half_cot

        ready = []
        summed = []
        waiting = None
        for pair in row_pairs(rate, range(rows)) + [None]:
            result = convolve(pair) if pair else None
            if waiting:
                finish(*waiting)
            waiting = result
            while len(ready) >= 2:
                grads = [(row, gcat_ref.at[row - HALO]) for row in ready[:2]]
                part = tap_sums(grads, lambda row: xt_ref[row], rate)
                total_ref[...] = total_ref[...] + part if summed else part
                summed.extend(ready[:2])
                del ready[:2]

    by_rate(rates_ref[0, mine], body)


def rims_kernel(
    rates_ref, a_ref, b_ref, pre_ref, cot_ref, mask_ref, near_ref, xt_own_ref, total_ref,
    grad_a_ref, grad_b_ref, keep_ref, send_ref,
    pad, xcat, halo, grads, xt_halo, gedge, flat, *, scale, paired,
):
    _, columns, channels = a_ref.shape
    rows = xt_own_ref.shape[0]
    clear_ends(pad, 4 * HALO, columns)
    by_side(a_ref, b_ref, halo)

    def flipped(row):
        if row < 0:
            return xt_halo[row + HALO]
        return xt_own_ref[row] if row < rows else xt_halo[row - rows + HALO]

    def body(rate):
        halves = []
        for side in range(2):
            used = range(HALO - rate, HALO) if side == 0 else range(rate)
            for place, k in enumerate(used):
                value = halo[side, k] * mask_ref[2 * side]
                part = pl.ds(place * columns, columns)
                spread(value, pad, side * HALO + k, xcat.at[side, part], rate)
                xt_halo[side * HALO + k] = value.T
            halves.append(
                jnp.dot(xcat[side, : rate * columns], near_ref[side], preferred_element_type=F32)
            )
        total = total_ref[...]
        for side, sums in enumerate(halves):
            edges = []
            for k in range(HALO):
                slot = side * HALO + k
                half_pre = pre_ref[slot]
                place = k if side == 0 else k - (HALO - rate)
                if 0 <= place < rate:
                    half_pre += 0.5 * sums[place * columns : (place + 1) * columns]
                grad = silu_grad(cot_ref[slot].astype(F32), half_pre)
                grads[side, k] = grad.astype(BF16)
                spread(grad, pad, 2 * HALO + slot, gedge.at[slot], -rate)
                edges.append((k + side * (rows - HALO), gedge.at[slot]))
            total = total + tap_sums(edges, flipped, rate)
        total = total * scale
        for a in range(3):
            for b in range(3):
                start = (a * 3 + b) * channels
                flat[start : start + channels] = total[
                    a * channels : (a + 1) * channels, b * channels : (b + 1) * channels
                ]

    by_rate(rates_ref[1, 0, 0], body)
    odd = lax.axis_index("tile") % 2
    grad_a_ref[...] = grads[1 - odd]
    grad_b_ref[...] = grads[odd]
    if not paired:
        keep_ref[0] = flat[...]
        return
    parts, share, _ = keep_ref.shape
    here = lax.axis_index("dp")
    for part in range(parts):
        keep_ref[part] = flat[pl.ds((2 * part + here) * share, share)]
        send_ref[part] = flat[pl.ds((2 * part + 1 - here) * share, share)].astype(BF16)


def last_kernel(
    rates_ref, from_a_ref, from_b_ref, grad_a_ref, grad_b_ref,
    grad_ref, cot_hbm, mask_ref, back_ref, far_ref,
    out_hbm,
    cbuf, obuf, pad, gcat, spare, theirs, ours, sems,
):
    rows, columns, channels = cot_hbm.shape
    inner = rows - 2 * HALO
    around = 2 * HALO
    chunks = rows // around
    cots, stores = [], []
    for k in range(chunks):
        part = pl.ds(k * around, around)
        cots.append(
            pltpu.make_async_copy(cot_hbm.at[part], cbuf.at[part], sems.at[k])
        )
        stores.append(
            pltpu.make_async_copy(obuf.at[part], out_hbm.at[part], sems.at[chunks + k])
        )
    for load in cots:
        load.start()
    clear_ends(pad, rows + 2 * HALO, columns)
    by_side(from_a_ref, from_b_ref, theirs)
    by_side(grad_a_ref, grad_b_ref, ours)

    def neighbour(side):
        rate = rates_ref[2 * side, 0, 0]
        for k in range(HALO):
            part = pl.ds(k * columns, columns)
            spread(theirs[side, k], pad, rows + side * HALO + k, spare.at[side, part], -rate)
        sums = jnp.dot(spare[side], far_ref[side], preferred_element_type=F32)
        parts = [sums[k * columns : (k + 1) * columns] for k in range(HALO)]
        none = jnp.zeros((columns, channels), F32)
        one = rate == 1
        if side:
            return [jnp.where(one, none, parts[0]), jnp.where(one, parts[0], parts[1])]
        return [jnp.where(one, parts[1], parts[0]), jnp.where(one, none, parts[1])]

    def body(rate):
        done = set()

        def shifted(row):
            if row not in done:
                done.add(row)
                if row < HALO:
                    value = ours[0, row]
                elif row < rows - HALO:
                    value = grad_ref[row - HALO]
                else:
                    value = ours[1, row - (rows - HALO)]
                spread(value, pad, row, gcat.at[row], -rate)
            return gcat.at[row]

        for chunk in range(chunks):
            start = chunk * around
            results = [
                (pair, input_sums(pair, rate, rows, shifted, back_ref))
                for pair in row_pairs(rate, range(start, start + around))
            ]
            terms = {0: 0, chunks - 1: 1}
            added = neighbour(terms[chunk]) if chunk in terms else None
            cots[chunk].wait()
            for pair, sums in results:
                for row, value in zip(pair, sums):
                    value = value + cbuf[row].astype(F32)
                    if row < HALO:
                        value = value + added[row]
                    elif row >= rows - HALO:
                        value = value + added[row - (rows - HALO)]
                    obuf[row] = value.astype(BF16) * mask_ref[1]
            stores[chunk].start()

    by_rate(rates_ref[1, 0, 0], body)
    for store in stores:
        store.wait()


def cut_kernel(x_hbm, a_ref, b_ref, sems):
    rows = x_hbm.shape[0]
    odd = lax.axis_index("tile") % 2
    copies = []
    for index, ref in enumerate((a_ref, b_ref)):
        start = (rows - HALO) * (odd if index else 1 - odd)
        for k in range(HALO):
            copies.append(
                pltpu.make_async_copy(x_hbm.at[start + k], ref.at[k], sems.at[index, k])
            )
    for copy in copies:
        copy.start()
    for copy in copies:
        copy.wait()


def swap(rows_a, rows_b, axis):
    count = lax.axis_size(axis)
    results = []
    for start, rows in ((0, rows_a), (1, rows_b)):
        pairs = [(i, i + 1) for i in range(start, count - 1, 2)]
        results.append(lax.ppermute(rows, axis, pairs + [(j, i) for i, j in pairs]))
    return results


def call(kernel, name, outs, specs, scratch, aliases=None, flops=0):
    memory = {"s": pltpu.SMEM, "v": pltpu.VMEM, "h": pltpu.HBM}
    ins, results = (
        [pl.BlockSpec(memory_space=memory[letter]) for letter in part] for part in specs.split(">")
    )
    return pl.pallas_call(
        kernel,
        name=name,
        out_shape=tuple(
            pltpu.HBM(shape, dtype) if letter == "h" else jax.ShapeDtypeStruct(shape, dtype)
            for (shape, dtype), letter in zip(outs, specs.split(">")[1])
        ),
        in_specs=ins,
        out_specs=tuple(results),
        scratch_shapes=scratch,
        input_output_aliases=aliases or {},
        cost_estimate=pl.CostEstimate(flops=flops, bytes_accessed=0, transcendentals=0),
        compiler_params=pltpu.CompilerParams(vmem_limit_bytes=VMEM_LIMIT),
    )


def in_hbm(array):
    return pltpu.with_memory_space_constraint(array, pltpu.HBM)


def shards(features, cotangent, tile_mask, work_lists, dilations, conv_weight, conv_bias):
    x, cot, lists = features[0], in_hbm(cotangent[0]), in_hbm(work_lists[0])
    dilations = in_hbm(dilations)
    rows, columns, channels = x.shape
    axes = ("tile", "dp")
    devices = lax.axis_size("tile") * lax.axis_size("dp")
    weight = in_hbm(conv_weight.reshape(9, channels, channels))
    bias = in_hbm(conv_bias.reshape(1, channels))
    inner = rows - 2 * HALO
    wide_row = 3 * channels
    whole = ((rows, columns, channels), BF16)

    def pads(count):
        return pltpu.VMEM((count, columns + 2 * EDGE, channels), F32)

    rim = ((HALO, columns, channels), BF16)
    sides = pltpu.VMEM((2, HALO, columns, channels), BF16)
    rows_a, rows_b = call(
        cut_kernel,
        "cut",
        [rim, rim],
        "h>vv",
        [pltpu.SemaphoreType.DMA((2, HALO))],
    )(in_hbm(x))
    x_a, x_b = swap(rows_a, rows_b, "tile")

    rates, grad, pre, xt, total, mask, cot_edge, back, near, far = call(
        first_kernel,
        "first",
        [
            ((3, 8, LANES), jnp.int32),
            ((inner, columns, channels), BF16),
            ((2 * HALO, columns, channels), F32),
            ((rows, channels, columns), BF16),
            ((wide_row, wide_row), F32),
            ((3, columns, channels), BF16),
            ((2 * HALO, columns, channels), BF16),
            ((4 * wide_row, 2 * channels), BF16),
            ((2, wide_row, channels), BF16),
            ((2, wide_row, channels), BF16),
        ],
        "hhhhhh>vvvvvvvvvv",
        [
            pltpu.SMEM(dilations.shape, jnp.int32),
            pltpu.VMEM(lists.shape, jnp.int32),
            pltpu.VMEM(bias.shape, F32),
            pltpu.VMEM((rows, columns, channels), BF16),
            pltpu.VMEM((rows, columns, channels), BF16),
            pltpu.VMEM((9, channels, channels), BF16),
            pads(rows),
            pltpu.VMEM((rows, columns, wide_row), BF16),
            pltpu.VMEM((inner, columns, wide_row), BF16),
            pltpu.VMEM((4 * wide_row, 2 * channels), BF16),
            pltpu.SemaphoreType.DMA((12,)),
        ],
        flops=BUSY,
    )(dilations, lists, in_hbm(x), cot, weight, bias)

    tap_rows = 9 * channels
    cores = lax.axis_size("dp")
    paired = cores == 2 and tap_rows % devices == 0
    share = (devices // 2, tap_rows // devices) if paired else (1, tap_rows)
    scale = 1.0 / math.sqrt(devices * lists.shape[1] * TILE * TILE)
    grad_a, grad_b, keep, send = call(
        lambda *refs: rims_kernel(*refs, scale=scale, paired=paired),
        "rims",
        [rim, rim, (share + (channels,), F32), (share + (channels,), BF16)],
        "vvvvvvvvv>vvvv",
        [
            pads(4 * HALO),
            pltpu.VMEM((2, HALO * columns, wide_row), BF16),
            sides,
            sides,
            pltpu.VMEM((2 * HALO, channels, columns), BF16),
            pltpu.VMEM((2 * HALO, columns, wide_row), BF16),
            pltpu.VMEM((tap_rows, channels), F32),
        ],
    )(rates, x_a, x_b, pre, cot_edge, mask, near, xt, total)

    from_a, from_b = swap(grad_a, grad_b, "tile")
    if paired:
        other = lax.ppermute(send, "dp", [(0, 1), (1, 0)])
        both = (keep + other.astype(F32)).astype(BF16)
        received = lax.all_to_all(both, "tile", 0, 0, tiled=True)
    else:
        received = lax.all_to_all(
            keep.astype(BF16).reshape(devices, -1), axes, 0, 0, tiled=True
        )

    (input_grad,) = call(
        last_kernel,
        "last",
        [whole],
        "vvvvvvhvvv>h",
        [
            pltpu.VMEM((rows, columns, channels), BF16),
            pltpu.VMEM((rows, columns, channels), BF16),
            pads(rows + 2 * HALO),
            pltpu.VMEM((rows, columns, wide_row), BF16),
            pltpu.VMEM((2, HALO * columns, wide_row), BF16),
            sides,
            sides,
            pltpu.SemaphoreType.DMA((2 * (rows // (2 * HALO)),)),
        ],
        flops=BUSY,
    )(
        rates, from_a, from_b, grad_a, grad_b,
        grad, cot, mask, back, far,
    )
    summed = jnp.sum(received.astype(F32), axis=0)
    return (input_grad[None], summed.reshape(-1))


def solution(mesh):
    placed = (
        P("dp", "tile", None, None),
        P("dp", "tile", None, None),
        P("dp", "tile", None),
        P("dp", None, None),
        P("dp", None),
        P(),
        P(),
    )
    return jax.shard_map(
        shards,
        mesh=mesh,
        in_specs=placed,
        out_specs=(P("dp", "tile", None, None), P(("tile", "dp"))),
        check_vma=False,
    )
```

```python
import math

import jax
import jax.numpy as jnp
from jax import lax
from jax.experimental import pallas as pl
from jax.experimental.pallas import tpu as pltpu
from jax.sharding import PartitionSpec as P

TILE = 12
HALO = 2
LANES = 128
EDGE = 8
RATES = (1, 2)
VMEM_LIMIT = 40 * 1024 * 1024
BUSY = 20_000_000_000

F32 = jnp.float32
BF16 = jnp.bfloat16


def cell_masks(lists_ref, middle, tiles_row, columns):
    ids = lists_ref[...]
    workers, width = ids.shape
    tile = lax.broadcasted_iota(jnp.int32, (3 * tiles_row, width), 0)
    target = (middle - 1) * tiles_row + tile
    found = ids[0:1] == target
    for worker in range(1, workers):
        found = found | (ids[worker : worker + 1] == target)
    named = jnp.dot(
        jnp.where(found, 1.0, 0.0).astype(BF16),
        jnp.ones((width, LANES), BF16),
        preferred_element_type=F32,
    ).astype(BF16)
    first = TILE * lax.broadcasted_iota(jnp.int32, (columns, tiles_row), 1)
    cell = lax.broadcasted_iota(jnp.int32, (columns, tiles_row), 0)
    inside = jnp.where((cell >= first) & (cell < first + TILE), 1.0, 0.0).astype(BF16)
    return [
        jnp.dot(
            inside, named[k * tiles_row : (k + 1) * tiles_row], preferred_element_type=F32
        ).astype(BF16)
        for k in range(3)
    ]


def row_pairs(rate, rows):
    rows = list(rows)
    pairs = []
    for start in range(0, len(rows), 2 * rate):
        for k in range(rate):
            pairs.append((rows[start + k], rows[start + k + rate]))
    return pairs


def by_rate(rate, body):
    for value in RATES:
        pl.when(rate == value)(lambda value=value: body(value))


def clear_ends(pad_ref, count, columns):
    ends = jnp.zeros((EDGE, pad_ref.shape[-1]), F32)
    for k in range(count):
        pad_ref[k, :EDGE] = ends
        pad_ref[k, EDGE + columns :] = ends


def spread(value, pad_ref, slot, target_ref, offset):
    columns, channels = value.shape
    pad_ref[slot, EDGE : EDGE + columns] = value.astype(F32)
    target_ref[:, :channels] = pad_ref[slot, pl.ds(EDGE - offset, columns)].astype(BF16)
    target_ref[:, channels : 2 * channels] = value.astype(BF16)
    target_ref[:, 2 * channels :] = pad_ref[slot, pl.ds(EDGE + offset, columns)].astype(BF16)


def by_side(a_ref, b_ref, sides_ref):
    odd = lax.axis_index("tile") % 2

    def order(low, high):
        sides_ref[0] = low[...]
        sides_ref[1] = high[...]

    pl.when(odd == 0)(lambda: order(b_ref, a_ref))
    pl.when(odd == 1)(lambda: order(a_ref, b_ref))


def silu_grad(half_cot, half_pre):
    turn = jnp.tanh(half_pre)
    return half_cot * (1.0 + turn + half_pre * (1.0 - turn * turn))


def tap_sums(grads, xts, rate):
    flipped = jnp.concatenate(
        [
            jnp.concatenate([xts(row + rate * a) for row, _ in grads], axis=1)
            for a in (-1, 0, 1)
        ],
        axis=0,
    )
    return jnp.dot(
        flipped,
        jnp.concatenate([ref[...] for _, ref in grads], axis=0),
        preferred_element_type=F32,
    )


def pair_rows(pair, rate, rows):
    reach = [pair[0] + rate * (k - 1) for k in range(4)]
    inside = [k for k in range(4) if 0 <= reach[k] < rows]
    return [reach[k] for k in inside], inside[0], inside[-1] + 1


def input_sums(pair, rate, rows, grads, wide_ref):
    near, low, high = pair_rows(pair, rate, rows)
    lhs = jnp.concatenate([grads(row)[...] for row in near], axis=1)
    width = wide_ref.shape[0] // 4
    both = jnp.dot(lhs, wide_ref[low * width : high * width], preferred_element_type=F32)
    half = both.shape[1] // 2
    return both[:, :half], both[:, half:]


def first_kernel(
    rates_hbm, lists_hbm, x_hbm, cot_hbm, w_hbm, bias_hbm,
    near_rates_ref, grad_ref, pre_ref, xt_ref, total_ref, mask_ref, cot_ref, near_ref,
    rates_ref, lists_ref, bias_ref, xbuf, cbuf, wbuf, pad, xcat, gcat_ref, wide, sems,
):
    rows, columns, channels = x_hbm.shape
    tiles_row = columns // TILE
    mine = lax.axis_index("tile")
    step = rows // 4
    loads = [pltpu.make_async_copy(w_hbm, wbuf, sems.at[0])]
    for source, target, base in ((x_hbm, xbuf, 1), (cot_hbm, cbuf, 5)):
        for k in range(4):
            part = pl.ds(k * step, step)
            loads.append(
                pltpu.make_async_copy(source.at[part], target.at[part], sems.at[base + k])
            )
    small = [
        pltpu.make_async_copy(source, target, sems.at[9 + k])
        for k, (source, target) in enumerate(
            ((lists_hbm, lists_ref), (rates_hbm, rates_ref), (bias_hbm, bias_ref))
        )
    ]
    for load in small + loads:
        load.start()
    for load in small:
        load.wait()
    last = rates_ref.shape[1] - 1
    for k in range(3):
        row = jnp.clip(mine + k - 1, 0, last)
        near_rates_ref[k] = jnp.full(near_rates_ref.shape[1:], rates_ref[0, row], jnp.int32)
    for k, value in enumerate(cell_masks(lists_ref, mine, tiles_row, columns)):
        mask_ref[k] = value
    clear_ends(pad, rows, columns)
    loads[0].wait()
    none = jnp.zeros((channels, channels), BF16)
    for col in range(3):
        for side in range(2):
            near_ref[side, col * channels : (col + 1) * channels] = wbuf[6 * side + col]
        for row in range(4):
            start = (row * 3 + col) * channels
            for out in range(2):
                tap = row - out
                wide[start : start + channels, out * channels : (out + 1) * channels] = (
                    wbuf[tap * 3 + col] if 0 <= tap < 3 else none
                )
    for load in loads[1:]:
        load.wait()
    half_bias = 0.5 * bias_ref[...]

    def body(rate):
        done = set()

        def prepare(row):
            if row in done:
                return
            done.add(row)
            value = xbuf[row] * mask_ref[1]
            spread(value, pad, row, xcat.at[row], rate)
            xt_ref[row] = value.T

        def convolve(pair):
            near, low, high = pair_rows(pair, rate, rows)
            for row in near:
                prepare(row)
            lhs = jnp.concatenate([xcat[row] for row in near], axis=1)
            width = wide.shape[0] // 4
            both = jnp.dot(
                lhs, wide[low * width : high * width], preferred_element_type=F32
            )
            return pair, (both[:, :channels], both[:, channels:])

        def finish(pair, sums):
            for row, value in zip(pair, sums):
                half_pre = 0.5 * value + half_bias
                half_cot = cbuf[row] * mask_ref[1] * 0.5
                if HALO <= row < rows - HALO:
                    grad = silu_grad(half_cot.astype(F32), half_pre)
                    spread(grad, pad, row, gcat_ref.at[row - HALO], -rate)
                    grad_ref[row - HALO] = grad.astype(BF16)
                    ready.append(row)
                else:
                    here = row if row < HALO else row - (rows - 2 * HALO)
                    pre_ref[here] = half_pre
                    cot_ref[here] = half_cot

        ready = []
        summed = []
        waiting = None
        for pair in row_pairs(rate, range(rows)) + [None]:
            result = convolve(pair) if pair else None
            if waiting:
                finish(*waiting)
            waiting = result
            while len(ready) >= 2:
                grads = [(row, gcat_ref.at[row - HALO]) for row in ready[:2]]
                part = tap_sums(grads, lambda row: xt_ref[row], rate)
                total_ref[...] = total_ref[...] + part if summed else part
                summed.extend(ready[:2])
                del ready[:2]

    by_rate(rates_ref[0, mine], body)


def rims_kernel(
    rates_ref, a_ref, b_ref, pre_ref, cot_ref, mask_ref, near_ref, xt_own_ref, total_ref,
    grad_a_ref, grad_b_ref, keep_ref, send_ref,
    pad, xcat, halo, grads, xt_halo, gedge, flat, *, scale, paired,
):
    _, columns, channels = a_ref.shape
    rows = xt_own_ref.shape[0]
    clear_ends(pad, 4 * HALO, columns)
    by_side(a_ref, b_ref, halo)

    def flipped(row):
        if row < 0:
            return xt_halo[row + HALO]
        return xt_own_ref[row] if row < rows else xt_halo[row - rows + HALO]

    def body(rate):
        halves = []
        for side in range(2):
            used = range(HALO - rate, HALO) if side == 0 else range(rate)
            for place, k in enumerate(used):
                value = halo[side, k] * mask_ref[2 * side]
                part = pl.ds(place * columns, columns)
                spread(value, pad, side * HALO + k, xcat.at[side, part], rate)
                xt_halo[side * HALO + k] = value.T
            halves.append(
                jnp.dot(xcat[side, : rate * columns], near_ref[side], preferred_element_type=F32)
            )
        total = total_ref[...]
        for side, sums in enumerate(halves):
            edges = []
            for k in range(HALO):
                slot = side * HALO + k
                half_pre = pre_ref[slot]
                place = k if side == 0 else k - (HALO - rate)
                if 0 <= place < rate:
                    half_pre += 0.5 * sums[place * columns : (place + 1) * columns]
                grad = silu_grad(cot_ref[slot].astype(F32), half_pre)
                grads[side, k] = grad.astype(BF16)
                spread(grad, pad, 2 * HALO + slot, gedge.at[slot], -rate)
                edges.append((k + side * (rows - HALO), gedge.at[slot]))
            total = total + tap_sums(edges, flipped, rate)
        total = total * scale
        for a in range(3):
            for b in range(3):
                start = (a * 3 + b) * channels
                flat[start : start + channels] = total[
                    a * channels : (a + 1) * channels, b * channels : (b + 1) * channels
                ]

    by_rate(rates_ref[1, 0, 0], body)
    odd = lax.axis_index("tile") % 2
    grad_a_ref[...] = grads[1 - odd]
    grad_b_ref[...] = grads[odd]
    if not paired:
        keep_ref[0] = flat[...]
        return
    parts, share, _ = keep_ref.shape
    here = lax.axis_index("dp")
    for part in range(parts):
        keep_ref[part] = flat[pl.ds((2 * part + here) * share, share)]
        send_ref[part] = flat[pl.ds((2 * part + 1 - here) * share, share)].astype(BF16)


def last_kernel(
    rates_ref, from_a_ref, from_b_ref, grad_a_ref, grad_b_ref,
    grad_ref, cot_hbm, mask_ref, w_hbm,
    out_hbm,
    wbuf, back_ref, far_ref, cbuf, obuf, pad, gcat, spare, theirs, ours, sems,
):
    rows, columns, channels = cot_hbm.shape
    inner = rows - 2 * HALO
    around = 2 * HALO
    chunks = rows // around
    cots, stores = [], []
    for k in range(chunks):
        part = pl.ds(k * around, around)
        cots.append(
            pltpu.make_async_copy(cot_hbm.at[part], cbuf.at[part], sems.at[k])
        )
        stores.append(
            pltpu.make_async_copy(obuf.at[part], out_hbm.at[part], sems.at[chunks + k])
        )
    weights = pltpu.make_async_copy(w_hbm, wbuf, sems.at[2 * chunks])
    for load in [weights] + cots:
        load.start()
    clear_ends(pad, rows + 2 * HALO, columns)
    by_side(from_a_ref, from_b_ref, theirs)
    by_side(grad_a_ref, grad_b_ref, ours)
    weights.wait()
    blank = jnp.zeros((channels, channels), BF16)
    for col in range(3):
        turned = [wbuf[tap * 3 + col].T for tap in range(3)]
        for side in range(2):
            far_ref[side, col * channels : (col + 1) * channels] = turned[2 - 2 * side]
        for row in range(4):
            start = (row * 3 + col) * channels
            for out in range(2):
                tap = out + 2 - row
                back_ref[start : start + channels, out * channels : (out + 1) * channels] = (
                    turned[tap] if 0 <= tap < 3 else blank
                )

    def neighbour(side):
        rate = rates_ref[2 * side, 0, 0]
        for k in range(HALO):
            part = pl.ds(k * columns, columns)
            spread(theirs[side, k], pad, rows + side * HALO + k, spare.at[side, part], -rate)
        sums = jnp.dot(spare[side], far_ref[side], preferred_element_type=F32)
        parts = [sums[k * columns : (k + 1) * columns] for k in range(HALO)]
        none = jnp.zeros((columns, channels), F32)
        one = rate == 1
        if side:
            return [jnp.where(one, none, parts[0]), jnp.where(one, parts[0], parts[1])]
        return [jnp.where(one, parts[1], parts[0]), jnp.where(one, none, parts[1])]

    def body(rate):
        done = set()

        def shifted(row):
            if row not in done:
                done.add(row)
                if row < HALO:
                    value = ours[0, row]
                elif row < rows - HALO:
                    value = grad_ref[row - HALO]
                else:
                    value = ours[1, row - (rows - HALO)]
                spread(value, pad, row, gcat.at[row], -rate)
            return gcat.at[row]

        for chunk in range(chunks):
            start = chunk * around
            results = [
                (pair, input_sums(pair, rate, rows, shifted, back_ref))
                for pair in row_pairs(rate, range(start, start + around))
            ]
            terms = {0: 0, chunks - 1: 1}
            added = neighbour(terms[chunk]) if chunk in terms else None
            cots[chunk].wait()
            for pair, sums in results:
                for row, value in zip(pair, sums):
                    value = value + cbuf[row].astype(F32)
                    if row < HALO:
                        value = value + added[row]
                    elif row >= rows - HALO:
                        value = value + added[row - (rows - HALO)]
                    obuf[row] = value.astype(BF16) * mask_ref[1]
            stores[chunk].start()

    by_rate(rates_ref[1, 0, 0], body)
    for store in stores:
        store.wait()


def cut_kernel(x_hbm, a_ref, b_ref, sems):
    rows = x_hbm.shape[0]
    odd = lax.axis_index("tile") % 2
    copies = []
    for index, ref in enumerate((a_ref, b_ref)):
        start = (rows - HALO) * (odd if index else 1 - odd)
        for k in range(HALO):
            copies.append(
                pltpu.make_async_copy(x_hbm.at[start + k], ref.at[k], sems.at[index, k])
            )
    for copy in copies:
        copy.start()
    for copy in copies:
        copy.wait()


def swap(rows_a, rows_b, axis):
    count = lax.axis_size(axis)
    results = []
    for start, rows in ((0, rows_a), (1, rows_b)):
        pairs = [(i, i + 1) for i in range(start, count - 1, 2)]
        results.append(lax.ppermute(rows, axis, pairs + [(j, i) for i, j in pairs]))
    return results


def call(kernel, name, outs, specs, scratch, aliases=None, flops=0):
    memory = {"s": pltpu.SMEM, "v": pltpu.VMEM, "h": pltpu.HBM}
    ins, results = (
        [pl.BlockSpec(memory_space=memory[letter]) for letter in part] for part in specs.split(">")
    )
    return pl.pallas_call(
        kernel,
        name=name,
        out_shape=tuple(
            pltpu.HBM(shape, dtype) if letter == "h" else jax.ShapeDtypeStruct(shape, dtype)
            for (shape, dtype), letter in zip(outs, specs.split(">")[1])
        ),
        in_specs=ins,
        out_specs=tuple(results),
        scratch_shapes=scratch,
        input_output_aliases=aliases or {},
        cost_estimate=pl.CostEstimate(flops=flops, bytes_accessed=0, transcendentals=0),
        compiler_params=pltpu.CompilerParams(vmem_limit_bytes=VMEM_LIMIT),
    )


def in_hbm(array):
    return pltpu.with_memory_space_constraint(array, pltpu.HBM)


def shards(features, cotangent, tile_mask, work_lists, dilations, conv_weight, conv_bias):
    x, cot, lists = features[0], in_hbm(cotangent[0]), in_hbm(work_lists[0])
    dilations = in_hbm(dilations)
    rows, columns, channels = x.shape
    axes = ("tile", "dp")
    devices = lax.axis_size("tile") * lax.axis_size("dp")
    weight = in_hbm(conv_weight.reshape(9, channels, channels))
    bias = in_hbm(conv_bias.reshape(1, channels))
    inner = rows - 2 * HALO
    wide_row = 3 * channels
    whole = ((rows, columns, channels), BF16)

    def pads(count):
        return pltpu.VMEM((count, columns + 2 * EDGE, channels), F32)

    rim = ((HALO, columns, channels), BF16)
    sides = pltpu.VMEM((2, HALO, columns, channels), BF16)
    rows_a, rows_b = call(
        cut_kernel,
        "cut",
        [rim, rim],
        "h>vv",
        [pltpu.SemaphoreType.DMA((2, HALO))],
    )(in_hbm(x))
    x_a, x_b = swap(rows_a, rows_b, "tile")

    rates, grad, pre, xt, total, mask, cot_edge, near = call(
        first_kernel,
        "first",
        [
            ((3, 8, LANES), jnp.int32),
            ((inner, columns, channels), BF16),
            ((2 * HALO, columns, channels), F32),
            ((rows, channels, columns), BF16),
            ((wide_row, wide_row), F32),
            ((3, columns, channels), BF16),
            ((2 * HALO, columns, channels), BF16),
            ((2, wide_row, channels), BF16),
        ],
        "hhhhhh>vvvvvvvv",
        [
            pltpu.SMEM(dilations.shape, jnp.int32),
            pltpu.VMEM(lists.shape, jnp.int32),
            pltpu.VMEM(bias.shape, F32),
            pltpu.VMEM((rows, columns, channels), BF16),
            pltpu.VMEM((rows, columns, channels), BF16),
            pltpu.VMEM((9, channels, channels), BF16),
            pads(rows),
            pltpu.VMEM((rows, columns, wide_row), BF16),
            pltpu.VMEM((inner, columns, wide_row), BF16),
            pltpu.VMEM((4 * wide_row, 2 * channels), BF16),
            pltpu.SemaphoreType.DMA((12,)),
        ],
        flops=BUSY,
    )(dilations, lists, in_hbm(x), cot, weight, bias)

    tap_rows = 9 * channels
    cores = lax.axis_size("dp")
    paired = cores == 2 and tap_rows % devices == 0
    share = (devices // 2, tap_rows // devices) if paired else (1, tap_rows)
    scale = 1.0 / math.sqrt(devices * lists.shape[1] * TILE * TILE)
    grad_a, grad_b, keep, send = call(
        lambda *refs: rims_kernel(*refs, scale=scale, paired=paired),
        "rims",
        [rim, rim, (share + (channels,), F32), (share + (channels,), BF16)],
        "vvvvvvvvv>vvvv",
        [
            pads(4 * HALO),
            pltpu.VMEM((2, HALO * columns, wide_row), BF16),
            sides,
            sides,
            pltpu.VMEM((2 * HALO, channels, columns), BF16),
            pltpu.VMEM((2 * HALO, columns, wide_row), BF16),
            pltpu.VMEM((tap_rows, channels), F32),
        ],
    )(rates, x_a, x_b, pre, cot_edge, mask, near, xt, total)

    from_a, from_b = swap(grad_a, grad_b, "tile")
    if paired:
        other = lax.ppermute(send, "dp", [(0, 1), (1, 0)])
        both = (keep + other.astype(F32)).astype(BF16)
        received = lax.all_to_all(both, "tile", 0, 0, tiled=True)
    else:
        received = lax.all_to_all(
            keep.astype(BF16).reshape(devices, -1), axes, 0, 0, tiled=True
        )

    (input_grad,) = call(
        last_kernel,
        "last",
        [whole],
        "vvvvvvhvh>h",
        [
            pltpu.VMEM((9, channels, channels), BF16),
            pltpu.VMEM((4 * wide_row, 2 * channels), BF16),
            pltpu.VMEM((2, wide_row, channels), BF16),
            pltpu.VMEM((rows, columns, channels), BF16),
            pltpu.VMEM((rows, columns, channels), BF16),
            pads(rows + 2 * HALO),
            pltpu.VMEM((rows, columns, wide_row), BF16),
            pltpu.VMEM((2, HALO * columns, wide_row), BF16),
            sides,
            sides,
            pltpu.SemaphoreType.DMA((2 * (rows // (2 * HALO)) + 1,)),
        ],
        flops=BUSY,
    )(
        rates, from_a, from_b, grad_a, grad_b,
        grad, cot, mask, weight,
    )
    summed = jnp.sum(received.astype(F32), axis=0)
    return (input_grad[None], summed.reshape(-1))


def solution(mesh):
    placed = (
        P("dp", "tile", None, None),
        P("dp", "tile", None, None),
        P("dp", "tile", None),
        P("dp", None, None),
        P("dp", None),
        P(),
        P(),
    )
    return jax.shard_map(
        shards,
        mesh=mesh,
        in_specs=placed,
        out_specs=(P("dp", "tile", None, None), P(("tile", "dp"))),
        check_vma=False,
    )
```

```python
import math

import jax
import jax.numpy as jnp
from jax import lax
from jax.experimental import pallas as pl
from jax.experimental.pallas import tpu as pltpu
from jax.sharding import PartitionSpec as P

TILE = 12
HALO = 2
LANES = 128
EDGE = 8
PACK = 16
RATES = (1, 2)
VMEM_LIMIT = 40 * 1024 * 1024
BUSY = 20_000_000_000

F32 = jnp.float32
BF16 = jnp.bfloat16


def cell_masks(lists_ref, middle, tiles_row, columns):
    ids = lists_ref[...]
    workers, width = ids.shape
    tile = lax.broadcasted_iota(jnp.int32, (3 * tiles_row, width), 0)
    target = (middle - 1) * tiles_row + tile
    found = ids[0:1] == target
    for worker in range(1, workers):
        found = found | (ids[worker : worker + 1] == target)
    named = jnp.dot(
        jnp.where(found, 1.0, 0.0).astype(BF16),
        jnp.ones((width, LANES), BF16),
        preferred_element_type=F32,
    ).astype(BF16)
    first = TILE * lax.broadcasted_iota(jnp.int32, (columns, tiles_row), 1)
    cell = lax.broadcasted_iota(jnp.int32, (columns, tiles_row), 0)
    inside = jnp.where((cell >= first) & (cell < first + TILE), 1.0, 0.0).astype(BF16)
    return [
        jnp.dot(
            inside, named[k * tiles_row : (k + 1) * tiles_row], preferred_element_type=F32
        ).astype(BF16)
        for k in range(3)
    ]


def row_pairs(rate, rows):
    rows = list(rows)
    pairs = []
    for start in range(0, len(rows), 2 * rate):
        for k in range(rate):
            pairs.append((rows[start + k], rows[start + k + rate]))
    return pairs


def by_rate(rate, body):
    for value in RATES:
        pl.when(rate == value)(lambda value=value: body(value))


def clear_ends(pad_ref, count, columns):
    ends = jnp.zeros((EDGE, pad_ref.shape[-1]), F32)
    for k in range(count):
        pad_ref[k, :EDGE] = ends
        pad_ref[k, EDGE + columns :] = ends


def spread(value, pad_ref, slot, target_ref, offset):
    columns, channels = value.shape
    pad_ref[slot, EDGE : EDGE + columns] = value.astype(F32)
    target_ref[:, :channels] = pad_ref[slot, pl.ds(EDGE - offset, columns)].astype(BF16)
    target_ref[:, channels : 2 * channels] = value.astype(BF16)
    target_ref[:, 2 * channels :] = pad_ref[slot, pl.ds(EDGE + offset, columns)].astype(BF16)


def by_side(a_ref, b_ref, sides_ref):
    odd = lax.axis_index("tile") % 2

    def order(low, high):
        sides_ref[0] = low[...]
        sides_ref[1] = high[...]

    pl.when(odd == 0)(lambda: order(b_ref, a_ref))
    pl.when(odd == 1)(lambda: order(a_ref, b_ref))


def silu_grad(half_cot, half_pre):
    turn = jnp.tanh(half_pre)
    return half_cot * (1.0 + turn + half_pre * (1.0 - turn * turn))


def tap_sums(grads, xts, rate):
    flipped = jnp.concatenate(
        [
            jnp.concatenate([xts(row + rate * a) for row, _ in grads], axis=1)
            for a in (-1, 0, 1)
        ],
        axis=0,
    )
    return jnp.dot(
        flipped,
        jnp.concatenate([ref[...] for _, ref in grads], axis=0),
        preferred_element_type=F32,
    )


def pair_rows(pair, rate, rows):
    reach = [pair[0] + rate * (k - 1) for k in range(4)]
    inside = [k for k in range(4) if 0 <= reach[k] < rows]
    return [reach[k] for k in inside], inside[0], inside[-1] + 1


def input_sums(pair, rate, rows, grads, wide_ref):
    near, low, high = pair_rows(pair, rate, rows)
    lhs = jnp.concatenate([grads(row)[...] for row in near], axis=1)
    width = wide_ref.shape[0] // 4
    both = jnp.dot(lhs, wide_ref[low * width : high * width], preferred_element_type=F32)
    half = both.shape[1] // 2
    return both[:, :half], both[:, half:]


def first_kernel(
    rates_hbm, lists_hbm, x_hbm, cot_hbm, w_hbm, bias_hbm,
    near_rates_ref, grad_ref, pre_ref, xt_ref, total_ref, mask_ref, cot_ref, back_ref, near_ref, far_ref,
    rates_ref, lists_ref, bias_ref, xbuf, cbuf, wbuf, pad, xcat, gcat_ref, wide, sems,
):
    rows, columns, channels = x_hbm.shape
    tiles_row = columns // TILE
    mine = lax.axis_index("tile")
    step = rows // 4
    loads = [pltpu.make_async_copy(w_hbm, wbuf, sems.at[0])]
    for source, target, base in ((x_hbm, xbuf, 1), (cot_hbm, cbuf, 5)):
        for k in range(4):
            part = pl.ds(k * step, step)
            loads.append(
                pltpu.make_async_copy(source.at[part], target.at[part], sems.at[base + k])
            )
    small = [
        pltpu.make_async_copy(source, target, sems.at[9 + k])
        for k, (source, target) in enumerate(
            ((lists_hbm, lists_ref), (rates_hbm, rates_ref), (bias_hbm, bias_ref))
        )
    ]
    for load in small + loads:
        load.start()
    for load in small:
        load.wait()
    last = rates_ref.shape[1] - 1
    for k in range(3):
        row = jnp.clip(mine + k - 1, 0, last)
        near_rates_ref[k] = jnp.full(near_rates_ref.shape[1:], rates_ref[0, row], jnp.int32)
    for k, value in enumerate(cell_masks(lists_ref, mine, tiles_row, columns)):
        mask_ref[k] = value
    clear_ends(pad, rows, columns)
    loads[0].wait()
    none = jnp.zeros((channels, channels), BF16)
    for col in range(3):
        there = slice(col * channels, (col + 1) * channels)
        turned = [wbuf[tap * 3 + col].T for tap in range(3)]
        for side in range(2):
            near_ref[side, there] = wbuf[6 * side + col]
            far_ref[side, there] = turned[2 - 2 * side]
        for row in range(4):
            start = (row * 3 + col) * channels
            here = slice(start, start + channels)
            for out in range(2):
                there = slice(out * channels, (out + 1) * channels)
                tap = row - out
                wide[here, there] = wbuf[tap * 3 + col] if 0 <= tap < 3 else none
                tap = out + 2 - row
                back_ref[here, there] = turned[tap] if 0 <= tap < 3 else none
    for load in loads[1:]:
        load.wait()
    half_bias = 0.5 * bias_ref[...]

    def body(rate):
        done = set()

        def prepare(row):
            if row in done:
                return
            done.add(row)
            value = xbuf[row] * mask_ref[1]
            spread(value, pad, row, xcat.at[row], rate)
            xt_ref[row] = value.T

        def convolve(pair):
            near, low, high = pair_rows(pair, rate, rows)
            for row in near:
                prepare(row)
            lhs = jnp.concatenate([xcat[row] for row in near], axis=1)
            width = wide.shape[0] // 4
            both = jnp.dot(
                lhs, wide[low * width : high * width], preferred_element_type=F32
            )
            return pair, (both[:, :channels], both[:, channels:])

        def finish(pair, sums):
            for row, value in zip(pair, sums):
                half_pre = 0.5 * value + half_bias
                half_cot = cbuf[row] * mask_ref[1] * 0.5
                if HALO <= row < rows - HALO:
                    grad = silu_grad(half_cot.astype(F32), half_pre)
                    spread(grad, pad, row, gcat_ref.at[row - HALO], -rate)
                    grad_ref[row - HALO] = grad.astype(BF16)
                    ready.append(row)
                else:
                    here = row if row < HALO else row - (rows - 2 * HALO)
                    pre_ref[here] = half_pre
                    cot_ref[here] = half_cot

        ready = []
        summed = []
        waiting = None
        for pair in row_pairs(rate, range(rows)) + [None]:
            result = convolve(pair) if pair else None
            if waiting:
                finish(*waiting)
            waiting = result
            while len(ready) >= 2:
                grads = [(row, gcat_ref.at[row - HALO]) for row in ready[:2]]
                part = tap_sums(grads, lambda row: xt_ref[row], rate)
                total_ref[...] = total_ref[...] + part if summed else part
                summed.extend(ready[:2])
                del ready[:2]

    by_rate(rates_ref[0, mine], body)


def rims_kernel(
    rates_ref, a_ref, b_ref, pre_ref, cot_ref, mask_ref, near_ref, xt_own_ref, total_ref,
    grad_a_ref, grad_b_ref, keep_ref, send_ref,
    pad, xcat, halo, grads, xt_halo, gedge, flat, *, scale, paired,
):
    _, columns, channels = a_ref.shape
    rows = xt_own_ref.shape[0]
    clear_ends(pad, 4 * HALO, columns)
    by_side(a_ref, b_ref, halo)

    def flipped(row):
        if row < 0:
            return xt_halo[row + HALO]
        return xt_own_ref[row] if row < rows else xt_halo[row - rows + HALO]

    def body(rate):
        halves = []
        for side in range(2):
            used = range(HALO - rate, HALO) if side == 0 else range(rate)
            for place, k in enumerate(used):
                value = halo[side, k] * mask_ref[2 * side]
                part = pl.ds(place * columns, columns)
                spread(value, pad, side * HALO + k, xcat.at[side, part], rate)
                xt_halo[side * HALO + k] = value.T
            halves.append(
                jnp.dot(xcat[side, : rate * columns], near_ref[side], preferred_element_type=F32)
            )
        total = total_ref[...]
        for side, sums in enumerate(halves):
            edges = []
            for k in range(HALO):
                slot = side * HALO + k
                half_pre = pre_ref[slot]
                place = k if side == 0 else k - (HALO - rate)
                if 0 <= place < rate:
                    half_pre += 0.5 * sums[place * columns : (place + 1) * columns]
                grad = silu_grad(cot_ref[slot].astype(F32), half_pre)
                grads[side, k] = grad.astype(BF16)
                spread(grad, pad, 2 * HALO + slot, gedge.at[slot], -rate)
                edges.append((k + side * (rows - HALO), gedge.at[slot]))
            total = total + tap_sums(edges, flipped, rate)
        total = total * scale
        for a in range(3):
            for b in range(3):
                start = (a * 3 + b) * channels
                flat[start : start + channels] = total[
                    a * channels : (a + 1) * channels, b * channels : (b + 1) * channels
                ]

    by_rate(rates_ref[1, 0, 0], body)
    odd = lax.axis_index("tile") % 2
    grad_a_ref[...] = grads[1 - odd]
    grad_b_ref[...] = grads[odd]
    if not paired:
        keep_ref[0] = flat[: keep_ref.shape[1]]
        return
    parts, share, _ = keep_ref.shape
    padded = send_ref.shape[1]
    flat[parts * 2 * share :] = jnp.zeros((flat.shape[0] - parts * 2 * share, channels), F32)
    here = lax.axis_index("dp")
    for part in range(parts):
        keep_ref[part] = flat[pl.ds((2 * part + here) * share, share)]
        send_ref[part] = flat[pl.ds((2 * part + 1 - here) * share, padded)].astype(BF16)


def last_kernel(
    rates_ref, from_a_ref, from_b_ref, grad_a_ref, grad_b_ref,
    grad_ref, cot_hbm, mask_ref, back_ref, far_ref,
    out_hbm,
    cbuf, obuf, pad, gcat, spare, theirs, ours, sems,
):
    rows, columns, channels = cot_hbm.shape
    inner = rows - 2 * HALO
    around = 2 * HALO
    chunks = rows // around
    cots, stores = [], []
    for k in range(chunks):
        part = pl.ds(k * around, around)
        cots.append(
            pltpu.make_async_copy(cot_hbm.at[part], cbuf.at[part], sems.at[k])
        )
        stores.append(
            pltpu.make_async_copy(obuf.at[part], out_hbm.at[part], sems.at[chunks + k])
        )
    for load in cots:
        load.start()
    clear_ends(pad, rows + 2 * HALO, columns)
    by_side(from_a_ref, from_b_ref, theirs)
    by_side(grad_a_ref, grad_b_ref, ours)

    def neighbour(side):
        rate = rates_ref[2 * side, 0, 0]
        for k in range(HALO):
            part = pl.ds(k * columns, columns)
            spread(theirs[side, k], pad, rows + side * HALO + k, spare.at[side, part], -rate)
        sums = jnp.dot(spare[side], far_ref[side], preferred_element_type=F32)
        parts = [sums[k * columns : (k + 1) * columns] for k in range(HALO)]
        none = jnp.zeros((columns, channels), F32)
        one = rate == 1
        if side:
            return [jnp.where(one, none, parts[0]), jnp.where(one, parts[0], parts[1])]
        return [jnp.where(one, parts[1], parts[0]), jnp.where(one, none, parts[1])]

    def body(rate):
        done = set()

        def shifted(row):
            if row not in done:
                done.add(row)
                if row < HALO:
                    value = ours[0, row]
                elif row < rows - HALO:
                    value = grad_ref[row - HALO]
                else:
                    value = ours[1, row - (rows - HALO)]
                spread(value, pad, row, gcat.at[row], -rate)
            return gcat.at[row]

        for chunk in range(chunks):
            start = chunk * around
            results = [
                (pair, input_sums(pair, rate, rows, shifted, back_ref))
                for pair in row_pairs(rate, range(start, start + around))
            ]
            terms = {0: 0, chunks - 1: 1}
            added = neighbour(terms[chunk]) if chunk in terms else None
            cots[chunk].wait()
            for pair, sums in results:
                for row, value in zip(pair, sums):
                    value = value + cbuf[row].astype(F32)
                    if row < HALO:
                        value = value + added[row]
                    elif row >= rows - HALO:
                        value = value + added[row - (rows - HALO)]
                    obuf[row] = value.astype(BF16) * mask_ref[1]
            stores[chunk].start()

    by_rate(rates_ref[1, 0, 0], body)
    for store in stores:
        store.wait()


def cut_kernel(x_hbm, a_ref, b_ref, sems):
    rows = x_hbm.shape[0]
    odd = lax.axis_index("tile") % 2
    copies = []
    for index, ref in enumerate((a_ref, b_ref)):
        start = (rows - HALO) * (odd if index else 1 - odd)
        for k in range(HALO):
            copies.append(
                pltpu.make_async_copy(x_hbm.at[start + k], ref.at[k], sems.at[index, k])
            )
    for copy in copies:
        copy.start()
    for copy in copies:
        copy.wait()


def swap(rows_a, rows_b, axis):
    count = lax.axis_size(axis)
    results = []
    for start, rows in ((0, rows_a), (1, rows_b)):
        pairs = [(i, i + 1) for i in range(start, count - 1, 2)]
        results.append(lax.ppermute(rows, axis, pairs + [(j, i) for i, j in pairs]))
    return results


def call(kernel, name, outs, specs, scratch, aliases=None, flops=0):
    memory = {"s": pltpu.SMEM, "v": pltpu.VMEM, "h": pltpu.HBM}
    ins, results = (
        [pl.BlockSpec(memory_space=memory[letter]) for letter in part] for part in specs.split(">")
    )
    return pl.pallas_call(
        kernel,
        name=name,
        out_shape=tuple(
            pltpu.HBM(shape, dtype) if letter == "h" else jax.ShapeDtypeStruct(shape, dtype)
            for (shape, dtype), letter in zip(outs, specs.split(">")[1])
        ),
        in_specs=ins,
        out_specs=tuple(results),
        scratch_shapes=scratch,
        input_output_aliases=aliases or {},
        cost_estimate=pl.CostEstimate(flops=flops, bytes_accessed=0, transcendentals=0),
        compiler_params=pltpu.CompilerParams(vmem_limit_bytes=VMEM_LIMIT),
    )


def in_hbm(array):
    return pltpu.with_memory_space_constraint(array, pltpu.HBM)


def shards(features, cotangent, tile_mask, work_lists, dilations, conv_weight, conv_bias):
    x, cot, lists = features[0], in_hbm(cotangent[0]), in_hbm(work_lists[0])
    dilations = in_hbm(dilations)
    rows, columns, channels = x.shape
    axes = ("tile", "dp")
    devices = lax.axis_size("tile") * lax.axis_size("dp")
    weight = in_hbm(conv_weight.reshape(9, channels, channels))
    bias = in_hbm(conv_bias.reshape(1, channels))
    inner = rows - 2 * HALO
    wide_row = 3 * channels
    whole = ((rows, columns, channels), BF16)

    def pads(count):
        return pltpu.VMEM((count, columns + 2 * EDGE, channels), F32)

    rim = ((HALO, columns, channels), BF16)
    sides = pltpu.VMEM((2, HALO, columns, channels), BF16)
    rows_a, rows_b = call(
        cut_kernel,
        "cut",
        [rim, rim],
        "h>vv",
        [pltpu.SemaphoreType.DMA((2, HALO))],
    )(in_hbm(x))
    x_a, x_b = swap(rows_a, rows_b, "tile")

    rates, grad, pre, xt, total, mask, cot_edge, back, near, far = call(
        first_kernel,
        "first",
        [
            ((3, 8, LANES), jnp.int32),
            ((inner, columns, channels), BF16),
            ((2 * HALO, columns, channels), F32),
            ((rows, channels, columns), BF16),
            ((wide_row, wide_row), F32),
            ((3, columns, channels), BF16),
            ((2 * HALO, columns, channels), BF16),
            ((4 * wide_row, 2 * channels), BF16),
            ((2, wide_row, channels), BF16),
            ((2, wide_row, channels), BF16),
        ],
        "hhhhhh>vvvvvvvvvv",
        [
            pltpu.SMEM(dilations.shape, jnp.int32),
            pltpu.VMEM(lists.shape, jnp.int32),
            pltpu.VMEM(bias.shape, F32),
            pltpu.VMEM((rows, columns, channels), BF16),
            pltpu.VMEM((rows, columns, channels), BF16),
            pltpu.VMEM((9, channels, channels), BF16),
            pads(rows),
            pltpu.VMEM((rows, columns, wide_row), BF16),
            pltpu.VMEM((inner, columns, wide_row), BF16),
            pltpu.VMEM((4 * wide_row, 2 * channels), BF16),
            pltpu.SemaphoreType.DMA((12,)),
        ],
        flops=BUSY,
    )(dilations, lists, in_hbm(x), cot, weight, bias)

    tap_rows = 9 * channels
    cores = lax.axis_size("dp")
    paired = cores == 2 and tap_rows % devices == 0
    share = (devices // 2, tap_rows // devices) if paired else (1, tap_rows)
    padded = -(-share[1] // PACK) * PACK
    scale = 1.0 / math.sqrt(devices * lists.shape[1] * TILE * TILE)
    grad_a, grad_b, keep, send = call(
        lambda *refs: rims_kernel(*refs, scale=scale, paired=paired),
        "rims",
        [rim, rim, (share + (channels,), F32), ((share[0], padded, channels), BF16)],
        "vvvvvvvvv>vvvv",
        [
            pads(4 * HALO),
            pltpu.VMEM((2, HALO * columns, wide_row), BF16),
            sides,
            sides,
            pltpu.VMEM((2 * HALO, channels, columns), BF16),
            pltpu.VMEM((2 * HALO, columns, wide_row), BF16),
            pltpu.VMEM((tap_rows + PACK, channels), F32),
        ],
    )(rates, x_a, x_b, pre, cot_edge, mask, near, xt, total)

    from_a, from_b = swap(grad_a, grad_b, "tile")
    if paired:
        other = lax.ppermute(send, "dp", [(0, 1), (1, 0)])
        both = (keep + other[:, : share[1]].astype(F32)).astype(BF16)
        received = lax.all_to_all(both, "tile", 0, 0, tiled=True)
    else:
        received = lax.all_to_all(
            keep.astype(BF16).reshape(devices, -1), axes, 0, 0, tiled=True
        )

    (input_grad,) = call(
        last_kernel,
        "last",
        [whole],
        "vvvvvvhvvv>h",
        [
            pltpu.VMEM((rows, columns, channels), BF16),
            pltpu.VMEM((rows, columns, channels), BF16),
            pads(rows + 2 * HALO),
            pltpu.VMEM((rows, columns, wide_row), BF16),
            pltpu.VMEM((2, HALO * columns, wide_row), BF16),
            sides,
            sides,
            pltpu.SemaphoreType.DMA((2 * (rows // (2 * HALO)),)),
        ],
        flops=BUSY,
    )(
        rates, from_a, from_b, grad_a, grad_b,
        grad, cot, mask, back, far,
    )
    summed = jnp.sum(received.astype(F32), axis=0)
    return (input_grad[None], summed.reshape(-1))


def solution(mesh):
    placed = (
        P("dp", "tile", None, None),
        P("dp", "tile", None, None),
        P("dp", "tile", None),
        P("dp", None, None),
        P("dp", None),
        P(),
        P(),
    )
    return jax.shard_map(
        shards,
        mesh=mesh,
        in_specs=placed,
        out_specs=(P("dp", "tile", None, None), P(("tile", "dp"))),
        check_vma=False,
    )
```

```python
import math

import jax
import jax.numpy as jnp
from jax import lax
from jax.experimental import pallas as pl
from jax.experimental.pallas import tpu as pltpu
from jax.sharding import PartitionSpec as P

TILE = 12
HALO = 2
LANES = 128
EDGE = 8
PACK = 16
RATES = (1, 2)
VMEM_LIMIT = 40 * 1024 * 1024
BUSY = 20_000_000_000

F32 = jnp.float32
BF16 = jnp.bfloat16


def cell_masks(lists_ref, middle, tiles_row, columns):
    ids = lists_ref[...]
    workers, width = ids.shape
    tile = lax.broadcasted_iota(jnp.int32, (3 * tiles_row, width), 0)
    target = (middle - 1) * tiles_row + tile
    found = ids[0:1] == target
    for worker in range(1, workers):
        found = found | (ids[worker : worker + 1] == target)
    named = jnp.dot(
        jnp.where(found, 1.0, 0.0).astype(BF16),
        jnp.ones((width, LANES), BF16),
        preferred_element_type=F32,
    ).astype(BF16)
    first = TILE * lax.broadcasted_iota(jnp.int32, (columns, tiles_row), 1)
    cell = lax.broadcasted_iota(jnp.int32, (columns, tiles_row), 0)
    inside = jnp.where((cell >= first) & (cell < first + TILE), 1.0, 0.0).astype(BF16)
    return [
        jnp.dot(
            inside, named[k * tiles_row : (k + 1) * tiles_row], preferred_element_type=F32
        ).astype(BF16)
        for k in range(3)
    ]


def row_pairs(rate, rows):
    rows = list(rows)
    pairs = []
    for start in range(0, len(rows), 2 * rate):
        for k in range(rate):
            pairs.append((rows[start + k], rows[start + k + rate]))
    return pairs


def by_rate(rate, body):
    for value in RATES:
        pl.when(rate == value)(lambda value=value: body(value))


def clear_ends(pad_ref, count, columns):
    ends = jnp.zeros((EDGE, pad_ref.shape[-1]), F32)
    for k in range(count):
        pad_ref[k, :EDGE] = ends
        pad_ref[k, EDGE + columns :] = ends


def spread(value, pad_ref, slot, target_ref, offset):
    columns, channels = value.shape
    pad_ref[slot, EDGE : EDGE + columns] = value.astype(F32)
    target_ref[:, :channels] = pad_ref[slot, pl.ds(EDGE - offset, columns)].astype(BF16)
    target_ref[:, channels : 2 * channels] = value.astype(BF16)
    target_ref[:, 2 * channels :] = pad_ref[slot, pl.ds(EDGE + offset, columns)].astype(BF16)


def by_side(a_ref, b_ref, sides_ref):
    odd = lax.axis_index("tile") % 2

    def order(low, high):
        sides_ref[0] = low[...]
        sides_ref[1] = high[...]

    pl.when(odd == 0)(lambda: order(b_ref, a_ref))
    pl.when(odd == 1)(lambda: order(a_ref, b_ref))


def silu_grad(half_cot, half_pre):
    turn = jnp.tanh(half_pre)
    return half_cot * (1.0 + turn + half_pre * (1.0 - turn * turn))


def tap_sums(grads, xts, rate):
    flipped = jnp.concatenate(
        [
            jnp.concatenate([xts(row + rate * a) for row, _ in grads], axis=1)
            for a in (-1, 0, 1)
        ],
        axis=0,
    )
    return jnp.dot(
        flipped,
        jnp.concatenate([ref[...] for _, ref in grads], axis=0),
        preferred_element_type=F32,
    )


def pair_rows(pair, rate, rows):
    reach = [pair[0] + rate * (k - 1) for k in range(4)]
    inside = [k for k in range(4) if 0 <= reach[k] < rows]
    return [reach[k] for k in inside], inside[0], inside[-1] + 1


def input_sums(pair, rate, rows, grads, wide_ref):
    near, low, high = pair_rows(pair, rate, rows)
    lhs = jnp.concatenate([grads(row)[...] for row in near], axis=1)
    width = wide_ref.shape[0] // 4
    both = jnp.dot(lhs, wide_ref[low * width : high * width], preferred_element_type=F32)
    half = both.shape[1] // 2
    return both[:, :half], both[:, half:]


def first_kernel(
    rates_hbm, lists_hbm, x_hbm, cot_hbm, w_hbm, bias_hbm,
    near_rates_ref, grad_ref, pre_ref, xt_ref, total_ref, mask_ref, cot_ref, back_ref, near_ref, far_ref,
    rates_ref, lists_ref, bias_ref, xbuf, cbuf, wbuf, pad, xcat, gcat_ref, wide, sems,
):
    rows, columns, channels = x_hbm.shape
    tiles_row = columns // TILE
    mine = lax.axis_index("tile")
    step = rows // 4
    loads = [pltpu.make_async_copy(w_hbm, wbuf, sems.at[0])]
    for source, target, base in ((x_hbm, xbuf, 1), (cot_hbm, cbuf, 5)):
        for k in range(4):
            part = pl.ds(k * step, step)
            loads.append(
                pltpu.make_async_copy(source.at[part], target.at[part], sems.at[base + k])
            )
    small = [
        pltpu.make_async_copy(source, target, sems.at[9 + k])
        for k, (source, target) in enumerate(
            ((lists_hbm, lists_ref), (rates_hbm, rates_ref), (bias_hbm, bias_ref))
        )
    ]
    for load in small + loads:
        load.start()
    for load in small:
        load.wait()
    last = rates_ref.shape[1] - 1
    for k in range(3):
        row = jnp.clip(mine + k - 1, 0, last)
        near_rates_ref[k] = jnp.full(near_rates_ref.shape[1:], rates_ref[0, row], jnp.int32)
    for k, value in enumerate(cell_masks(lists_ref, mine, tiles_row, columns)):
        mask_ref[k] = value
    clear_ends(pad, rows, columns)
    loads[0].wait()
    none = jnp.zeros((channels, channels), BF16)
    for col in range(3):
        there = slice(col * channels, (col + 1) * channels)
        turned = [wbuf[tap * 3 + col].T for tap in range(3)]
        for side in range(2):
            near_ref[side, there] = wbuf[6 * side + col]
            far_ref[side, there] = turned[2 - 2 * side]
        for row in range(4):
            start = (row * 3 + col) * channels
            here = slice(start, start + channels)
            for out in range(2):
                there = slice(out * channels, (out + 1) * channels)
                tap = row - out
                wide[here, there] = wbuf[tap * 3 + col] if 0 <= tap < 3 else none
                tap = out + 2 - row
                back_ref[here, there] = turned[tap] if 0 <= tap < 3 else none
    for load in loads[1:5]:
        load.wait()
    half_bias = 0.5 * bias_ref[...]

    def body(rate):
        done = set()

        def prepare(row):
            if row in done:
                return
            done.add(row)
            value = xbuf[row] * mask_ref[1]
            spread(value, pad, row, xcat.at[row], rate)
            xt_ref[row] = value.T

        def convolve(pair):
            near, low, high = pair_rows(pair, rate, rows)
            for row in near:
                prepare(row)
            lhs = jnp.concatenate([xcat[row] for row in near], axis=1)
            width = wide.shape[0] // 4
            both = jnp.dot(
                lhs, wide[low * width : high * width], preferred_element_type=F32
            )
            return pair, (both[:, :channels], both[:, channels:])

        def finish(pair, sums):
            for row, value in zip(pair, sums):
                half_pre = 0.5 * value + half_bias
                half_cot = cbuf[row] * mask_ref[1] * 0.5
                if HALO <= row < rows - HALO:
                    grad = silu_grad(half_cot.astype(F32), half_pre)
                    spread(grad, pad, row, gcat_ref.at[row - HALO], -rate)
                    grad_ref[row - HALO] = grad.astype(BF16)
                    ready.append(row)
                else:
                    here = row if row < HALO else row - (rows - 2 * HALO)
                    pre_ref[here] = half_pre
                    cot_ref[here] = half_cot

        ready = []
        summed = []
        waiting = None
        landed = False
        for pair in row_pairs(rate, range(rows)) + [None]:
            result = convolve(pair) if pair else None
            if waiting:
                if not landed:
                    landed = True
                    for load in loads[5:]:
                        load.wait()
                finish(*waiting)
            waiting = result
            while len(ready) >= 2:
                grads = [(row, gcat_ref.at[row - HALO]) for row in ready[:2]]
                part = tap_sums(grads, lambda row: xt_ref[row], rate)
                total_ref[...] = total_ref[...] + part if summed else part
                summed.extend(ready[:2])
                del ready[:2]

    by_rate(rates_ref[0, mine], body)


def rims_kernel(
    rates_ref, a_ref, b_ref, pre_ref, cot_ref, mask_ref, near_ref, xt_own_ref, total_ref,
    grad_a_ref, grad_b_ref, keep_ref, send_ref,
    pad, xcat, halo, grads, xt_halo, gedge, flat, *, scale, paired,
):
    _, columns, channels = a_ref.shape
    rows = xt_own_ref.shape[0]
    clear_ends(pad, 4 * HALO, columns)
    by_side(a_ref, b_ref, halo)

    def flipped(row):
        if row < 0:
            return xt_halo[row + HALO]
        return xt_own_ref[row] if row < rows else xt_halo[row - rows + HALO]

    def body(rate):
        halves = []
        for side in range(2):
            used = range(HALO - rate, HALO) if side == 0 else range(rate)
            for place, k in enumerate(used):
                value = halo[side, k] * mask_ref[2 * side]
                part = pl.ds(place * columns, columns)
                spread(value, pad, side * HALO + k, xcat.at[side, part], rate)
                xt_halo[side * HALO + k] = value.T
            halves.append(
                jnp.dot(xcat[side, : rate * columns], near_ref[side], preferred_element_type=F32)
            )
        total = total_ref[...]
        for side, sums in enumerate(halves):
            edges = []
            for k in range(HALO):
                slot = side * HALO + k
                half_pre = pre_ref[slot]
                place = k if side == 0 else k - (HALO - rate)
                if 0 <= place < rate:
                    half_pre += 0.5 * sums[place * columns : (place + 1) * columns]
                grad = silu_grad(cot_ref[slot].astype(F32), half_pre)
                grads[side, k] = grad.astype(BF16)
                spread(grad, pad, 2 * HALO + slot, gedge.at[slot], -rate)
                edges.append((k + side * (rows - HALO), gedge.at[slot]))
            total = total + tap_sums(edges, flipped, rate)
        total = total * scale
        for a in range(3):
            for b in range(3):
                start = (a * 3 + b) * channels
                flat[start : start + channels] = total[
                    a * channels : (a + 1) * channels, b * channels : (b + 1) * channels
                ]

    by_rate(rates_ref[1, 0, 0], body)
    odd = lax.axis_index("tile") % 2
    grad_a_ref[...] = grads[1 - odd]
    grad_b_ref[...] = grads[odd]
    if not paired:
        keep_ref[0] = flat[: keep_ref.shape[1]]
        return
    parts, share, _ = keep_ref.shape
    padded = send_ref.shape[1]
    flat[parts * 2 * share :] = jnp.zeros((flat.shape[0] - parts * 2 * share, channels), F32)
    here = lax.axis_index("dp")
    for part in range(parts):
        keep_ref[part] = flat[pl.ds((2 * part + here) * share, share)]
        send_ref[part] = flat[pl.ds((2 * part + 1 - here) * share, padded)].astype(BF16)


def last_kernel(
    rates_ref, from_a_ref, from_b_ref, grad_a_ref, grad_b_ref,
    grad_ref, cot_hbm, mask_ref, back_ref, far_ref,
    out_hbm,
    cbuf, obuf, pad, gcat, spare, theirs, ours, sems,
):
    rows, columns, channels = cot_hbm.shape
    inner = rows - 2 * HALO
    around = 2 * HALO
    chunks = rows // around
    cots, stores = [], []
    for k in range(chunks):
        part = pl.ds(k * around, around)
        cots.append(
            pltpu.make_async_copy(cot_hbm.at[part], cbuf.at[part], sems.at[k])
        )
        stores.append(
            pltpu.make_async_copy(obuf.at[part], out_hbm.at[part], sems.at[chunks + k])
        )
    for load in cots:
        load.start()
    clear_ends(pad, rows + 2 * HALO, columns)
    by_side(from_a_ref, from_b_ref, theirs)
    by_side(grad_a_ref, grad_b_ref, ours)

    def neighbour(side):
        rate = rates_ref[2 * side, 0, 0]
        for k in range(HALO):
            part = pl.ds(k * columns, columns)
            spread(theirs[side, k], pad, rows + side * HALO + k, spare.at[side, part], -rate)
        sums = jnp.dot(spare[side], far_ref[side], preferred_element_type=F32)
        parts = [sums[k * columns : (k + 1) * columns] for k in range(HALO)]
        none = jnp.zeros((columns, channels), F32)
        one = rate == 1
        if side:
            return [jnp.where(one, none, parts[0]), jnp.where(one, parts[0], parts[1])]
        return [jnp.where(one, parts[1], parts[0]), jnp.where(one, none, parts[1])]

    def body(rate):
        done = set()

        def shifted(row):
            if row not in done:
                done.add(row)
                if row < HALO:
                    value = ours[0, row]
                elif row < rows - HALO:
                    value = grad_ref[row - HALO]
                else:
                    value = ours[1, row - (rows - HALO)]
                spread(value, pad, row, gcat.at[row], -rate)
            return gcat.at[row]

        for chunk in range(chunks):
            start = chunk * around
            results = [
                (pair, input_sums(pair, rate, rows, shifted, back_ref))
                for pair in row_pairs(rate, range(start, start + around))
            ]
            terms = {0: 0, chunks - 1: 1}
            added = neighbour(terms[chunk]) if chunk in terms else None
            cots[chunk].wait()
            for pair, sums in results:
                for row, value in zip(pair, sums):
                    value = value + cbuf[row].astype(F32)
                    if row < HALO:
                        value = value + added[row]
                    elif row >= rows - HALO:
                        value = value + added[row - (rows - HALO)]
                    obuf[row] = value.astype(BF16) * mask_ref[1]
            stores[chunk].start()

    by_rate(rates_ref[1, 0, 0], body)
    for store in stores:
        store.wait()


def cut_kernel(x_hbm, a_ref, b_ref, sems):
    rows = x_hbm.shape[0]
    odd = lax.axis_index("tile") % 2
    copies = []
    for index, ref in enumerate((a_ref, b_ref)):
        start = (rows - HALO) * (odd if index else 1 - odd)
        for k in range(HALO):
            copies.append(
                pltpu.make_async_copy(x_hbm.at[start + k], ref.at[k], sems.at[index, k])
            )
    for copy in copies:
        copy.start()
    for copy in copies:
        copy.wait()


def swap(rows_a, rows_b, axis):
    count = lax.axis_size(axis)
    results = []
    for start, rows in ((0, rows_a), (1, rows_b)):
        pairs = [(i, i + 1) for i in range(start, count - 1, 2)]
        results.append(lax.ppermute(rows, axis, pairs + [(j, i) for i, j in pairs]))
    return results


def call(kernel, name, outs, specs, scratch, aliases=None, flops=0):
    memory = {"s": pltpu.SMEM, "v": pltpu.VMEM, "h": pltpu.HBM}
    ins, results = (
        [pl.BlockSpec(memory_space=memory[letter]) for letter in part] for part in specs.split(">")
    )
    return pl.pallas_call(
        kernel,
        name=name,
        out_shape=tuple(
            pltpu.HBM(shape, dtype) if letter == "h" else jax.ShapeDtypeStruct(shape, dtype)
            for (shape, dtype), letter in zip(outs, specs.split(">")[1])
        ),
        in_specs=ins,
        out_specs=tuple(results),
        scratch_shapes=scratch,
        input_output_aliases=aliases or {},
        cost_estimate=pl.CostEstimate(flops=flops, bytes_accessed=0, transcendentals=0),
        compiler_params=pltpu.CompilerParams(vmem_limit_bytes=VMEM_LIMIT),
    )


def in_hbm(array):
    return pltpu.with_memory_space_constraint(array, pltpu.HBM)


def shards(features, cotangent, tile_mask, work_lists, dilations, conv_weight, conv_bias):
    x, cot, lists = features[0], in_hbm(cotangent[0]), in_hbm(work_lists[0])
    dilations = in_hbm(dilations)
    rows, columns, channels = x.shape
    axes = ("tile", "dp")
    devices = lax.axis_size("tile") * lax.axis_size("dp")
    weight = in_hbm(conv_weight.reshape(9, channels, channels))
    bias = in_hbm(conv_bias.reshape(1, channels))
    inner = rows - 2 * HALO
    wide_row = 3 * channels
    whole = ((rows, columns, channels), BF16)

    def pads(count):
        return pltpu.VMEM((count, columns + 2 * EDGE, channels), F32)

    rim = ((HALO, columns, channels), BF16)
    sides = pltpu.VMEM((2, HALO, columns, channels), BF16)
    rows_a, rows_b = call(
        cut_kernel,
        "cut",
        [rim, rim],
        "h>vv",
        [pltpu.SemaphoreType.DMA((2, HALO))],
    )(in_hbm(x))
    x_a, x_b = swap(rows_a, rows_b, "tile")

    rates, grad, pre, xt, total, mask, cot_edge, back, near, far = call(
        first_kernel,
        "first",
        [
            ((3, 8, LANES), jnp.int32),
            ((inner, columns, channels), BF16),
            ((2 * HALO, columns, channels), F32),
            ((rows, channels, columns), BF16),
            ((wide_row, wide_row), F32),
            ((3, columns, channels), BF16),
            ((2 * HALO, columns, channels), BF16),
            ((4 * wide_row, 2 * channels), BF16),
            ((2, wide_row, channels), BF16),
            ((2, wide_row, channels), BF16),
        ],
        "hhhhhh>vvvvvvvvvv",
        [
            pltpu.SMEM(dilations.shape, jnp.int32),
            pltpu.VMEM(lists.shape, jnp.int32),
            pltpu.VMEM(bias.shape, F32),
            pltpu.VMEM((rows, columns, channels), BF16),
            pltpu.VMEM((rows, columns, channels), BF16),
            pltpu.VMEM((9, channels, channels), BF16),
            pads(rows),
            pltpu.VMEM((rows, columns, wide_row), BF16),
            pltpu.VMEM((inner, columns, wide_row), BF16),
            pltpu.VMEM((4 * wide_row, 2 * channels), BF16),
            pltpu.SemaphoreType.DMA((12,)),
        ],
        flops=BUSY,
    )(dilations, lists, in_hbm(x), cot, weight, bias)

    tap_rows = 9 * channels
    cores = lax.axis_size("dp")
    paired = cores == 2 and tap_rows % devices == 0
    share = (devices // 2, tap_rows // devices) if paired else (1, tap_rows)
    padded = -(-share[1] // PACK) * PACK
    scale = 1.0 / math.sqrt(devices * lists.shape[1] * TILE * TILE)
    grad_a, grad_b, keep, send = call(
        lambda *refs: rims_kernel(*refs, scale=scale, paired=paired),
        "rims",
        [rim, rim, (share + (channels,), F32), ((share[0], padded, channels), BF16)],
        "vvvvvvvvv>vvvv",
        [
            pads(4 * HALO),
            pltpu.VMEM((2, HALO * columns, wide_row), BF16),
            sides,
            sides,
            pltpu.VMEM((2 * HALO, channels, columns), BF16),
            pltpu.VMEM((2 * HALO, columns, wide_row), BF16),
            pltpu.VMEM((tap_rows + PACK, channels), F32),
        ],
    )(rates, x_a, x_b, pre, cot_edge, mask, near, xt, total)

    from_a, from_b = swap(grad_a, grad_b, "tile")
    if paired:
        other = lax.ppermute(send, "dp", [(0, 1), (1, 0)])
        both = (keep + other[:, : share[1]].astype(F32)).astype(BF16)
        received = lax.all_to_all(both, "tile", 0, 0, tiled=True)
    else:
        received = lax.all_to_all(
            keep.astype(BF16).reshape(devices, -1), axes, 0, 0, tiled=True
        )

    (input_grad,) = call(
        last_kernel,
        "last",
        [whole],
        "vvvvvvhvvv>h",
        [
            pltpu.VMEM((rows, columns, channels), BF16),
            pltpu.VMEM((rows, columns, channels), BF16),
            pads(rows + 2 * HALO),
            pltpu.VMEM((rows, columns, wide_row), BF16),
            pltpu.VMEM((2, HALO * columns, wide_row), BF16),
            sides,
            sides,
            pltpu.SemaphoreType.DMA((2 * (rows // (2 * HALO)),)),
        ],
        flops=BUSY,
    )(
        rates, from_a, from_b, grad_a, grad_b,
        grad, cot, mask, back, far,
    )
    summed = jnp.sum(received.astype(F32), axis=0)
    return (input_grad[None], summed.reshape(-1))


def solution(mesh):
    placed = (
        P("dp", "tile", None, None),
        P("dp", "tile", None, None),
        P("dp", "tile", None),
        P("dp", None, None),
        P("dp", None),
        P(),
        P(),
    )
    return jax.shard_map(
        shards,
        mesh=mesh,
        in_specs=placed,
        out_specs=(P("dp", "tile", None, None), P(("tile", "dp"))),
        check_vma=False,
    )
```
